128 devices in a mesh: bead: 8 (over z, core), gx: 4 (over y), gy: 4 (over x).
Axes of the slice: x: 4, y: 4, z: 4, core: 2. Of those that a mesh axis runs over, the one named last changes fastest.
Arguments:
- positions: float32 [32, 3, 16384], P('bead', None, ('gx', 'gy')), may hold values from 0 to 3
- momenta: float32 [32, 3, 16384], P('bead', None, ('gx', 'gy')), may hold values from -0.24 to 0.24
- types: int32 [16384], P(('gx', 'gy')), may hold values from 0 to 1
- ghost_rows: int32 [2048], P(('gx', 'gy')), may hold values from 0 to 1023
- neighbours: int32 [16, 16384], P(None, ('gx', 'gy')), may hold values from 0 to 2175
- counts: int32 [16384], P(('gx', 'gy')), may hold values from 8 to 16
- hardness: float32 [2], replicated, may hold values from 0.5 to 1
- chi_w1: float32 [2, 25, 30], replicated, may hold values from -1 to 1
- chi_w2: float32 [2, 25, 25], replicated, may hold values from -1.25 to 1.25
- chi_w3: float32 [2, 25], replicated, may hold values from -1.25 to 1.25
- en_w1: float32 [2, 25, 31], replicated, may hold values from -1 to 1
- en_w2: float32 [2, 25, 25], replicated, may hold values from -1.25 to 1.25
- en_w3: float32 [2, 25], replicated, may hold values from -1.25 to 1.25
Outputs:
- new_positions: float32 [32, 3, 16384], P('bead', None, ('gx', 'gy'))
- new_momenta: float32 [32, 3, 16384], P('bead', None, ('gx', 'gy'))
- charges: float32 [32, 16384], P('bead', ('gx', 'gy'))
- energies: float32 [32, 16384], P('bead', ('gx', 'gy'))
The draws below stay inside these ranges and needn't reach their ends.
All inputs are finite; a program needn't handle non-finite values.
Results may differ from the reference program's by a relative error of at most 0.0003.
Values sent between devices are 32-bit elements; how exact they have to be, the bound alone decides.
A program may use at most 128 MiB of HBM per device.

```python
import math
import jax
import jax.numpy as jnp
from jax import lax

A_DEV = 1024
NB = 16
S = 30
H = 25
ITERS = 5
BEADS = 32
GHOST = 128
ATOMS = 16384
GHOST_ALL = 2048
N_GX = 4
N_GY = 4


def plant(drawn, stream_key, low, high):
    longest = drawn.shape.index(max(drawn.shape))
    spots = []
    for shift in (0, 1):
        where = [jax.random.randint(jax.random.fold_in(stream_key, axis), (), 0, length) for axis, length in enumerate(drawn.shape)]
        where[longest] = (where[longest] + shift) % drawn.shape[longest]
        spots.append(tuple(where))
    return drawn.at[spots[0]].set(low).at[spots[1]].set(high)


def level_of(rng, extent, pieces, smallest, top_value):
    loudness = 1.0
    for position, shards_of in pieces:
        draws = jax.random.uniform(jax.random.fold_in(jax.random.fold_in(rng, 6), position), (shards_of,), jnp.float32, smallest / len(pieces), top_value / len(pieces))
        loudness = loudness * jnp.repeat(jnp.exp(draws), extent[position] // shards_of).reshape((-1,) + (1,) * (len(extent) - 1 - position))
    return loudness


def centred(stream_key, shape, deviation, bound, shards=(), held_as=jnp.bfloat16):
    factor_of = level_of(stream_key, shape, shards, -0.22, 0.18) if shards else 1.0
    result = jax.random.normal(stream_key, shape, jnp.float32) * deviation * factor_of
    return jnp.minimum(jnp.maximum(result, -bound), bound).astype(held_as)


def setup_inputs(seed: int = 0) -> dict:
    key_of = jax.random.split(jax.random.key(seed), 14)
    positions = jnp.clip(3.0 * jax.random.uniform(key_of[0], (BEADS, 3, ATOMS), jnp.float32) ** level_of(key_of[0], (BEADS, 3, ATOMS), ((0, 8), (2, 16)), -0.2, 0.2), 0.0, 3.0)
    momenta = centred(key_of[1], (BEADS, 3, ATOMS), 0.03, 0.24, ((0, 8), (2, 16)), jnp.float32)
    types = plant(jax.random.randint(key_of[2], (ATOMS,), 0, 2), jax.random.fold_in(key_of[2], 1), 0, 1).astype(jnp.int32)
    ghost_rows = plant(jax.random.randint(key_of[3], (GHOST_ALL,), 0, A_DEV), jax.random.fold_in(key_of[3], 1), 0, A_DEV - 1).astype(jnp.int32)
    neighbours = plant(jax.random.randint(key_of[4], (NB, ATOMS), 0, A_DEV + 9 * GHOST), jax.random.fold_in(key_of[4], 1), 0, (A_DEV + 9 * GHOST) - 1).astype(jnp.int32)
    counts = plant(jax.random.randint(key_of[5], (ATOMS,), NB // 2, NB + 1), jax.random.fold_in(key_of[5], 1), NB // 2, NB).astype(jnp.int32)
    hardness = jnp.clip(jax.random.uniform(key_of[6], (2,), jnp.float32, 0.5, 1.0), 0.5, 1.0)
    chi_w1 = centred(key_of[7], (2, H, S), S ** -0.5, 1.0, (), jnp.float32)
    chi_w2 = centred(key_of[8], (2, H, H), H ** -0.5, 1.25, (), jnp.float32)
    chi_w3 = centred(key_of[9], (2, H), H ** -0.5, 1.25, (), jnp.float32)
    en_w1 = centred(key_of[10], (2, H, S + 1), (S + 1) ** -0.5, 1.0, (), jnp.float32)
    en_w2 = centred(key_of[11], (2, H, H), H ** -0.5, 1.25, (), jnp.float32)
    en_w3 = centred(key_of[12], (2, H), H ** -0.5, 1.25, (), jnp.float32)
    return {"positions": positions, "momenta": momenta, "types": types, "ghost_rows": ghost_rows, "neighbours": neighbours, "counts": counts, "hardness": hardness, "chi_w1": chi_w1, "chi_w2": chi_w2, "chi_w3": chi_w3, "en_w1": en_w1, "en_w2": en_w2, "en_w3": en_w3}


PRECISE = lax.Precision.HIGHEST
STEP = 0.5
CYCLE_FREQ = 40.0
CUTOFF = 4.0
HEAVY_MASS = 16.0
CHI_SCALE = 4.0
COUPLING_SCALE = 16.0

def mode_tables(beads):
    row_ids = jnp.arange(beads, dtype=jnp.float32)[:, None]
    col_ids = jnp.arange(beads, dtype=jnp.int32)[None, :]
    angle = 2.0 * math.pi * row_ids * col_ids.astype(jnp.float32) / beads
    edge = (col_ids == 0) | (2 * col_ids == beads)
    scaled = math.sqrt(2.0 / beads)
    matrix = jnp.where(edge, jnp.cos(angle) / math.sqrt(beads), jnp.where(2 * col_ids < beads, scaled * jnp.cos(angle), scaled * jnp.sin(angle)))
    frequency = 2.0 * CYCLE_FREQ * jnp.sin(math.pi * jnp.arange(beads, dtype=jnp.float32) / beads)
    return (matrix, frequency)

def rotate_modes(normal_modes, masses, frequency):
    top_freq = 2.0 * CYCLE_FREQ
    coord_part = normal_modes[:, 0]
    moment_part = normal_modes[:, 1]
    omega = frequency[:, None, None]
    cosine = jnp.cos(omega * STEP)
    sine_part = jnp.sin(omega * STEP)
    moving = omega > 0
    safe_omega = jnp.where(moving, omega, 1.0)
    drift_term = jnp.where(moving, top_freq * sine_part / (masses * safe_omega), top_freq * STEP / masses)
    restoring = -(masses * omega / top_freq) * sine_part
    return jnp.stack([cosine * coord_part + drift_term * moment_part, restoring * coord_part + cosine * moment_part], 1)

def radial_terms(dist_sq, heavy_w, light_w, half):
    heavy_rows = []
    light_rows = []
    for slot_index in range(half):
        decay_rate = 0.2 * 20.0 ** (slot_index / (half - 1))
        falloff = jnp.exp(-decay_rate * dist_sq)
        heavy_rows.append(lax.optimization_barrier(jnp.sum(heavy_w * falloff, axis=-2)))
        light_rows.append(lax.optimization_barrier(jnp.sum(light_w * falloff, axis=-2)))
    return jnp.log1p(jnp.stack(heavy_rows + light_rows, axis=-2))

def network(features, first_w, second_w, third_w, heavy):
    results = []
    for element in range(2):
        hidden = jnp.tanh(jnp.einsum('hs,...sa->...ha', first_w[element], features, precision=PRECISE))
        hidden = jnp.tanh(jnp.einsum('hk,...ka->...ha', second_w[element], hidden, precision=PRECISE))
        results.append(jnp.einsum('h,...ha->...a', third_w[element], hidden, precision=PRECISE))
    return jnp.where(heavy, results[0], results[1])

def with_ghosts(values, ghost_index):
    leading = values.shape[:-2]
    gathered_index = jnp.broadcast_to(ghost_index, leading + ghost_index.shape)
    lent = jnp.take_along_axis(values, gathered_index, axis=-1)
    lent = lent.reshape(leading + (N_GX, N_GY, ghost_index.shape[-1]))
    blocks = [jnp.roll(lent, (1 - shift_x, 1 - shift_y), axis=(-3, -2)) for shift_x in range(3) for shift_y in range(3)]
    joined = jnp.concatenate(blocks, -1).reshape(leading + (N_GX * N_GY, -1))
    return jnp.concatenate([values, joined], -1)

def lookup(value_table, neighbour_index):
    flat_index = neighbour_index.reshape(neighbour_index.shape[0], -1)
    flat_index = jnp.broadcast_to(flat_index, value_table.shape[:-1] + flat_index.shape[-1:])
    found = jnp.take_along_axis(value_table, flat_index, axis=-1)
    return found.reshape(value_table.shape[:-1] + neighbour_index.shape[1:])

def spread_back(terms, neighbour_index, ghost_index):
    leading = terms.shape[:-3]
    bricks = N_GX * N_GY
    ghost_count = ghost_index.shape[-1]
    brick_ids = jnp.arange(bricks, dtype=jnp.int32)
    table = jnp.zeros(leading + (bricks, A_DEV + 9 * ghost_count), terms.dtype)
    table = table.at[..., brick_ids[:, None, None], neighbour_index].add(terms)
    blocks = table[..., A_DEV:].reshape(leading + (N_GX, N_GY, 3, 3, ghost_count))
    received = jnp.zeros(leading + (N_GX, N_GY, ghost_count), terms.dtype)
    for first_pick in range(3):
        for second_pick in range(3):
            received = received + jnp.roll(blocks[..., first_pick, second_pick, :], (first_pick - 1, second_pick - 1), axis=(-3, -2))
    received = received.reshape(leading + (bricks, ghost_count))
    return table[..., :A_DEV].at[..., brick_ids[:, None], ghost_index].add(received)

def solve(operate, right_sides):
    solution = jnp.zeros_like(right_sides)
    residual = right_sides
    direction = right_sides
    norm_now = lax.optimization_barrier(jnp.sum(residual * residual, axis=(-2, -1), keepdims=True))
    for sweep in range(ITERS):
        applied = operate(direction)
        step_len = norm_now / lax.optimization_barrier(jnp.sum(direction * applied, axis=(-2, -1), keepdims=True))
        solution = solution + step_len * direction
        residual = residual - step_len * applied
        norm_next = lax.optimization_barrier(jnp.sum(residual * residual, axis=(-2, -1), keepdims=True))
        direction = residual + norm_next / norm_now * direction
        norm_now = norm_next
    return solution

def reference(positions, momenta, types, ghost_rows, neighbours, counts, hardness, chi_w1, chi_w2, chi_w3, en_w1, en_w2, en_w3):
    matrix, frequency = mode_tables(BEADS)
    heavy_atoms = types == 0
    masses = jnp.where(heavy_atoms, HEAVY_MASS, 1.0)
    phase_space = jnp.stack([positions, momenta], 1)
    normal_modes = jnp.einsum('jk,jsca->ksca', matrix, phase_space, precision=PRECISE)
    advanced = jnp.einsum('jk,ksca->jsca', matrix, rotate_modes(normal_modes, masses, frequency), precision=PRECISE)
    new_positions = advanced[:, 0]
    new_momenta = advanced[:, 1]
    bricks = N_GX * N_GY
    neighbour_index = neighbours.reshape(NB, bricks, A_DEV).transpose(1, 0, 2)
    ghost_index = ghost_rows.reshape(bricks, -1)
    heavy = heavy_atoms.reshape(bricks, A_DEV)
    heavy_f = heavy.astype(jnp.float32)
    slots = jnp.arange(NB, dtype=jnp.int32)[None, :, None]
    in_tile = (slots < counts.reshape(bricks, A_DEV)[:, None, :]).astype(jnp.float32)
    hardness_atom = jnp.where(heavy, hardness[0], hardness[1])
    near_heavy = lookup(with_ghosts(heavy_f, ghost_index), neighbour_index)

    def one_bead(coords):
        neighbour_pos = lookup(with_ghosts(coords, ghost_index), neighbour_index)
        offsets = neighbour_pos - coords[:, :, None, :]
        dist_sq = lax.optimization_barrier(jnp.sum(offsets * offsets, 0))
        distance = jnp.sqrt(dist_sq)
        smooth = jnp.where(distance < CUTOFF, 0.5 * (jnp.cos(math.pi * distance / CUTOFF) + 1.0), 0.0) * in_tile
        features = radial_terms(dist_sq, smooth * near_heavy, smooth * (1.0 - near_heavy), chi_w1.shape[2] // 2)
        chi = network(features, chi_w1, chi_w2, chi_w3, heavy)
        coupling = COUPLING_SCALE / NB * smooth / jnp.sqrt(1.0 + dist_sq)
        degree = 0.5 * (lax.optimization_barrier(jnp.sum(coupling, -2)) + spread_back(coupling, neighbour_index, ghost_index))
        diagonal_term = hardness_atom + degree

        def operate(vector):
            near_values = lookup(with_ghosts(vector, ghost_index), neighbour_index)
            forward = lax.optimization_barrier(jnp.sum(coupling * near_values, -2))
            backward = spread_back(coupling * vector[:, :, None, :], neighbour_index, ghost_index)
            return diagonal_term * vector - 0.5 * (forward + backward)
        right_sides = jnp.stack([-CHI_SCALE * chi, jnp.ones_like(chi)])
        solution = solve(operate, right_sides)
        totals = lax.optimization_barrier(jnp.sum(solution, axis=(1, 2)))
        charges = solution[0] - totals[0] / totals[1] * solution[1]
        energies = network(jnp.concatenate([features, charges[:, None, :]], 1), en_w1, en_w2, en_w3, heavy)
        return (charges, energies)
    coords_all = new_positions.reshape(BEADS, 3, bricks, A_DEV)
    charges, energies = lax.map(one_bead, coords_all)
    return (new_positions, new_momenta, charges.reshape(BEADS, -1), energies.reshape(BEADS, -1))
```

```python
import functools
import math

import jax
import jax.numpy as jnp
import numpy as np
from jax import lax
from jax.experimental import pallas as pl
from jax.experimental.pallas import tpu as pltpu
from jax.sharding import PartitionSpec as P

MESH = pl.DeviceIdType.MESH
F32 = jnp.float32
BF16 = jnp.bfloat16
HIGHEST = lax.Precision.HIGHEST
ITERS = 5
STEP = 0.5
TOP_FREQ = 80.0
CUTOFF = 4.0
HEAVY_MASS = 16.0
CHI_SCALE = 4.0
LANES = 128
BEADS = 32
GROUPS = 8
PER = 4
ATOMS = 1024
CHUNKS = ATOMS // LANES
SLOTS = 16
TABLE = ATOMS + 9 * LANES
HALF = 15
FEATS = 2 * HALF
SIDE = 4
BRICKS = SIDE * SIDE
BAND = 16
WIDE = 256
BLOCKS = -(-TABLE // WIDE)
VMEM_LIMIT = 60 * 1024 * 1024


def propagator():
    k = np.arange(BEADS)
    omega = TOP_FREQ * np.sin(math.pi * k / BEADS)
    cosine = np.cos(omega * STEP)
    sine = np.sin(omega * STEP)
    drift = np.where(k > 0, TOP_FREQ * sine / np.where(k > 0, omega, 1.0), TOP_FREQ * STEP)
    restoring = -(omega / TOP_FREQ) * sine
    gap = (k[:, None] - k[None, :]) % BEADS

    def spread(weights):
        line = (weights[None, :] * np.cos(2 * math.pi * k[:, None] * k[None, :] / BEADS)).sum(1) / BEADS
        return line[gap]

    keep, push, pull = spread(cosine), spread(drift), spread(restoring)
    zero = np.zeros_like(keep)
    plain = np.block([[keep, zero], [zero, keep]])
    massive = np.block([[zero, push], [pull, zero]])
    order = np.array([half * BEADS + g * PER + b for g in range(GROUPS) for half in range(2) for b in range(PER)])
    both = np.concatenate([plain[order][:, order], massive[order][:, order]], 0)
    return both.astype(np.float32)


def sublanes(shape):
    return lax.broadcasted_iota(jnp.int32, shape, 0)


def lane_take(table, lane):
    return jnp.take_along_axis(table, lane, axis=1, mode="promise_in_bounds")


def row_bits(rows, count):
    return [(rows & (LANES << bit)) != 0 for bit in range(count)]


def pick(parts, bits):
    level = 0
    while len(parts) > 1:
        nxt = [
            jnp.where(bits[level], parts[i + 1], parts[i]) for i in range(0, len(parts) - 1, 2)
        ]
        if len(parts) % 2:
            nxt.append(parts[-1])
        parts = nxt
        level += 1
    return parts[0]


def brick_at(dx, dy):
    return {
        "gx": lax.rem(lax.axis_index("gx") + dx + SIDE, SIDE),
        "gy": lax.rem(lax.axis_index("gy") + dy + SIDE, SIDE),
    }


AROUND = [(a, c) for a in range(3) for c in range(3) if (a, c) != (1, 1)]


def propagate_kernel(
    matrix_ref,
    pos_ref,
    mom_ref,
    types_ref,
    ghost_ref,
    newpos_ref,
    newmom_ref,
    tab_ref,
    stage,
    modes,
    moved,
    back,
    lent,
    send1,
    recv1,
    send2,
    recv2,
    send3,
    recv3,
):
    me = lax.axis_index("bead")
    width = 3 * LANES
    barrier = pltpu.get_barrier_semaphore()
    for o in range(1, GROUPS):
        pl.semaphore_signal(
            barrier, inc=1, device_id={"bead": lax.rem(me + o, GROUPS)}, device_id_type=MESH
        )
    for a, c in AROUND:
        pl.semaphore_signal(barrier, inc=1, device_id=brick_at(a - 1, c - 1), device_id_type=MESH)
    sub = sublanes((8, LANES))
    low = sub < PER
    for d in range(CHUNKS):
        for c in range(3):
            at = d * width + c * LANES
            stage[0:PER, at : at + LANES] = pos_ref[:, c, d * LANES : (d + 1) * LANES]
            stage[PER:8, at : at + LANES] = mom_ref[:, c, d * LANES : (d + 1) * LANES]
    pl.semaphore_wait(barrier, GROUPS - 1 + len(AROUND))
    copies = []
    for o in range(1, GROUPS):
        to = lax.rem(me + o, GROUPS)
        cp = pltpu.make_async_remote_copy(
            src_ref=stage.at[:, pl.ds(pl.multiple_of(to * width, LANES), width)],
            dst_ref=modes.at[pl.ds(pl.multiple_of(me * 8, 8), 8), :],
            send_sem=send1.at[o],
            recv_sem=recv1.at[o],
            device_id={"bead": to},
            device_id_type=MESH,
        )
        cp.start()
        copies.append(cp)
    mine = pl.ds(pl.multiple_of(me * 8, 8), 8)
    my_lanes = pl.ds(pl.multiple_of(me * width, LANES), width)
    modes[mine, :] = stage[:, my_lanes]
    heavy = jnp.where(types_ref[...] == 0, 1.0, 0.0)
    ghost_rows = jnp.broadcast_to(ghost_ref[...], (8, LANES))
    ghost_lane = ghost_rows & (LANES - 1)
    ghost_bits = row_bits(ghost_rows, 3)
    for d in range(CHUNKS):
        tab_ref[3, :, d * LANES : (d + 1) * LANES] = jnp.broadcast_to(
            heavy[:, d * LANES : (d + 1) * LANES], (8, LANES)
        )
    my_types = types_ref[:, pl.ds(pl.multiple_of(me * LANES, LANES), LANES)]
    mass = jnp.where(my_types == 0, HEAVY_MASS, 1.0)
    mass = jnp.broadcast_to(mass, (8, LANES))
    factor = jnp.where(low, 1.0 / mass, mass)
    factor = jnp.concatenate([factor] * 3, 1)
    for cp in copies:
        cp.wait()
    both = jnp.dot(matrix_ref[...], modes[...], precision=HIGHEST, preferred_element_type=F32)
    for g in range(GROUPS):
        rows = slice(g * 8, g * 8 + 8)
        moved[rows, :] = both[rows] + both[64 + g * 8 : 72 + g * 8] * factor
    copies = []
    for o in range(1, GROUPS):
        to = lax.rem(me + o, GROUPS)
        cp = pltpu.make_async_remote_copy(
            src_ref=moved.at[pl.ds(pl.multiple_of(to * 8, 8), 8), :],
            dst_ref=back.at[:, my_lanes],
            send_sem=send2.at[o],
            recv_sem=recv2.at[o],
            device_id={"bead": to},
            device_id_type=MESH,
        )
        cp.start()
        copies.append(cp)
    back[:, my_lanes] = moved[mine, :]
    for cp in copies:
        cp.wait()
    for c in range(3):
        for d in range(CHUNKS):
            at = d * width + c * LANES
            v = back[:, at : at + LANES]
            newpos_ref[:, c, d * LANES : (d + 1) * LANES] = v[0:PER]
            newmom_ref[:, c, d * LANES : (d + 1) * LANES] = v[PER:8]
            tab_ref[c, :, d * LANES : (d + 1) * LANES] = jnp.where(low, v, pltpu.roll(v, PER, 0))
    for c in range(4):
        lent[c] = pick(
            [lane_take(tab_ref[c, :, d * LANES : (d + 1) * LANES], ghost_lane) for d in range(CHUNKS)],
            ghost_bits,
        )
    copies = []
    for n, (a, c) in enumerate(AROUND):
        at = ATOMS + (3 * a + c) * LANES
        cp = pltpu.make_async_remote_copy(
            src_ref=lent,
            dst_ref=tab_ref.at[:, :, at : at + LANES],
            send_sem=send3.at[n],
            recv_sem=recv3.at[n],
            device_id=brick_at(1 - a, 1 - c),
            device_id_type=MESH,
        )
        cp.start()
        copies.append(cp)
    at = ATOMS + 4 * LANES
    tab_ref[:, :, at : at + LANES] = lent[...]
    for cp in copies:
        cp.wait()


def network(features, w1_ref, w2_ref, w3_ref, heavy):
    results = []
    for e in range(2):
        h = jnp.tanh(jnp.dot(w1_ref[e], features, precision=HIGHEST, preferred_element_type=F32))
        h = jnp.tanh(jnp.dot(w2_ref[e], h, precision=HIGHEST, preferred_element_type=F32))
        results.append(
            jnp.dot(w3_ref[e : e + 1, :], h, precision=HIGHEST, preferred_element_type=F32)
        )
    return jnp.where(heavy, results[0], results[1])


def features_kernel(
    tab_ref,
    idx_ref,
    counts_ref,
    types_ref,
    w1_ref,
    w2_ref,
    w3_ref,
    coup_ref,
    feat_ref,
    rhs_ref,
    pairs,
):
    sub = sublanes((8, LANES))
    low = sub < PER
    low_all = sublanes((8, ATOMS)) < PER
    for kp in range(SLOTS // 2):
        pairs[kp] = jnp.where(
            low_all,
            jnp.broadcast_to(idx_ref[2 * kp : 2 * kp + 1, :], (8, ATOMS)),
            jnp.broadcast_to(idx_ref[2 * kp + 1 : 2 * kp + 2, :], (8, ATOMS)),
        )
    slot_off = jnp.where(low, 0, 1)
    cos_scale = (math.pi / (2.0 * CUTOFF)) ** 2
    cos_terms = [(-1.0) ** n * cos_scale**n / math.factorial(2 * n) for n in range(8)]
    feat_ref[...] = jnp.zeros_like(feat_ref)

    def chunk_step(ci, carry):
        lanes = pl.ds(pl.multiple_of(ci * LANES, LANES), LANES)
        own = [tab_ref[c, :, lanes] for c in range(3)]
        count = jnp.broadcast_to(counts_ref[:, lanes], (8, LANES))

        def pair_step(kp, sums):
            rows = pairs[kp, :, lanes]
            lane = rows & (LANES - 1)
            bits = row_bits(rows, 5)
            near = [
                pick(
                    [
                        lane_take(tab_ref[c, :, t * LANES : (t + 1) * LANES], lane)
                        for t in range(TABLE // LANES)
                    ],
                    bits,
                )
                for c in range(4)
            ]
            dist_sq = sum((near[c] - own[c]) ** 2 for c in range(3))
            close = jnp.minimum(dist_sq, CUTOFF * CUTOFF)
            wave = jnp.full_like(close, cos_terms[-1])
            for term in cos_terms[-2::-1]:
                wave = wave * close + term
            used = ((2 * kp + slot_off) < count) & (dist_sq < CUTOFF * CUTOFF)
            smooth = jnp.where(used, wave * wave, 0.0)
            heavy_w = smooth * near[3]
            light_w = smooth - heavy_w
            coupling = smooth * lax.rsqrt(1.0 + dist_sq)
            turned = pltpu.roll(coupling, PER, 0)
            coup_ref[2 * kp, :, lanes] = jnp.where(low, coupling, turned)
            coup_ref[2 * kp + 1, :, lanes] = jnp.where(low, turned, coupling)
            out = []
            for s in range(HALF):
                eta = 0.2 * 20.0 ** (s / (HALF - 1))
                falloff = jnp.exp(dist_sq * (-eta))
                out.append(sums[2 * s] + heavy_w * falloff)
                out.append(sums[2 * s + 1] + light_w * falloff)
            return tuple(out)

        sums = lax.fori_loop(
            0, SLOTS // 2, pair_step, tuple(jnp.zeros((8, LANES), F32) for _ in range(FEATS))
        )
        for s in range(HALF):
            for e in range(2):
                v = sums[2 * s + e]
                v = jnp.log(1.0 + (v + pltpu.roll(v, PER, 0)))
                row = (e * HALF + s) * PER
                feat_ref[ci, row : row + PER, :] = v[0:PER]
        return carry

    lax.fori_loop(0, CHUNKS, chunk_step, 0)
    heavy = types_ref[...] == 0
    for b in range(PER):
        f = jnp.concatenate(
            [feat_ref[d, pl.ds(b, FEATS, stride=PER), :] for d in range(CHUNKS)], 1
        )
        chi = network(f, w1_ref, w2_ref, w3_ref, heavy)
        rhs_ref[b : b + 1, :] = -CHI_SCALE * chi
    rhs_ref[PER:8, :] = jnp.ones((PER, ATOMS), F32)


def solve_kernel(
    hardness_ref,
    rhs_ref,
    coup_ref,
    idx_ref,
    types_ref,
    ghost_ref,
    charge_ref,
    rows_all,
    onehot,
    ghost_onehot,
    residual,
    direction,
    image,
    total,
    degree,
    table,
    scattered,
    spread,
    lent,
    backin,
    parts,
    send1,
    recv1,
    send2,
    recv2,
    send3,
    recv3,
):
    gx, gy = lax.axis_index("gx"), lax.axis_index("gy")
    me = gx * SIDE + gy
    others = [(o // SIDE, o % SIDE) for o in range(1, BRICKS)]
    barrier = pltpu.get_barrier_semaphore()
    for dx, dy in others:
        pl.semaphore_signal(barrier, inc=1, device_id=brick_at(dx, dy), device_id_type=MESH)
    sub = sublanes((8, LANES))
    low = sub < PER
    ghost_rows = jnp.broadcast_to(ghost_ref[...], (8, LANES))
    ghost_lane = ghost_rows & (LANES - 1)
    ghost_bits = row_bits(ghost_rows, 3)
    within = sublanes((WIDE, ATOMS)).astype(F32).astype(BF16)

    for k in range(SLOTS):
        rows_all[k] = jnp.broadcast_to(idx_ref[k : k + 1, :], (8, ATOMS))

    def build(k, carry):
        wide = (rows_all[k] & (WIDE - 1)).astype(F32)
        wide = jnp.concatenate([wide, wide], 0).astype(BF16)
        wide = jnp.concatenate([wide] * (WIDE // BAND), 0)
        onehot[k] = jnp.where(within == wide, 1.0, 0.0).astype(BF16)
        return carry

    lax.fori_loop(0, SLOTS, build, 0)
    for d in range(CHUNKS):
        rows = sublanes((LANES, LANES)) + d * LANES
        hit = rows == jnp.broadcast_to(ghost_ref[...], (LANES, LANES))
        ghost_onehot[d * LANES : (d + 1) * LANES, :] = jnp.where(hit, 1.0, 0.0).astype(BF16)
    hard = jnp.where(types_ref[...] == 0, hardness_ref[0], hardness_ref[1])
    residual[...] = rhs_ref[...]
    direction[...] = jnp.zeros_like(direction)
    image[...] = jnp.zeros_like(image)
    total[...] = jnp.zeros_like(total)
    degree[...] = jnp.zeros_like(degree)
    pl.semaphore_wait(barrier, len(others))

    def split(v):
        top = v.astype(BF16).astype(F32)
        return jnp.concatenate([top, v - top], 0).astype(BF16)

    def sweep(it, state):
        norm_prev, curve_prev, sum_prev, sum_total = state
        parity = lax.rem(it, 2)
        lent[0] = pick(
            [lane_take(residual[:, d * LANES : (d + 1) * LANES], ghost_lane) for d in range(CHUNKS)],
            ghost_bits,
        )
        first = []
        for n, (a, c) in enumerate(AROUND):
            at = ATOMS + (3 * a + c) * LANES
            cp = pltpu.make_async_remote_copy(
                src_ref=lent.at[0],
                dst_ref=table.at[:, at : at + LANES],
                send_sem=send1.at[n],
                recv_sem=recv1.at[n],
                device_id=brick_at(1 - a, 1 - c),
                device_id_type=MESH,
            )
            cp.start()
            first.append(cp)
        table[:, 0:ATOMS] = residual[...]
        table[:, ATOMS + 4 * LANES : ATOMS + 5 * LANES] = lent[0]
        scattered[...] = jnp.zeros_like(scattered)

        def scatter(k, carry):
            terms = split(coup_ref[k] * residual[...])
            block = (rows_all[k] >> 8).astype(F32)
            block = jnp.concatenate([block, block], 0).astype(BF16)
            zero = jnp.zeros_like(terms)
            tall = jnp.concatenate([jnp.where(block == b, terms, zero) for b in range(BLOCKS)], 0)
            scattered[...] += lax.dot_general(
                tall, onehot[k], (((1,), (1,)), ((), ())), preferred_element_type=F32
            )
            return carry

        lax.fori_loop(0, SLOTS, scatter, 0)
        for t in range(9):
            n = CHUNKS + t
            row, col = (n // 2) * BAND, (n % 2) * LANES
            spread[t] = (
                scattered[row : row + 8, col : col + LANES]
                + scattered[row + 8 : row + 16, col : col + LANES]
            )
        second = []
        for n, (a, c) in enumerate(AROUND):
            t = 3 * a + c
            cp = pltpu.make_async_remote_copy(
                src_ref=spread.at[t],
                dst_ref=backin.at[t],
                send_sem=send2.at[n],
                recv_sem=recv2.at[n],
                device_id=brick_at(a - 1, c - 1),
                device_id_type=MESH,
            )
            cp.start()
            second.append(cp)
        for cp in first:
            cp.wait()

        def gather(k, acc):
            out = []
            for d in range(CHUNKS):
                lanes = slice(d * LANES, (d + 1) * LANES)
                rows = rows_all[k, :, lanes]
                lane = rows & (LANES - 1)
                near = pick(
                    [
                        lane_take(table[:, t * LANES : (t + 1) * LANES], lane)
                        for t in range(TABLE // LANES)
                    ],
                    row_bits(rows, 5),
                )
                out.append(acc[d] + coup_ref[k, :, lanes] * near)
            return tuple(out)

        forward = lax.fori_loop(
            0, SLOTS, gather, tuple(jnp.zeros((8, LANES), F32) for _ in range(CHUNKS))
        )
        forward = jnp.concatenate(forward, 1)
        for cp in second:
            cp.wait()
        received = spread[4]
        for a, c in AROUND:
            received = received + backin[3 * a + c]
        returned = lax.dot_general(
            split(received), ghost_onehot[...], (((1,), (1,)), ((), ())), preferred_element_type=F32
        )
        pieces = []
        for d in range(CHUNKS):
            row, col = (d // 2) * BAND, (d % 2) * LANES
            pieces.append(
                scattered[row : row + 8, col : col + LANES]
                + scattered[row + 8 : row + 16, col : col + LANES]
            )
        around = forward + jnp.concatenate(pieces, 1) + returned[0:8] + returned[8:16]
        low_all = sublanes((8, ATOMS)) < PER
        fresh = 0.5 * jnp.where(low_all, pltpu.roll(around, PER, 0), around)
        deg = jnp.where(it == 0, fresh, degree[...])
        degree[...] = deg
        r = residual[...]
        w = (hard + deg) * r - 0.5 * around

        def lanes_sum(v):
            return jnp.sum(v, axis=1, keepdims=True)

        s_prev = image[...]
        lane_id = lax.broadcasted_iota(jnp.int32, (8, LANES), 1)
        dots = [lanes_sum(r * r), lanes_sum(r * w), lanes_sum(r * s_prev), lanes_sum(r)]
        mine = jnp.where(
            lane_id == 0, dots[0], jnp.where(lane_id == 1, dots[1], jnp.where(lane_id == 2, dots[2], dots[3]))
        )
        parts[parity, me] = mine
        third = []
        for n, (dx, dy) in enumerate(others):
            cp = pltpu.make_async_remote_copy(
                src_ref=parts.at[parity, me],
                dst_ref=parts.at[parity, me],
                send_sem=send3.at[parity, n],
                recv_sem=recv3.at[parity, n],
                device_id=brick_at(dx, dy),
                device_id_type=MESH,
            )
            cp.start()
            third.append(cp)
        for cp in third:
            cp.wait()
        whole = parts[parity, 0]
        for n in range(1, BRICKS):
            whole = whole + parts[parity, n]
        norm, rw, rs, r_sum = (whole[:, n : n + 1] for n in range(4))
        beta = jnp.where(it == 0, 0.0, norm / norm_prev)
        curve = rw + 2.0 * beta * rs + beta * beta * curve_prev
        alpha = norm / curve
        p = r + beta * direction[...]
        s = w + beta * s_prev
        direction[...] = p
        image[...] = s
        total[...] += alpha * p
        residual[...] = r - alpha * s
        p_sum = r_sum + beta * sum_prev
        return norm, curve, p_sum, sum_total + alpha * p_sum

    zero = jnp.zeros((8, 1), F32)
    state = lax.fori_loop(0, ITERS, sweep, (zero + 1.0, zero, zero, zero))
    sums = state[3]
    ratio = sums[0:PER] / sums[PER:8]
    charge_ref[...] = total[0:PER, :] - ratio * total[PER:8, :]


def energies_kernel(feat_ref, charge_ref, types_ref, w1_ref, w2_ref, w3_ref, out_ref, full):
    full[...] = feat_ref[...]
    for d in range(CHUNKS):
        full[d, FEATS * PER : (FEATS + 1) * PER, :] = charge_ref[:, d * LANES : (d + 1) * LANES]
    heavy = types_ref[...] == 0
    for b in range(PER):
        f = jnp.concatenate(
            [full[d, pl.ds(b, FEATS + 1, stride=PER), :] for d in range(CHUNKS)], 1
        )
        out_ref[b : b + 1, :] = network(f, w1_ref, w2_ref, w3_ref, heavy)


def vmem(count):
    return [pl.BlockSpec(memory_space=pltpu.VMEM)] * count


def params(collective=None):
    if collective is None:
        return pltpu.CompilerParams(vmem_limit_bytes=VMEM_LIMIT)
    return pltpu.CompilerParams(
        vmem_limit_bytes=VMEM_LIMIT, collective_id=collective, has_side_effects=True
    )


def sds(*shape, dtype=F32):
    return jax.ShapeDtypeStruct(shape, dtype)


DMA = pltpu.SemaphoreType.DMA


def propagate(positions, momenta, types, ghost_rows):
    return pl.pallas_call(
        propagate_kernel,
        name="propagate",
        out_shape=(sds(PER, 3, ATOMS), sds(PER, 3, ATOMS), sds(4, 8, TABLE)),
        in_specs=vmem(5),
        out_specs=tuple(vmem(3)),
        scratch_shapes=[
            pltpu.VMEM((8, 3 * ATOMS), F32),
            pltpu.VMEM((64, 3 * LANES), F32),
            pltpu.VMEM((64, 3 * LANES), F32),
            pltpu.VMEM((8, 3 * ATOMS), F32),
            pltpu.VMEM((4, 8, LANES), F32),
            DMA((GROUPS,)),
            DMA((GROUPS,)),
            DMA((GROUPS,)),
            DMA((GROUPS,)),
            DMA((8,)),
            DMA((8,)),
        ],
        compiler_params=params(0),
    )(jnp.asarray(propagator()), positions, momenta, types, ghost_rows)


def features(tab, neighbours, counts, types, w1, w2, w3):
    return pl.pallas_call(
        features_kernel,
        name="features",
        out_shape=(sds(SLOTS, 8, ATOMS), sds(CHUNKS, LANES, LANES), sds(8, ATOMS)),
        in_specs=vmem(7),
        out_specs=tuple(vmem(3)),
        scratch_shapes=[pltpu.VMEM((SLOTS // 2, 8, ATOMS), jnp.int32)],
        compiler_params=params(),
    )(tab, neighbours, counts, types, w1, w2, w3)


def equilibrate(hardness, rhs, coup, neighbours, types, ghost_rows):
    return pl.pallas_call(
        solve_kernel,
        name="equilibrate",
        out_shape=sds(PER, ATOMS),
        in_specs=[pl.BlockSpec(memory_space=pltpu.SMEM)] + vmem(5),
        out_specs=vmem(1)[0],
        scratch_shapes=[
            pltpu.VMEM((SLOTS, 8, ATOMS), jnp.int32),
            pltpu.VMEM((SLOTS, WIDE, ATOMS), BF16),
            pltpu.VMEM((ATOMS, LANES), BF16),
            pltpu.VMEM((8, ATOMS), F32),
            pltpu.VMEM((8, ATOMS), F32),
            pltpu.VMEM((8, ATOMS), F32),
            pltpu.VMEM((8, ATOMS), F32),
            pltpu.VMEM((8, ATOMS), F32),
            pltpu.VMEM((8, TABLE), F32),
            pltpu.VMEM((BLOCKS * BAND, WIDE), F32),
            pltpu.VMEM((9, 8, LANES), F32),
            pltpu.VMEM((1, 8, LANES), F32),
            pltpu.VMEM((9, 8, LANES), F32),
            pltpu.VMEM((2, BRICKS, 8, LANES), F32),
            DMA((8,)),
            DMA((8,)),
            DMA((8,)),
            DMA((8,)),
            DMA((2, BRICKS)),
            DMA((2, BRICKS)),
        ],
        compiler_params=params(1),
    )(hardness, rhs, coup, neighbours, types, ghost_rows)


def final_energies(feats, charges, types, w1, w2, w3):
    return pl.pallas_call(
        energies_kernel,
        name="energies",
        out_shape=sds(PER, ATOMS),
        in_specs=vmem(6),
        out_specs=vmem(1)[0],
        scratch_shapes=[pltpu.VMEM((CHUNKS, LANES, LANES), F32)],
        compiler_params=params(),
    )(feats, charges, types, w1, w2, w3)


def on_device(
    positions,
    momenta,
    types,
    ghost_rows,
    neighbours,
    counts,
    hardness,
    chi_w1,
    chi_w2,
    chi_w3,
    en_w1,
    en_w2,
    en_w3,
):
    types = types.reshape(1, ATOMS)
    counts = counts.reshape(1, ATOMS)
    ghost_rows = ghost_rows.reshape(1, LANES)
    new_positions, new_momenta, tab = propagate(positions, momenta, types, ghost_rows)
    coup, feats, rhs = features(tab, neighbours, counts, types, chi_w1, chi_w2, chi_w3)
    charges = equilibrate(hardness, rhs, coup, neighbours, types, ghost_rows)
    energies = final_energies(feats, charges, types, en_w1, en_w2, en_w3)
    return (new_positions, new_momenta, charges, energies)


def solution(mesh):
    placed = (
        P("bead", None, ("gx", "gy")),
        P("bead", None, ("gx", "gy")),
        P(("gx", "gy")),
        P(("gx", "gy")),
        P(None, ("gx", "gy")),
        P(("gx", "gy")),
        P(),
        P(),
        P(),
        P(),
        P(),
        P(),
        P(),
    )
    return jax.shard_map(
        on_device,
        mesh=mesh,
        in_specs=placed,
        out_specs=(
            P("bead", None, ("gx", "gy")),
            P("bead", None, ("gx", "gy")),
            P("bead", ("gx", "gy")),
            P("bead", ("gx", "gy")),
        ),
        check_vma=False,
    )
```

```python
import functools
import math

import jax
import jax.numpy as jnp
import numpy as np
from jax import lax
from jax.experimental import pallas as pl
from jax.experimental.pallas import tpu as pltpu
from jax.sharding import PartitionSpec as P

MESH = pl.DeviceIdType.MESH
F32 = jnp.float32
BF16 = jnp.bfloat16
HIGHEST = lax.Precision.HIGHEST
ITERS = 5
STEP = 0.5
TOP_FREQ = 80.0
CUTOFF = 4.0
HEAVY_MASS = 16.0
CHI_SCALE = 4.0
LANES = 128
BEADS = 32
GROUPS = 8
PER = 4
ATOMS = 1024
CHUNKS = ATOMS // LANES
SLOTS = 16
TABLE = ATOMS + 8 * LANES
HALF = 15
FEATS = 2 * HALF
SIDE = 4
PAD = 32
BRICKS = SIDE * SIDE
BAND = 16
WIDE = 256
BLOCKS = TABLE // WIDE
OWN_BLOCKS = ATOMS // WIDE
EDGES = SLOTS * ATOMS
GROUP = 4
TOTAL_ATOMS = ATOMS * BRICKS
TINY = 1e-30
SELF = ATOMS + 4 * LANES
VMEM_LIMIT = 60 * 1024 * 1024


def propagator():
    k = np.arange(BEADS)
    omega = TOP_FREQ * np.sin(math.pi * k / BEADS)
    cosine = np.cos(omega * STEP)
    sine = np.sin(omega * STEP)
    drift = np.where(k > 0, TOP_FREQ * sine / np.where(k > 0, omega, 1.0), TOP_FREQ * STEP)
    restoring = -(omega / TOP_FREQ) * sine
    gap = (k[:, None] - k[None, :]) % BEADS

    def spread(weights):
        line = (weights[None, :] * np.cos(2 * math.pi * k[:, None] * k[None, :] / BEADS)).sum(1) / BEADS
        return line[gap]

    keep, push, pull = spread(cosine), spread(drift), spread(restoring)
    zero = np.zeros_like(keep)
    plain = np.block([[keep, zero], [zero, keep]])
    massive = np.block([[zero, push], [pull, zero]])
    order = np.array([half * BEADS + g * PER + b for g in range(GROUPS) for half in range(2) for b in range(PER)])
    both = np.concatenate([plain[order][:, order], massive[order][:, order]], 0)
    return both.astype(np.float32)


def sublanes(shape):
    return lax.broadcasted_iota(jnp.int32, shape, 0)


def lane_take(table, lane):
    return jnp.take_along_axis(table, lane, axis=1, mode="promise_in_bounds")


def row_bits(rows, count):
    return [(rows & (LANES << bit)) != 0 for bit in range(count)]


def pick(parts, bits):
    level = 0
    while len(parts) > 1:
        nxt = [
            jnp.where(bits[level], parts[i + 1], parts[i]) for i in range(0, len(parts) - 1, 2)
        ]
        if len(parts) % 2:
            nxt.append(parts[-1])
        parts = nxt
        level += 1
    return parts[0]


def split(v):
    top = v.astype(BF16).astype(F32)
    return jnp.concatenate([top, v - top], 0).astype(BF16)


def halves(v):
    top = v.astype(BF16)
    return top, (v - top.astype(F32)).astype(BF16)


def lanes_sum(v):
    return jnp.sum(v, axis=1, keepdims=True)


def fold(v, low):
    return jnp.where(low, v, pltpu.roll(v, PER, 0))


def brick_at(dx, dy):
    return {
        "gx": lax.rem(lax.axis_index("gx") + dx + SIDE, SIDE),
        "gy": lax.rem(lax.axis_index("gy") + dy + SIDE, SIDE),
    }


AROUND = [(a, c) for a in range(3) for c in range(3) if (a, c) != (1, 1)]


def load_weights(w1_ref, w2_ref, w3_ref, wide1, wide2, wide3):
    rows, cols = w1_ref.shape[0], w1_ref.shape[2]
    for ref in (wide1, wide2, wide3):
        ref[...] = jnp.zeros_like(ref)
    for e in range(2):
        at = e * PAD
        wide1[at : at + rows, 0:cols] = w1_ref[:, e, :]
        wide2[at : at + rows, at : at + rows] = w2_ref[:, e, :]
        wide3[e : e + 1, at : at + rows] = w3_ref[e : e + 1, :]


def product(w, f):
    w_top, w_rest = halves(w)
    f_top, f_rest = halves(f)
    rows = w.shape[0]
    both = jnp.dot(jnp.concatenate([w_top, w_rest], 0), f_top, preferred_element_type=F32)
    return both[0:rows] + both[rows:] + jnp.dot(w_top, f_rest, preferred_element_type=F32)


def network(feat_ref, wide1, wide2, wide3, heavy):
    f = jnp.concatenate(
        [feat_ref[d, pl.ds(b, PAD, stride=PER), :] for b in range(PER) for d in range(CHUNKS)], 1
    )
    h = jnp.tanh(product(wide1[...], f))
    h = jnp.tanh(product(wide2[...], h))
    out = product(wide3[...], h)
    return [
        jnp.where(
            heavy, out[0:1, b * ATOMS : (b + 1) * ATOMS], out[1:2, b * ATOMS : (b + 1) * ATOMS]
        )
        for b in range(PER)
    ]


def main_kernel(
    hardness_ref,
    matrix_ref,
    pos_ref,
    mom_ref,
    types_ref,
    ghost_ref,
    idx_ref,
    counts_ref,
    w1_ref,
    w2_ref,
    w3_ref,
    newpos_ref,
    newmom_ref,
    charge_ref,
    feat_ref,
    stage,
    modes,
    moved,
    back,
    lent_pos,
    lent_heavy,
    tab,
    idx16,
    heavy16,
    rows_all,
    pairs,
    heavy_pairs,
    block_ids,
    onehot,
    onehot_t,
    ghost_onehot,
    coup,
    coup_own,
    coup_ghost,
    dist,
    weight_h,
    weight_l,
    wide1,
    wide2,
    wide3,
    residual,
    image,
    image2,
    direction,
    steps,
    total,
    degree,
    ghost_table,
    spread,
    lent,
    backin,
    parts,
    send1,
    recv1,
    send2,
    recv2,
    send3,
    recv3,
    send4,
    recv4,
    send_a,
    recv_a,
    send_b,
    recv_b,
    send_d,
    recv_d,
):
    group = lax.axis_index("bead")
    me = lax.axis_index("gx") * SIDE + lax.axis_index("gy")
    others = [(o // SIDE, o % SIDE) for o in range(1, BRICKS)]
    barrier = pltpu.get_barrier_semaphore()
    for o in range(1, GROUPS):
        pl.semaphore_signal(
            barrier, inc=1, device_id={"bead": lax.rem(group + o, GROUPS)}, device_id_type=MESH
        )
    for dx, dy in others:
        pl.semaphore_signal(barrier, inc=1, device_id=brick_at(dx, dy), device_id_type=MESH)

    low = sublanes((8, LANES)) < PER
    low_all = sublanes((8, ATOMS)) < PER
    own_width = 3 * LANES
    width = 2 * own_width
    ghost_rows = jnp.broadcast_to(ghost_ref[...], (8, LANES))
    ghost_lane = ghost_rows & (LANES - 1)
    ghost_bits = row_bits(ghost_rows, 3)

    def at_ghosts(v):
        return pick(
            [lane_take(v[:, d * LANES : (d + 1) * LANES], ghost_lane) for d in range(CHUNKS)],
            ghost_bits,
        )

    heavy_row = types_ref[...] == 0
    heavy = jnp.where(heavy_row, 1.0, 0.0)
    tab[3, :, 0:ATOMS] = jnp.broadcast_to(heavy, (8, ATOMS))
    ghost_heavy = at_ghosts(jnp.broadcast_to(heavy, (8, ATOMS)))
    lent_heavy[...] = ghost_heavy
    for c in range(3):
        v = jnp.concatenate([pos_ref[c], mom_ref[c]], 0)
        g = at_ghosts(v)
        for d in range(CHUNKS):
            at = d * width + c * LANES
            stage[:, at : at + LANES] = v[:, d * LANES : (d + 1) * LANES]
            stage[:, at + own_width : at + own_width + LANES] = g
    pl.semaphore_wait(barrier, GROUPS - 1 + len(others))

    mine = pl.ds(pl.multiple_of(group * 8, 8), 8)
    mine_too = pl.ds(pl.multiple_of(64 + group * 8, 8), 8)
    copies = []
    for o in range(1, GROUPS):
        to = lax.rem(group + o, GROUPS)
        cp = pltpu.make_async_remote_copy(
            src_ref=stage.at[:, pl.ds(pl.multiple_of(to * width, LANES), width)],
            dst_ref=modes.at[mine, :],
            send_sem=send1.at[o],
            recv_sem=recv1.at[o],
            device_id={"bead": to},
            device_id_type=MESH,
        )
        cp.start()
        copies.append(cp)
    heavy_copies = []
    for g, (a, c) in enumerate(AROUND):
        at = ATOMS + g * LANES
        cp = pltpu.make_async_remote_copy(
            src_ref=lent_heavy,
            dst_ref=tab.at[3, :, at : at + LANES],
            send_sem=send4.at[g],
            recv_sem=recv4.at[g],
            device_id=brick_at(1 - a, 1 - c),
            device_id_type=MESH,
        )
        cp.start()
        heavy_copies.append(cp)
    modes[mine, :] = stage[:, pl.ds(pl.multiple_of(group * width, LANES), width)]

    for half in range(2):
        for d in range(CHUNKS):
            lanes = slice(d * LANES, (d + 1) * LANES)
            rows = idx_ref[half * 8 : half * 8 + 8, lanes]
            local = lane_take(ghost_rows, rows & (LANES - 1))
            rows = jnp.where(
                rows < SELF, rows, jnp.where(rows < SELF + LANES, local, rows - LANES)
            )
            idx16[half * 8 : half * 8 + 8, lanes] = rows
    for k in range(SLOTS):
        rows_all[k] = jnp.broadcast_to(idx16[k : k + 1, :], (8, ATOMS))
        block_ids[k] = jnp.broadcast_to(
            (idx16[k : k + 1, :] >> 8).astype(F32), (BAND, ATOMS)
        ).astype(BF16)
    for kp in range(SLOTS // 2):
        pairs[kp] = jnp.where(low_all, rows_all[2 * kp], rows_all[2 * kp + 1])
    within = sublanes((WIDE, ATOMS)).astype(F32).astype(BF16)
    for k in range(SLOTS):
        wide = jnp.broadcast_to((idx16[k : k + 1, :] & (WIDE - 1)).astype(F32), (BAND, ATOMS))
        wide = jnp.concatenate([wide.astype(BF16)] * (WIDE // BAND), 0)
        onehot[:, k * ATOMS : (k + 1) * ATOMS] = jnp.where(within == wide, 1.0, 0.0).astype(BF16)
    for d in range(CHUNKS):
        rows = sublanes((LANES, LANES)) + d * LANES
        hit = rows == jnp.broadcast_to(ghost_ref[...], (LANES, LANES))
        ghost_onehot[d * LANES : (d + 1) * LANES, :] = jnp.where(hit, 1.0, 0.0).astype(BF16)
    load_weights(w1_ref, w2_ref, w3_ref, wide1, wide2, wide3)
    my_types = types_ref[:, pl.ds(pl.multiple_of(group * LANES, LANES), LANES)]
    mass = jnp.broadcast_to(jnp.where(my_types == 0, HEAVY_MASS, 1.0), (8, LANES))
    factor = jnp.concatenate([jnp.where(low, 1.0 / mass, mass)] * 3, 1)
    ghost_mass = jnp.where(ghost_heavy > 0.0, HEAVY_MASS, 1.0)
    ghost_factor = jnp.concatenate([1.0 / ghost_mass] * 3, 1)

    for cp in copies:
        cp.wait()
    ghost_matrix = jnp.concatenate([matrix_ref[mine, :], matrix_ref[mine_too, :]], 0)
    both = jnp.dot(
        ghost_matrix, modes[:, own_width:width], precision=HIGHEST, preferred_element_type=F32
    )
    ghost_pos = both[0:8] + both[8:16] * ghost_factor
    for c in range(3):
        lent_pos[c] = fold(ghost_pos[:, c * LANES : (c + 1) * LANES], low)
    pos_copies = []
    for g, (a, c) in enumerate(AROUND):
        at = ATOMS + g * LANES
        cp = pltpu.make_async_remote_copy(
            src_ref=lent_pos,
            dst_ref=tab.at[0:3, :, at : at + LANES],
            send_sem=send3.at[g],
            recv_sem=recv3.at[g],
            device_id=brick_at(1 - a, 1 - c),
            device_id_type=MESH,
        )
        cp.start()
        pos_copies.append(cp)
    both = jnp.dot(
        matrix_ref[...], modes[:, 0:own_width], precision=HIGHEST, preferred_element_type=F32
    )
    for g in range(GROUPS):
        rows = slice(g * 8, g * 8 + 8)
        moved[rows, :] = both[rows] + both[64 + g * 8 : 72 + g * 8] * factor
    my_lanes = pl.ds(pl.multiple_of(group * own_width, LANES), own_width)
    copies = []
    for o in range(1, GROUPS):
        to = lax.rem(group + o, GROUPS)
        cp = pltpu.make_async_remote_copy(
            src_ref=moved.at[pl.ds(pl.multiple_of(to * 8, 8), 8), :],
            dst_ref=back.at[:, my_lanes],
            send_sem=send2.at[o],
            recv_sem=recv2.at[o],
            device_id={"bead": to},
            device_id_type=MESH,
        )
        cp.start()
        copies.append(cp)
    back[:, my_lanes] = moved[mine, :]

    for cp in heavy_copies:
        cp.wait()
    for half in range(2):
        for d in range(CHUNKS):
            lanes = slice(d * LANES, (d + 1) * LANES)
            rows = idx16[half * 8 : half * 8 + 8, lanes]
            lane = rows & (LANES - 1)
            heavy16[half * 8 : half * 8 + 8, lanes] = pick(
                [
                    lane_take(tab[3, :, t * LANES : (t + 1) * LANES], lane)
                    for t in range(TABLE // LANES)
                ],
                row_bits(rows, 4),
            )
    for kp in range(SLOTS // 2):
        heavy_pairs[kp] = jnp.where(
            low_all,
            jnp.broadcast_to(heavy16[2 * kp : 2 * kp + 1, :], (8, ATOMS)),
            jnp.broadcast_to(heavy16[2 * kp + 1 : 2 * kp + 2, :], (8, ATOMS)),
        )
    for k in range(SLOTS):
        onehot_t[k * ATOMS : (k + 1) * ATOMS, :] = jnp.transpose(
            onehot[:, k * ATOMS : (k + 1) * ATOMS]
        )

    for cp in copies:
        cp.wait()
    for c in range(3):
        for d in range(CHUNKS):
            at = d * own_width + c * LANES
            v = back[:, at : at + LANES]
            newpos_ref[c, :, d * LANES : (d + 1) * LANES] = v[0:PER]
            newmom_ref[c, :, d * LANES : (d + 1) * LANES] = v[PER:8]
            tab[c, :, d * LANES : (d + 1) * LANES] = fold(v, low)
    for cp in pos_copies:
        cp.wait()

    slot_off = jnp.where(low, 0, 1)
    cos_scale = (math.pi / (2.0 * CUTOFF)) ** 2
    cos_terms = [(-1.0) ** n * cos_scale**n / math.factorial(2 * n) for n in range(8)]

    def geometry(ci, carry):
        lanes = pl.ds(pl.multiple_of(ci * LANES, LANES), LANES)
        own = [tab[c, :, lanes] for c in range(3)]
        count = jnp.broadcast_to(counts_ref[:, lanes], (8, LANES))
        for kp in range(SLOTS // 2):
            rows = pairs[kp, :, lanes]
            lane = rows & (LANES - 1)
            bits = row_bits(rows, 4)
            dist_sq = jnp.zeros((8, LANES), F32)
            for c in range(3):
                near = pick(
                    [
                        lane_take(tab[c, :, t * LANES : (t + 1) * LANES], lane)
                        for t in range(TABLE // LANES)
                    ],
                    bits,
                )
                dist_sq = dist_sq + (near - own[c]) ** 2
            close = jnp.minimum(dist_sq, CUTOFF * CUTOFF)
            wave = jnp.full_like(close, cos_terms[-1])
            for term in cos_terms[-2::-1]:
                wave = wave * close + term
            used = ((2 * kp + slot_off) < count) & (dist_sq < CUTOFF * CUTOFF)
            smooth = jnp.where(used, wave * wave, 0.0)
            heavy_w = smooth * heavy_pairs[kp, :, lanes]
            dist[kp, :, lanes] = dist_sq
            weight_h[kp, :, lanes] = heavy_w
            weight_l[kp, :, lanes] = smooth - heavy_w
            coupling = smooth * lax.rsqrt(1.0 + dist_sq)
            turned = pltpu.roll(coupling, PER, 0)
            for k, v in ((2 * kp, jnp.where(low, coupling, turned)), (2 * kp + 1, jnp.where(low, turned, coupling))):
                inside = rows_all[k, :, lanes] < ATOMS
                coup[k, :, lanes] = v
                coup_own[k, :, lanes] = jnp.where(inside, v, 0.0)
                coup_ghost[k, :, lanes] = jnp.where(inside, 0.0, v)
        return carry

    lax.fori_loop(0, CHUNKS, geometry, 0)

    def scatter(terms_of):
        acc = jnp.zeros((BLOCKS * BAND, WIDE), F32)
        for g in range(SLOTS // GROUP):
            tall = []
            for k in range(g * GROUP, (g + 1) * GROUP):
                terms = split(terms_of(k))
                zero = jnp.zeros_like(terms)
                ids = block_ids[k]
                tall.append(
                    jnp.concatenate([jnp.where(ids == b, terms, zero) for b in range(BLOCKS)], 0)
                )
            rows = slice(g * GROUP * ATOMS, (g + 1) * GROUP * ATOMS)
            acc = acc + jnp.dot(
                jnp.concatenate(tall, 1), onehot_t[rows, :], preferred_element_type=F32
            )
        return acc

    def chunk_of(acc, n):
        row, col = (n // 2) * BAND, (n % 2) * LANES
        return acc[row : row + 8, col : col + LANES] + acc[row + 8 : row + 16, col : col + LANES]

    def send_back(acc, par):
        out = []
        for g, (a, c) in enumerate(AROUND):
            spread[par, g] = chunk_of(acc, CHUNKS + g)
        for g, (a, c) in enumerate(AROUND):
            cp = pltpu.make_async_remote_copy(
                src_ref=spread.at[par, g],
                dst_ref=backin.at[par, g],
                send_sem=send_b.at[par, g],
                recv_sem=recv_b.at[par, g],
                device_id=brick_at(a - 1, c - 1),
                device_id_type=MESH,
            )
            cp.start()
            out.append(cp)
        return out

    def own_part(acc):
        return jnp.concatenate([chunk_of(acc, d) for d in range(CHUNKS)], 1)

    def take_back(copies, par):
        for cp in copies:
            cp.wait()
        received = backin[par, 0]
        for g in range(1, len(AROUND)):
            received = received + backin[par, g]
        returned = lax.dot_general(
            split(received), ghost_onehot[...], (((1,), (1,)), ((), ())), preferred_element_type=F32
        )
        return returned[0:8] + returned[8:16]

    def forward(v, weights, acc):
        tall = jnp.concatenate(
            [split(v[:, q * WIDE : (q + 1) * WIDE]) for q in range(OWN_BLOCKS)], 0
        )
        for g in range(SLOTS // GROUP):
            cols = slice(g * GROUP * ATOMS, (g + 1) * GROUP * ATOMS)
            found = jnp.dot(tall, onehot[:, cols], preferred_element_type=F32)
            for kk in range(GROUP):
                k = g * GROUP + kk
                f = found[:, kk * ATOMS : (kk + 1) * ATOMS]
                near = [
                    f[q * BAND : q * BAND + 8] + f[q * BAND + 8 : q * BAND + 16]
                    for q in range(OWN_BLOCKS)
                ]
                rows = rows_all[k]
                acc = acc + weights[k] * pick(near, [(rows & WIDE) != 0, (rows & (2 * WIDE)) != 0])
        return acc

    acc = scatter(lambda k: coup[k])
    first_back = send_back(acc, 1)
    degree[...] = own_part(acc)

    feat_ref[...] = jnp.zeros_like(feat_ref)

    def radial(ci, carry):
        lanes = pl.ds(pl.multiple_of(ci * LANES, LANES), LANES)
        sums = [jnp.zeros((8, LANES), F32) for _ in range(FEATS)]
        for kp in range(SLOTS // 2):
            d = dist[kp, :, lanes]
            wh = weight_h[kp, :, lanes]
            wl = weight_l[kp, :, lanes]
            for s in range(HALF):
                eta = 0.2 * 20.0 ** (s / (HALF - 1))
                falloff = jnp.exp(d * (-eta))
                sums[s] = sums[s] + wh * falloff
                sums[HALF + s] = sums[HALF + s] + wl * falloff
        for s in range(FEATS):
            v = jnp.log(1.0 + (sums[s] + pltpu.roll(sums[s], PER, 0)))
            feat_ref[ci, s * PER : (s + 1) * PER, :] = v[0:PER]
        return carry

    lax.fori_loop(0, CHUNKS, radial, 0)
    for b, chi in enumerate(network(feat_ref, wide1, wide2, wide3, heavy_row)):
        residual[b : b + 1, :] = -CHI_SCALE * chi
    residual[PER:8, :] = jnp.broadcast_to(1.0 - heavy, (PER, ATOMS))
    around = degree[...] + take_back(first_back, 1)
    for k in range(SLOTS):
        around = around + coup[k]
    h0, h1 = hardness_ref[0], hardness_ref[1]
    hard = jnp.where(heavy_row, h0, h1)
    degree[...] = hard + 0.5 * around

    def apply(ref, par, dots):
        lent[par] = at_ghosts(ref[...])
        first = []
        for g, (a, c) in enumerate(AROUND):
            cp = pltpu.make_async_remote_copy(
                src_ref=lent.at[par],
                dst_ref=ghost_table.at[par, :, g * LANES : (g + 1) * LANES],
                send_sem=send_a.at[par, g],
                recv_sem=recv_a.at[par, g],
                device_id=brick_at(1 - a, 1 - c),
                device_id_type=MESH,
            )
            cp.start()
            first.append(cp)
        third = send_dots(par) if dots else []
        acc = scatter(lambda k: coup[k] * ref[...])
        second = send_back(acc, par)
        around = forward(ref[...], coup_own, own_part(acc))
        for cp in first:
            cp.wait()
        around = forward(ghost_table[par], coup_ghost, around)
        around = around + take_back(second, par)
        return degree[...] * ref[...] - 0.5 * around, third

    lane_id = lax.broadcasted_iota(jnp.int32, (8, LANES), 1)

    def send_dots(par):
        r = residual[...]
        dots = [lanes_sum(r * r), lanes_sum(r * image[...]), lanes_sum(r * steps[...]), lanes_sum(r)]
        v = dots[3]
        for n in (2, 1, 0):
            v = jnp.where(lane_id == n, dots[n], v)
        parts[par, me] = v
        out = []
        for n, (dx, dy) in enumerate(others):
            cp = pltpu.make_async_remote_copy(
                src_ref=parts.at[par, me],
                dst_ref=parts.at[par, me],
                send_sem=send_d.at[par, n],
                recv_sem=recv_d.at[par, n],
                device_id=brick_at(dx, dy),
                device_id_type=MESH,
            )
            cp.start()
            out.append(cp)
        return out

    def take_dots(copies, par):
        for cp in copies:
            cp.wait()
        whole = parts[par, 0]
        for n in range(1, BRICKS):
            whole = whole + parts[par, n]
        return [whole[:, n : n + 1] for n in range(4)]

    alpha_max = 2.0 / jnp.minimum(h0, h1)

    def step_sizes(dots, state, start):
        norm, rw, rs, r_sum = dots
        norm_prev, curve_prev, sum_prev, sum_total = state
        beta = jnp.where(start, 0.0, norm / jnp.maximum(norm_prev, TINY))
        curve = rw + 2.0 * beta * rs + beta * beta * curve_prev
        alpha = jnp.minimum(norm / jnp.maximum(curve, TINY), alpha_max)
        p_sum = r_sum + beta * sum_prev
        return alpha, beta, (norm, curve, p_sum, sum_total + alpha * p_sum)

    image[...] = apply(residual, 0, False)[0]
    for ref in (direction, steps, image2, total):
        ref[...] = jnp.zeros_like(ref)
    high = jnp.logical_not(low_all)
    high_col = sublanes((8, 1)) >= PER

    def sweep(it, state):
        par = lax.rem(it + 1, 2)
        start = it == 0
        q, third = apply(image, par, True)
        dots = take_dots(third, par)
        light = dots[3]
        alpha, beta, state = step_sizes(dots, state, start)
        r, w = residual[...], image[...]
        z = q + beta * image2[...]
        s = w + beta * steps[...]
        p = r + beta * direction[...]
        x = total[...] + alpha * p
        r_new = r - alpha * s
        w_new = w - alpha * z
        known = jnp.logical_and(start, high)
        gap = h1 - h0
        hard_sum = (TOTAL_ATOMS - light) * h0 + light * h1
        c0 = light / hard_sum
        c1 = -TOTAL_ATOMS / hard_sum
        direction[...] = jnp.where(known, 1.0, p)
        steps[...] = jnp.where(known, hard, s)
        image2[...] = jnp.where(known, h0 * hard + gap * w, z)
        total[...] = jnp.where(known, TOTAL_ATOMS / hard_sum, x)
        residual[...] = jnp.where(known, gap * (c0 + c1 * r), r_new)
        image[...] = jnp.where(known, gap * (c0 * hard + c1 * w), w_new)
        exact = (
            jnp.full((8, 1), TOTAL_ATOMS, F32),
            hard_sum,
            jnp.full((8, 1), TOTAL_ATOMS, F32),
            TOTAL_ATOMS / hard_sum * TOTAL_ATOMS,
        )
        known_col = jnp.logical_and(start, high_col)
        return tuple(jnp.where(known_col, e, v) for e, v in zip(exact, state))

    zero = jnp.zeros((8, 1), F32)
    state = lax.fori_loop(0, ITERS - 1, sweep, (zero + 1.0, zero, zero, zero))
    par = ITERS % 2
    dots = take_dots(send_dots(par), par)
    alpha, beta, state = step_sizes(dots, state, False)
    x = total[...] + alpha * (residual[...] + beta * direction[...])
    sums = state[3]
    charge_ref[...] = x[0:PER] - (sums[0:PER] / sums[PER:8]) * x[PER:8]


def energies_kernel(
    feat_ref,
    charge_ref,
    newpos_ref,
    newmom_ref,
    types_ref,
    w1_ref,
    w2_ref,
    w3_ref,
    pos_out,
    mom_out,
    charge_out,
    out_ref,
    full,
    wide1,
    wide2,
    wide3,
):
    pos_out[...] = newpos_ref[...]
    mom_out[...] = newmom_ref[...]
    charge_out[...] = charge_ref[...]
    load_weights(w1_ref, w2_ref, w3_ref, wide1, wide2, wide3)
    full[...] = feat_ref[...]
    for d in range(CHUNKS):
        full[d, FEATS * PER : (FEATS + 1) * PER, :] = charge_ref[:, d * LANES : (d + 1) * LANES]
    for b, e in enumerate(network(full, wide1, wide2, wide3, types_ref[...] == 0)):
        out_ref[b : b + 1, :] = e


def vmem(count):
    return [pl.BlockSpec(memory_space=pltpu.VMEM)] * count


def sds(*shape, dtype=F32):
    return jax.ShapeDtypeStruct(shape, dtype)


def f32(*shape):
    return pltpu.VMEM(shape, F32)


def on_device(
    positions,
    momenta,
    types,
    ghost_rows,
    neighbours,
    counts,
    hardness,
    chi_w1,
    chi_w2,
    chi_w3,
    en_w1,
    en_w2,
    en_w3,
):
    types = types.reshape(1, ATOMS)
    counts = counts.reshape(1, ATOMS)
    ghost_rows = ghost_rows.reshape(1, LANES)
    turn = lambda v: jnp.transpose(v, (1, 0, 2))
    dma = pltpu.SemaphoreType.DMA
    i32 = jnp.int32
    networks = [f32(2 * PAD, PAD), f32(2 * PAD, 2 * PAD), f32(8, 2 * PAD)]
    new_pos, new_mom, charges, feats = pl.pallas_call(
        main_kernel,
        name="main",
        out_shape=(
            sds(3, PER, ATOMS),
            sds(3, PER, ATOMS),
            sds(PER, ATOMS),
            sds(CHUNKS, LANES, LANES),
        ),
        in_specs=[pl.BlockSpec(memory_space=pltpu.SMEM)] + vmem(10),
        out_specs=tuple(vmem(4)),
        scratch_shapes=[
            f32(8, 6 * ATOMS),
            f32(64, 6 * LANES),
            f32(64, 3 * LANES),
            f32(8, 3 * ATOMS),
            f32(3, 8, LANES),
            f32(8, LANES),
            f32(4, 8, TABLE),
            pltpu.VMEM((SLOTS, ATOMS), i32),
            f32(SLOTS, ATOMS),
            pltpu.VMEM((SLOTS, 8, ATOMS), i32),
            pltpu.VMEM((SLOTS // 2, 8, ATOMS), i32),
            f32(SLOTS // 2, 8, ATOMS),
            pltpu.VMEM((SLOTS, BAND, ATOMS), BF16),
            pltpu.VMEM((WIDE, EDGES), BF16),
            pltpu.VMEM((EDGES, WIDE), BF16),
            pltpu.VMEM((ATOMS, LANES), BF16),
            f32(SLOTS, 8, ATOMS),
            f32(SLOTS, 8, ATOMS),
            f32(SLOTS, 8, ATOMS),
            f32(SLOTS // 2, 8, ATOMS),
            f32(SLOTS // 2, 8, ATOMS),
            f32(SLOTS // 2, 8, ATOMS),
            *networks,
            *[f32(8, ATOMS) for _ in range(7)],
            f32(2, 8, ATOMS),
            f32(2, 8, 8, LANES),
            f32(2, 8, LANES),
            f32(2, 8, 8, LANES),
            f32(2, BRICKS, 8, LANES),
            *[dma((GROUPS,)) for _ in range(4)],
            *[dma((8,)) for _ in range(4)],
            *[dma((2, 8)) for _ in range(4)],
            *[dma((2, BRICKS)) for _ in range(2)],
        ],
        compiler_params=pltpu.CompilerParams(
            vmem_limit_bytes=VMEM_LIMIT, collective_id=0, has_side_effects=True
        ),
    )(
        hardness,
        jnp.asarray(propagator()),
        turn(positions),
        turn(momenta),
        types,
        ghost_rows,
        neighbours,
        counts,
        turn(chi_w1),
        turn(chi_w2),
        chi_w3,
    )
    new_pos, new_mom, charges, energies = pl.pallas_call(
        energies_kernel,
        name="energies",
        out_shape=(sds(3, PER, ATOMS), sds(3, PER, ATOMS), sds(PER, ATOMS), sds(PER, ATOMS)),
        in_specs=vmem(8),
        out_specs=tuple(vmem(4)),
        scratch_shapes=[f32(CHUNKS, LANES, LANES), *networks],
        compiler_params=pltpu.CompilerParams(vmem_limit_bytes=VMEM_LIMIT),
    )(feats, charges, new_pos, new_mom, types, turn(en_w1), turn(en_w2), en_w3)
    return (turn(new_pos), turn(new_mom), charges, energies)


def solution(mesh):
    placed = (
        P("bead", None, ("gx", "gy")),
        P("bead", None, ("gx", "gy")),
        P(("gx", "gy")),
        P(("gx", "gy")),
        P(None, ("gx", "gy")),
        P(("gx", "gy")),
        P(),
        P(),
        P(),
        P(),
        P(),
        P(),
        P(),
    )
    return jax.shard_map(
        on_device,
        mesh=mesh,
        in_specs=placed,
        out_specs=(
            P("bead", None, ("gx", "gy")),
            P("bead", None, ("gx", "gy")),
            P("bead", ("gx", "gy")),
            P("bead", ("gx", "gy")),
        ),
        check_vma=False,
    )
```

```python
import functools
import math

import jax
import jax.numpy as jnp
import numpy as np
from jax import lax
from jax.experimental import pallas as pl
from jax.experimental.pallas import tpu as pltpu
from jax.sharding import PartitionSpec as P

MESH = pl.DeviceIdType.MESH
F32 = jnp.float32
BF16 = jnp.bfloat16
HIGHEST = lax.Precision.HIGHEST
ITERS = 5
STEP = 0.5
TOP_FREQ = 80.0
CUTOFF = 4.0
HEAVY_MASS = 16.0
CHI_SCALE = 4.0
LANES = 128
BEADS = 32
GROUPS = 8
PER = 4
ATOMS = 1024
CHUNKS = ATOMS // LANES
SLOTS = 16
TABLE = ATOMS + 8 * LANES
HALF = 15
FEATS = 2 * HALF
SIDE = 4
PAD = 32
BRICKS = SIDE * SIDE
BAND = 16
WIDE = 256
BLOCKS = TABLE // WIDE
OWN_BLOCKS = ATOMS // WIDE
EDGES = SLOTS * ATOMS
GROUP = 4
TOTAL_ATOMS = ATOMS * BRICKS
TINY = 1e-30
SELF = ATOMS + 4 * LANES
VMEM_LIMIT = 60 * 1024 * 1024


def propagator():
    k = np.arange(BEADS)
    omega = TOP_FREQ * np.sin(math.pi * k / BEADS)
    cosine = np.cos(omega * STEP)
    sine = np.sin(omega * STEP)
    drift = np.where(k > 0, TOP_FREQ * sine / np.where(k > 0, omega, 1.0), TOP_FREQ * STEP)
    restoring = -(omega / TOP_FREQ) * sine
    gap = (k[:, None] - k[None, :]) % BEADS

    def spread(weights):
        line = (weights[None, :] * np.cos(2 * math.pi * k[:, None] * k[None, :] / BEADS)).sum(1) / BEADS
        return line[gap]

    keep, push, pull = spread(cosine), spread(drift), spread(restoring)
    zero = np.zeros_like(keep)
    plain = np.block([[keep, zero], [zero, keep]])
    massive = np.block([[zero, push], [pull, zero]])
    order = np.array([half * BEADS + g * PER + b for g in range(GROUPS) for half in range(2) for b in range(PER)])
    both = np.concatenate([plain[order][:, order], massive[order][:, order]], 0)
    return both.astype(np.float32)


def sublanes(shape):
    return lax.broadcasted_iota(jnp.int32, shape, 0)


def lane_take(table, lane):
    return jnp.take_along_axis(table, lane, axis=1, mode="promise_in_bounds")


def row_bits(rows, count):
    return [(rows & (LANES << bit)) != 0 for bit in range(count)]


def pick(parts, bits):
    level = 0
    while len(parts) > 1:
        nxt = [
            jnp.where(bits[level], parts[i + 1], parts[i]) for i in range(0, len(parts) - 1, 2)
        ]
        if len(parts) % 2:
            nxt.append(parts[-1])
        parts = nxt
        level += 1
    return parts[0]


def split(v):
    top = v.astype(BF16).astype(F32)
    return jnp.concatenate([top, v - top], 0).astype(BF16)


def halves(v):
    top = v.astype(BF16)
    return top, (v - top.astype(F32)).astype(BF16)


def lanes_sum(v):
    return jnp.sum(v, axis=1, keepdims=True)


def fold(v, low):
    return jnp.where(low, v, pltpu.roll(v, PER, 0))


def brick_at(dx, dy):
    return {
        "gx": lax.rem(lax.axis_index("gx") + dx + SIDE, SIDE),
        "gy": lax.rem(lax.axis_index("gy") + dy + SIDE, SIDE),
    }


AROUND = [(a, c) for a in range(3) for c in range(3) if (a, c) != (1, 1)]


def load_weights(w1_ref, w2_ref, w3_ref, wide1, wide2, wide3):
    rows, cols = w1_ref.shape[0], w1_ref.shape[2]
    for ref in (wide1, wide2, wide3):
        ref[...] = jnp.zeros_like(ref)
    for e in range(2):
        at = e * PAD
        wide1[at : at + rows, 0:cols] = w1_ref[:, e, :]
        wide2[at : at + rows, at : at + rows] = w2_ref[:, e, :]
        wide3[e : e + 1, at : at + rows] = w3_ref[e : e + 1, :]


def product(w, f):
    w_top, w_rest = halves(w)
    f_top, f_rest = halves(f)
    rows = w.shape[0]
    both = jnp.dot(jnp.concatenate([w_top, w_rest], 0), f_top, preferred_element_type=F32)
    return both[0:rows] + both[rows:] + jnp.dot(w_top, f_rest, preferred_element_type=F32)


def features_of(feat_ref):
    return jnp.concatenate(
        [feat_ref[d, pl.ds(b, PAD, stride=PER), :] for b in range(PER) for d in range(CHUNKS)], 1
    )


def network(hidden, wide2, wide3, heavy):
    h = jnp.tanh(product(wide2[...], jnp.tanh(hidden)))
    out = product(wide3[...], h)
    return [
        jnp.where(
            heavy, out[0:1, b * ATOMS : (b + 1) * ATOMS], out[1:2, b * ATOMS : (b + 1) * ATOMS]
        )
        for b in range(PER)
    ]


def main_kernel(
    hardness_hbm,
    matrix_hbm,
    pos_hbm,
    mom_hbm,
    types_hbm,
    ghost_hbm,
    idx_hbm,
    counts_hbm,
    w1_hbm,
    w2_hbm,
    w3_hbm,
    v1_hbm,
    v2_hbm,
    v3_hbm,
    newpos_hbm,
    newmom_hbm,
    charge_hbm,
    energy_hbm,
    hardness_ref,
    matrix_ref,
    pos_ref,
    mom_ref,
    types_ref,
    ghost_ref,
    idx_ref,
    counts_ref,
    w1_ref,
    w2_ref,
    w3_ref,
    v1_ref,
    v2_ref,
    v3_ref,
    newpos_ref,
    newmom_ref,
    charge_ref,
    energy_ref,
    feat_ref,
    stage,
    modes,
    moved,
    back,
    lent_pos,
    lent_heavy,
    tab,
    idx16,
    heavy16,
    rows_all,
    pairs,
    heavy_pairs,
    block_ids,
    onehot,
    onehot_t,
    ghost_onehot,
    coup,
    dist,
    weight_h,
    weight_l,
    wide1,
    wide2,
    wide3,
    last1,
    last2,
    last3,
    first_layer,
    residual,
    image,
    image2,
    direction,
    steps,
    total,
    degree,
    spread,
    lent,
    ghost_in,
    backin,
    parts,
    send1,
    recv1,
    send2,
    recv2,
    send3,
    recv3,
    send4,
    recv4,
    send_a,
    recv_a,
    send_b,
    recv_b,
    send_d,
    recv_d,
    loads,
    stores,
):
    group = lax.axis_index("bead")
    me = lax.axis_index("gx") * SIDE + lax.axis_index("gy")
    others = [(o // SIDE, o % SIDE) for o in range(1, BRICKS)]
    barrier = pltpu.get_barrier_semaphore()
    for o in range(1, GROUPS):
        pl.semaphore_signal(
            barrier, inc=1, device_id={"bead": lax.rem(group + o, GROUPS)}, device_id_type=MESH
        )
    for a, c in AROUND:
        pl.semaphore_signal(barrier, inc=1, device_id=brick_at(a - 1, c - 1), device_id_type=MESH)
    loading = [
        pltpu.make_async_copy(src, dst, loads.at[n])
        for n, (src, dst) in enumerate(
            (
                (pos_hbm, pos_ref),
                (mom_hbm, mom_ref),
                (ghost_hbm, ghost_ref),
                (types_hbm, types_ref),
                (idx_hbm, idx_ref),
                (matrix_hbm, matrix_ref),
                (counts_hbm, counts_ref),
                (hardness_hbm, hardness_ref),
                (w1_hbm, w1_ref),
                (w2_hbm, w2_ref),
                (w3_hbm, w3_ref),
                (v1_hbm, v1_ref),
                (v2_hbm, v2_ref),
                (v3_hbm, v3_ref),
            )
        )
    ]
    for cp in loading:
        cp.start()
    for cp in loading[0:4]:
        cp.wait()

    low = sublanes((8, LANES)) < PER
    low_all = sublanes((8, ATOMS)) < PER
    own_width = 3 * LANES
    width = 2 * own_width
    ghost_rows = jnp.broadcast_to(ghost_ref[...], (8, LANES))
    ghost_lane = ghost_rows & (LANES - 1)
    ghost_bits = row_bits(ghost_rows, 3)

    def at_ghosts(v):
        return pick(
            [lane_take(v[:, d * LANES : (d + 1) * LANES], ghost_lane) for d in range(CHUNKS)],
            ghost_bits,
        )

    heavy_row = types_ref[...] == 0
    heavy = jnp.where(heavy_row, 1.0, 0.0)
    tab[3, :, 0:ATOMS] = jnp.broadcast_to(heavy, (8, ATOMS))
    ghost_heavy = at_ghosts(jnp.broadcast_to(heavy, (8, ATOMS)))
    lent_heavy[...] = ghost_heavy
    for c in range(3):
        v = jnp.concatenate([pos_ref[c], mom_ref[c]], 0)
        g = at_ghosts(v)
        for d in range(CHUNKS):
            at = d * width + c * LANES
            stage[:, at : at + LANES] = v[:, d * LANES : (d + 1) * LANES]
            stage[:, at + own_width : at + own_width + LANES] = g
    pl.semaphore_wait(barrier, GROUPS - 1 + len(AROUND))

    mine = pl.ds(pl.multiple_of(group * 8, 8), 8)
    mine_too = pl.ds(pl.multiple_of(64 + group * 8, 8), 8)
    copies = []
    for o in range(1, GROUPS):
        to = lax.rem(group + o, GROUPS)
        cp = pltpu.make_async_remote_copy(
            src_ref=stage.at[:, pl.ds(pl.multiple_of(to * width, LANES), width)],
            dst_ref=modes.at[mine, :],
            send_sem=send1.at[o],
            recv_sem=recv1.at[o],
            device_id={"bead": to},
            device_id_type=MESH,
        )
        cp.start()
        copies.append(cp)
    heavy_copies = []
    for g, (a, c) in enumerate(AROUND):
        at = ATOMS + g * LANES
        cp = pltpu.make_async_remote_copy(
            src_ref=lent_heavy,
            dst_ref=tab.at[3, :, at : at + LANES],
            send_sem=send4.at[g],
            recv_sem=recv4.at[g],
            device_id=brick_at(1 - a, 1 - c),
            device_id_type=MESH,
        )
        cp.start()
        heavy_copies.append(cp)
    modes[mine, :] = stage[:, pl.ds(pl.multiple_of(group * width, LANES), width)]

    for cp in loading[4:]:
        cp.wait()
    for half in range(2):
        for d in range(CHUNKS):
            lanes = slice(d * LANES, (d + 1) * LANES)
            rows = idx_ref[half * 8 : half * 8 + 8, lanes]
            local = lane_take(ghost_rows, rows & (LANES - 1))
            rows = jnp.where(
                rows < SELF, rows, jnp.where(rows < SELF + LANES, local, rows - LANES)
            )
            idx16[half * 8 : half * 8 + 8, lanes] = rows
    for k in range(SLOTS):
        rows_all[k] = jnp.broadcast_to(idx16[k : k + 1, :], (8, ATOMS))
        block_ids[k] = jnp.broadcast_to(
            (idx16[k : k + 1, :] >> 8).astype(F32), (BAND, ATOMS)
        ).astype(BF16)
    for kp in range(SLOTS // 2):
        pairs[kp] = jnp.where(low_all, rows_all[2 * kp], rows_all[2 * kp + 1])
    within = sublanes((WIDE, ATOMS)).astype(F32).astype(BF16)
    for k in range(SLOTS):
        wide = jnp.broadcast_to((idx16[k : k + 1, :] & (WIDE - 1)).astype(F32), (BAND, ATOMS))
        wide = jnp.concatenate([wide.astype(BF16)] * (WIDE // BAND), 0)
        onehot[:, k * ATOMS : (k + 1) * ATOMS] = jnp.where(within == wide, 1.0, 0.0).astype(BF16)
    load_weights(w1_ref, w2_ref, w3_ref, wide1, wide2, wide3)
    load_weights(v1_ref, v2_ref, v3_ref, last1, last2, last3)
    my_types = types_ref[:, pl.ds(pl.multiple_of(group * LANES, LANES), LANES)]
    mass = jnp.broadcast_to(jnp.where(my_types == 0, HEAVY_MASS, 1.0), (8, LANES))
    factor = jnp.concatenate([jnp.where(low, 1.0 / mass, mass)] * 3, 1)
    ghost_mass = jnp.where(ghost_heavy > 0.0, HEAVY_MASS, 1.0)
    ghost_factor = jnp.concatenate([1.0 / ghost_mass] * 3, 1)

    for cp in copies:
        cp.wait()
    ghost_matrix = jnp.concatenate([matrix_ref[mine, :], matrix_ref[mine_too, :]], 0)
    both = jnp.dot(
        ghost_matrix, modes[:, own_width:width], precision=HIGHEST, preferred_element_type=F32
    )
    ghost_pos = both[0:8] + both[8:16] * ghost_factor
    for c in range(3):
        lent_pos[c] = fold(ghost_pos[:, c * LANES : (c + 1) * LANES], low)
    pos_copies = []
    for g, (a, c) in enumerate(AROUND):
        at = ATOMS + g * LANES
        cp = pltpu.make_async_remote_copy(
            src_ref=lent_pos,
            dst_ref=tab.at[0:3, :, at : at + LANES],
            send_sem=send3.at[g],
            recv_sem=recv3.at[g],
            device_id=brick_at(1 - a, 1 - c),
            device_id_type=MESH,
        )
        cp.start()
        pos_copies.append(cp)
    both = jnp.dot(
        matrix_ref[...], modes[:, 0:own_width], precision=HIGHEST, preferred_element_type=F32
    )
    for g in range(GROUPS):
        rows = slice(g * 8, g * 8 + 8)
        moved[rows, :] = both[rows] + both[64 + g * 8 : 72 + g * 8] * factor
    my_lanes = pl.ds(pl.multiple_of(group * own_width, LANES), own_width)
    copies = []
    for o in range(1, GROUPS):
        to = lax.rem(group + o, GROUPS)
        cp = pltpu.make_async_remote_copy(
            src_ref=moved.at[pl.ds(pl.multiple_of(to * 8, 8), 8), :],
            dst_ref=back.at[:, my_lanes],
            send_sem=send2.at[o],
            recv_sem=recv2.at[o],
            device_id={"bead": to},
            device_id_type=MESH,
        )
        cp.start()
        copies.append(cp)
    back[:, my_lanes] = moved[mine, :]

    for d in range(CHUNKS):
        rows = sublanes((LANES, LANES)) + d * LANES
        hit = rows == jnp.broadcast_to(ghost_ref[...], (LANES, LANES))
        hit = jnp.where(hit, 1.0, 0.0).astype(BF16)
        ghost_onehot[:, d * LANES : (d + 1) * LANES] = jnp.transpose(hit)
    for cp in heavy_copies:
        cp.wait()
    for half in range(2):
        for d in range(CHUNKS):
            lanes = slice(d * LANES, (d + 1) * LANES)
            rows = idx16[half * 8 : half * 8 + 8, lanes]
            lane = rows & (LANES - 1)
            heavy16[half * 8 : half * 8 + 8, lanes] = pick(
                [
                    lane_take(tab[3, :, t * LANES : (t + 1) * LANES], lane)
                    for t in range(TABLE // LANES)
                ],
                row_bits(rows, 4),
            )
    for kp in range(SLOTS // 2):
        heavy_pairs[kp] = jnp.where(
            low_all,
            jnp.broadcast_to(heavy16[2 * kp : 2 * kp + 1, :], (8, ATOMS)),
            jnp.broadcast_to(heavy16[2 * kp + 1 : 2 * kp + 2, :], (8, ATOMS)),
        )
    for k in range(SLOTS):
        onehot_t[k * ATOMS : (k + 1) * ATOMS, :] = jnp.transpose(
            onehot[:, k * ATOMS : (k + 1) * ATOMS]
        )

    for cp in copies:
        cp.wait()
    for c in range(3):
        for d in range(CHUNKS):
            at = d * own_width + c * LANES
            v = back[:, at : at + LANES]
            newpos_ref[c, :, d * LANES : (d + 1) * LANES] = v[0:PER]
            newmom_ref[c, :, d * LANES : (d + 1) * LANES] = v[PER:8]
            tab[c, :, d * LANES : (d + 1) * LANES] = fold(v, low)
    storing = [
        pltpu.make_async_copy(newpos_ref, newpos_hbm, stores.at[0]),
        pltpu.make_async_copy(newmom_ref, newmom_hbm, stores.at[1]),
    ]
    for cp in storing:
        cp.start()
    for cp in pos_copies:
        cp.wait()

    slot_off = jnp.where(low, 0, 1)
    cos_scale = (math.pi / (2.0 * CUTOFF)) ** 2
    cos_terms = [(-1.0) ** n * cos_scale**n / math.factorial(2 * n) for n in range(8)]

    def geometry(ci, carry):
        lanes = pl.ds(pl.multiple_of(ci * LANES, LANES), LANES)
        own = [tab[c, :, lanes] for c in range(3)]
        count = jnp.broadcast_to(counts_ref[:, lanes], (8, LANES))
        for kp in range(SLOTS // 2):
            rows = pairs[kp, :, lanes]
            lane = rows & (LANES - 1)
            bits = row_bits(rows, 4)
            dist_sq = jnp.zeros((8, LANES), F32)
            for c in range(3):
                near = pick(
                    [
                        lane_take(tab[c, :, t * LANES : (t + 1) * LANES], lane)
                        for t in range(TABLE // LANES)
                    ],
                    bits,
                )
                dist_sq = dist_sq + (near - own[c]) ** 2
            close = jnp.minimum(dist_sq, CUTOFF * CUTOFF)
            wave = jnp.full_like(close, cos_terms[-1])
            for term in cos_terms[-2::-1]:
                wave = wave * close + term
            used = ((2 * kp + slot_off) < count) & (dist_sq < CUTOFF * CUTOFF)
            smooth = jnp.where(used, wave * wave, 0.0)
            heavy_w = smooth * heavy_pairs[kp, :, lanes]
            dist[kp, :, lanes] = dist_sq
            weight_h[kp, :, lanes] = heavy_w
            weight_l[kp, :, lanes] = smooth - heavy_w
            coupling = smooth * lax.rsqrt(1.0 + dist_sq)
            turned = pltpu.roll(coupling, PER, 0)
            for k, v in ((2 * kp, jnp.where(low, coupling, turned)), (2 * kp + 1, jnp.where(low, turned, coupling))):
                coup[k, :, lanes] = v
        return carry

    lax.fori_loop(0, CHUNKS, geometry, 0)

    def scatter(terms_of, beside=None):
        acc = jnp.zeros((BLOCKS * BAND, WIDE), F32)
        for g in range(SLOTS // GROUP):
            if beside is not None:
                beside(g)
            tall = []
            for k in range(g * GROUP, (g + 1) * GROUP):
                terms = split(terms_of(k))
                zero = jnp.zeros_like(terms)
                ids = block_ids[k]
                tall.append(
                    jnp.concatenate([jnp.where(ids == b, terms, zero) for b in range(BLOCKS)], 0)
                )
            rows = slice(g * GROUP * ATOMS, (g + 1) * GROUP * ATOMS)
            acc = acc + jnp.dot(
                jnp.concatenate(tall, 1), onehot_t[rows, :], preferred_element_type=F32
            )
        return acc

    def chunk_of(acc, n):
        row, col = (n // 2) * BAND, (n % 2) * LANES
        return acc[row : row + 8, col : col + LANES] + acc[row + 8 : row + 16, col : col + LANES]

    def send_back(acc, par):
        out = []
        for g, (a, c) in enumerate(AROUND):
            spread[par, g] = chunk_of(acc, CHUNKS + g)
        for g, (a, c) in enumerate(AROUND):
            cp = pltpu.make_async_remote_copy(
                src_ref=spread.at[par, g],
                dst_ref=backin.at[par, g],
                send_sem=send_b.at[par, g],
                recv_sem=recv_b.at[par, g],
                device_id=brick_at(a - 1, c - 1),
                device_id_type=MESH,
            )
            cp.start()
            out.append(cp)
        return out

    def own_part(acc):
        return jnp.concatenate([chunk_of(acc, d) for d in range(CHUNKS)], 1)

    def take_back(copies, par):
        for cp in copies:
            cp.wait()
        received = backin[par, 0]
        for g in range(1, len(AROUND)):
            received = received + backin[par, g]
        returned = lax.dot_general(
            split(received), ghost_onehot[...], (((1,), (0,)), ((), ())), preferred_element_type=F32
        )
        return returned[0:8] + returned[8:16]

    def blocks_of(pieces):
        return jnp.concatenate([split(v) for v in pieces], 0)

    def by_product(tall, g, inside, acc):
        cols = slice(g * GROUP * ATOMS, (g + 1) * GROUP * ATOMS)
        found = jnp.dot(tall, onehot[:, cols], preferred_element_type=F32)
        for kk in range(GROUP):
            k = g * GROUP + kk
            f = found[:, kk * ATOMS : (kk + 1) * ATOMS]
            near = [
                f[q * BAND : q * BAND + 8] + f[q * BAND + 8 : q * BAND + 16]
                for q in range(OWN_BLOCKS)
            ]
            rows = rows_all[k]
            near = pick(near, [(rows & WIDE) != 0, (rows & (2 * WIDE)) != 0])
            hit = (rows < ATOMS) if inside else (rows >= ATOMS)
            acc = acc + jnp.where(hit, coup[k], 0.0) * near
        return acc

    def by_lookup(chunks, g, acc):
        out = []
        for d in range(CHUNKS):
            lanes = slice(d * LANES, (d + 1) * LANES)
            v = acc[:, lanes]
            for k in range(g * GROUP, (g + 1) * GROUP):
                rows = rows_all[k, :, lanes]
                lane = rows & (LANES - 1)
                near = pick([lane_take(t, lane) for t in chunks], row_bits(rows, 3))
                v = v + jnp.where(rows >= ATOMS, coup[k, :, lanes], 0.0) * near
            out.append(v)
        return jnp.concatenate(out, 1)

    def forward_own(v, acc):
        tall = blocks_of([v[:, q * WIDE : (q + 1) * WIDE] for q in range(OWN_BLOCKS)])
        for g in range(SLOTS // GROUP):
            acc = by_product(tall, g, True, acc)
        return acc

    def forward_ghosts(par, acc):
        chunks = [ghost_in[par, t] for t in range(len(AROUND))]
        tall = blocks_of(
            [jnp.concatenate(chunks[2 * q : 2 * q + 2], 1) for q in range(OWN_BLOCKS)]
        )
        half = SLOTS // GROUP // 2
        for g in range(half):
            acc = by_product(tall, g, False, acc)
            acc = by_lookup(chunks, half + g, acc)
        return acc

    feat_ref[...] = jnp.zeros_like(feat_ref)

    def radial(ci):
        lanes = slice(ci * LANES, (ci + 1) * LANES)
        sums = [jnp.zeros((8, LANES), F32) for _ in range(FEATS)]
        for kp in range(SLOTS // 2):
            d = dist[kp, :, lanes]
            wh = weight_h[kp, :, lanes]
            wl = weight_l[kp, :, lanes]
            for s in range(HALF):
                rate = -0.2 * 20.0 ** (s / (HALF - 1)) * math.log2(math.e)
                falloff = jnp.exp2(d * rate)
                sums[s] = sums[s] + wh * falloff
                sums[HALF + s] = sums[HALF + s] + wl * falloff
        for s in range(FEATS):
            v = jnp.log(1.0 + (sums[s] + pltpu.roll(sums[s], PER, 0)))
            feat_ref[ci, s * PER : (s + 1) * PER, :] = v[0:PER]

    def radial_pair(g):
        radial(2 * g)
        radial(2 * g + 1)

    acc = scatter(lambda k: coup[k], radial_pair)
    first_back = send_back(acc, 2)
    around = own_part(acc)
    for k in range(SLOTS):
        around = around + coup[k]
    degree[...] = around

    hidden = product(wide1[...], features_of(feat_ref))
    for b, chi in enumerate(network(hidden, wide2, wide3, heavy_row)):
        residual[b : b + 1, :] = -CHI_SCALE * chi
    residual[PER:8, :] = jnp.broadcast_to(1.0 - heavy, (PER, ATOMS))
    h0, h1 = hardness_ref[0], hardness_ref[1]
    hard = jnp.where(heavy_row, h0, h1)

    lane_id = lax.broadcasted_iota(jnp.int32, (8, LANES), 1)

    def dots_of(r):
        dots = [lanes_sum(r * r), lanes_sum(r * image[...]), lanes_sum(r * steps[...]), lanes_sum(r)]
        v = dots[3]
        for n in (2, 1, 0):
            v = jnp.where(lane_id == n, dots[n], v)
        return v

    def send_lent(ref, par):
        lent[par] = at_ghosts(ref[...])
        out = []
        for g, (a, c) in enumerate(AROUND):
            cp = pltpu.make_async_remote_copy(
                src_ref=lent.at[par],
                dst_ref=ghost_in.at[par, g],
                send_sem=send_a.at[par, g],
                recv_sem=recv_a.at[par, g],
                device_id=brick_at(1 - a, 1 - c),
                device_id_type=MESH,
            )
            cp.start()
            out.append(cp)
        return out

    def send_dots(par, targets):
        out = []
        for dx, dy in targets:
            n = dx * SIDE + dy
            cp = pltpu.make_async_remote_copy(
                src_ref=parts.at[par, me],
                dst_ref=parts.at[par, me],
                send_sem=send_d.at[par, n],
                recv_sem=recv_d.at[par, n],
                device_id=brick_at(dx, dy),
                device_id_type=MESH,
            )
            cp.start()
            out.append(cp)
        return out

    def take_dots(copies, par):
        for cp in copies:
            cp.wait()
        whole = parts[par, 0]
        for n in range(1, BRICKS):
            whole = whole + parts[par, n]
        return [whole[:, n : n + 1] for n in range(4)]

    alpha_max = 2.0 / jnp.minimum(h0, h1)

    def step_sizes(dots, state, start):
        norm, rw, rs, r_sum = dots
        norm_prev, curve_prev, sum_prev, sum_total = state
        beta = jnp.where(start, 0.0, norm / jnp.maximum(norm_prev, TINY))
        curve = rw + 2.0 * beta * rs + beta * beta * curve_prev
        alpha = jnp.minimum(norm / jnp.maximum(curve, TINY), alpha_max)
        p_sum = r_sum + beta * sum_prev
        return alpha, beta, (norm, curve, p_sum, sum_total + alpha * p_sum)

    copies = send_lent(residual, 0)
    acc = scatter(lambda k: coup[k] * residual[...])
    second = send_back(acc, 0)
    around = forward_own(residual[...], own_part(acc))
    deg = hard + 0.5 * (degree[...] + take_back(first_back, 2))
    degree[...] = deg
    for cp in copies:
        cp.wait()
    around = forward_ghosts(0, around)
    image[...] = deg * residual[...] - 0.5 * (around + take_back(second, 0))
    for ref in (direction, steps, image2, total):
        ref[...] = jnp.zeros_like(ref)
    high = jnp.logical_not(low_all)
    high_col = sublanes((8, 1)) >= PER

    def sweep(it, state):
        par = lax.rem(it + 1, 2)
        start = it == 0
        r, w = residual[...], image[...]
        first = send_lent(image, par)
        parts[par, me] = dots_of(r)
        third = send_dots(par, others)
        acc = scatter(lambda k: coup[k] * image[...])
        second = send_back(acc, par)
        around = forward_own(w, own_part(acc))
        for cp in first:
            cp.wait()
        around = forward_ghosts(par, around)
        dots = take_dots(third, par)
        light = dots[3]
        alpha, beta, state = step_sizes(dots, state, start)
        q = degree[...] * w - 0.5 * (around + take_back(second, par))
        z = q + beta * image2[...]
        s = w + beta * steps[...]
        p = r + beta * direction[...]
        x = total[...] + alpha * p
        r_new = r - alpha * s
        w_new = w - alpha * z
        known = jnp.logical_and(start, high)
        gap = h1 - h0
        hard_sum = (TOTAL_ATOMS - light) * h0 + light * h1
        c0 = light / hard_sum
        c1 = -TOTAL_ATOMS / hard_sum
        direction[...] = jnp.where(known, 1.0, p)
        steps[...] = jnp.where(known, hard, s)
        image2[...] = jnp.where(known, h0 * hard + gap * w, z)
        total[...] = jnp.where(known, TOTAL_ATOMS / hard_sum, x)
        residual[...] = jnp.where(known, gap * (c0 + c1 * r), r_new)
        image[...] = jnp.where(known, gap * (c0 * hard + c1 * w), w_new)
        exact = (
            jnp.full((8, 1), TOTAL_ATOMS, F32),
            hard_sum,
            jnp.full((8, 1), TOTAL_ATOMS, F32),
            TOTAL_ATOMS / hard_sum * TOTAL_ATOMS,
        )
        known_col = jnp.logical_and(start, high_col)
        return tuple(jnp.where(known_col, e, v) for e, v in zip(exact, state))

    zero = jnp.zeros((8, 1), F32)
    state = lax.fori_loop(0, ITERS - 1, sweep, (zero + 1.0, zero, zero, zero))
    par = ITERS % 2
    parts[par, me] = dots_of(residual[...])
    third = send_dots(par, others)
    first_layer[...] = product(last1[...], features_of(feat_ref))
    dots = take_dots(third, par)
    alpha, beta, state = step_sizes(dots, state, False)
    x = total[...] + alpha * (residual[...] + beta * direction[...])
    sums = state[3]
    charges = x[0:PER] - (sums[0:PER] / sums[PER:8]) * x[PER:8]
    charge_ref[...] = charges
    storing.append(pltpu.make_async_copy(charge_ref, charge_hbm, stores.at[2]))
    storing[2].start()
    column = last1[:, FEATS : FEATS + 1]
    hidden = jnp.concatenate(
        [
            first_layer[:, b * ATOMS : (b + 1) * ATOMS] + column * charges[b : b + 1]
            for b in range(PER)
        ],
        1,
    )
    for b, e in enumerate(network(hidden, last2, last3, heavy_row)):
        energy_ref[b : b + 1, :] = e
    storing.append(pltpu.make_async_copy(energy_ref, energy_hbm, stores.at[3]))
    storing[3].start()
    for cp in storing:
        cp.wait()


def outputs_kernel(a_ref, b_ref, c_ref, d_ref, a_out, b_out, c_out, d_out):
    for src, dst in ((a_ref, a_out), (b_ref, b_out), (c_ref, c_out), (d_ref, d_out)):
        dst[...] = src[...]


def vmem(count):
    return [pl.BlockSpec(memory_space=pltpu.VMEM)] * count


def anywhere(count):
    return [pl.BlockSpec(memory_space=pl.ANY)] * count


def sds(*shape, dtype=F32):
    return jax.ShapeDtypeStruct(shape, dtype)


def f32(*shape):
    return pltpu.VMEM(shape, F32)


def on_device(
    positions,
    momenta,
    types,
    ghost_rows,
    neighbours,
    counts,
    hardness,
    chi_w1,
    chi_w2,
    chi_w3,
    en_w1,
    en_w2,
    en_w3,
):
    turn = lambda v: jnp.transpose(v, (1, 0, 2))
    dma = pltpu.SemaphoreType.DMA
    networks = [f32(2 * PAD, PAD), f32(2 * PAD, 2 * PAD), f32(8, 2 * PAD)]
    operands = (
        hardness,
        jnp.asarray(propagator()),
        turn(positions),
        turn(momenta),
        types.reshape(1, ATOMS),
        ghost_rows.reshape(1, LANES),
        neighbours,
        counts.reshape(1, ATOMS),
        turn(chi_w1),
        turn(chi_w2),
        chi_w3,
        turn(en_w1),
        turn(en_w2),
        en_w3,
    )
    outputs = (sds(3, PER, ATOMS), sds(3, PER, ATOMS), sds(PER, ATOMS), sds(PER, ATOMS))
    results = pl.pallas_call(
        main_kernel,
        name="main",
        out_shape=outputs,
        in_specs=anywhere(len(operands)),
        out_specs=tuple(anywhere(len(outputs))),
        scratch_shapes=[
            pltpu.SMEM(hardness.shape, F32),
            *[pltpu.VMEM(v.shape, v.dtype) for v in operands[1:]],
            *[f32(*v.shape) for v in outputs],
            f32(CHUNKS, LANES, LANES),
            f32(8, 6 * ATOMS),
            f32(64, 6 * LANES),
            f32(64, 3 * LANES),
            f32(8, 3 * ATOMS),
            f32(3, 8, LANES),
            f32(8, LANES),
            f32(4, 8, TABLE),
            pltpu.VMEM((SLOTS, ATOMS), jnp.int32),
            f32(SLOTS, ATOMS),
            pltpu.VMEM((SLOTS, 8, ATOMS), jnp.int32),
            pltpu.VMEM((SLOTS // 2, 8, ATOMS), jnp.int32),
            f32(SLOTS // 2, 8, ATOMS),
            pltpu.VMEM((SLOTS, BAND, ATOMS), BF16),
            pltpu.VMEM((WIDE, EDGES), BF16),
            pltpu.VMEM((EDGES, WIDE), BF16),
            pltpu.VMEM((LANES, ATOMS), BF16),
            f32(SLOTS, 8, ATOMS),
            f32(SLOTS // 2, 8, ATOMS),
            f32(SLOTS // 2, 8, ATOMS),
            f32(SLOTS // 2, 8, ATOMS),
            *networks,
            *networks,
            f32(2 * PAD, PER * ATOMS),
            *[f32(8, ATOMS) for _ in range(7)],
            f32(3, 8, 8, LANES),
            f32(2, 8, LANES),
            f32(2, 8, 8, LANES),
            f32(3, 8, 8, LANES),
            f32(2, BRICKS, 8, LANES),
            *[dma((GROUPS,)) for _ in range(4)],
            *[dma((8,)) for _ in range(4)],
            *[dma((2, 8)) for _ in range(2)],
            *[dma((3, 8)) for _ in range(2)],
            *[dma((2, BRICKS)) for _ in range(2)],
            dma((len(operands),)),
            dma((len(outputs),)),
        ],
        compiler_params=pltpu.CompilerParams(
            vmem_limit_bytes=VMEM_LIMIT, collective_id=0, has_side_effects=True
        ),
    )(*operands)
    new_pos, new_mom, charges, energies = pl.pallas_call(
        outputs_kernel,
        name="outputs",
        out_shape=outputs,
        in_specs=vmem(len(outputs)),
        out_specs=tuple(vmem(len(outputs))),
    )(*results)
    return (turn(new_pos), turn(new_mom), charges, energies)


def solution(mesh):
    placed = (
        P("bead", None, ("gx", "gy")),
        P("bead", None, ("gx", "gy")),
        P(("gx", "gy")),
        P(("gx", "gy")),
        P(None, ("gx", "gy")),
        P(("gx", "gy")),
        P(),
        P(),
        P(),
        P(),
        P(),
        P(),
        P(),
    )
    return jax.shard_map(
        on_device,
        mesh=mesh,
        in_specs=placed,
        out_specs=(
            P("bead", None, ("gx", "gy")),
            P("bead", None, ("gx", "gy")),
            P("bead", ("gx", "gy")),
            P("bead", ("gx", "gy")),
        ),
        check_vma=False,
    )
```

```python
import functools
import math

import jax
import jax.numpy as jnp
import numpy as np
from jax import lax
from jax.experimental import pallas as pl
from jax.experimental.pallas import tpu as pltpu
from jax.sharding import PartitionSpec as P

MESH = pl.DeviceIdType.MESH
F32 = jnp.float32
BF16 = jnp.bfloat16
HIGHEST = lax.Precision.HIGHEST
ITERS = 5
STEP = 0.5
TOP_FREQ = 80.0
CUTOFF = 4.0
HEAVY_MASS = 16.0
CHI_SCALE = 4.0
LANES = 128
BEADS = 32
GROUPS = 8
PER = 4
ATOMS = 1024
CHUNKS = ATOMS // LANES
SLOTS = 16
TABLE = ATOMS + 8 * LANES
HALF = 15
FEATS = 2 * HALF
SIDE = 4
PAD = 32
BRICKS = SIDE * SIDE
BAND = 16
WIDE = 256
BLOCKS = TABLE // WIDE
OWN_BLOCKS = ATOMS // WIDE
EDGES = SLOTS * ATOMS
GROUP = 4
TOTAL_ATOMS = ATOMS * BRICKS
TINY = 1e-30
SELF = ATOMS + 4 * LANES
VMEM_LIMIT = 60 * 1024 * 1024


def propagator():
    k = np.arange(BEADS)
    omega = TOP_FREQ * np.sin(math.pi * k / BEADS)
    cosine = np.cos(omega * STEP)
    sine = np.sin(omega * STEP)
    drift = np.where(k > 0, TOP_FREQ * sine / np.where(k > 0, omega, 1.0), TOP_FREQ * STEP)
    restoring = -(omega / TOP_FREQ) * sine
    gap = (k[:, None] - k[None, :]) % BEADS

    def spread(weights):
        line = (weights[None, :] * np.cos(2 * math.pi * k[:, None] * k[None, :] / BEADS)).sum(1) / BEADS
        return line[gap]

    keep, push, pull = spread(cosine), spread(drift), spread(restoring)
    zero = np.zeros_like(keep)
    plain = np.block([[keep, zero], [zero, keep]])
    massive = np.block([[zero, push], [pull, zero]])
    order = np.array([half * BEADS + g * PER + b for g in range(GROUPS) for half in range(2) for b in range(PER)])
    both = np.concatenate([plain[order][:, order], massive[order][:, order]], 0)
    return both.astype(np.float32)


def sublanes(shape):
    return lax.broadcasted_iota(jnp.int32, shape, 0)


def lane_take(table, lane):
    return jnp.take_along_axis(table, lane, axis=1, mode="promise_in_bounds")


def row_bits(rows, count):
    return [(rows & (LANES << bit)) != 0 for bit in range(count)]


def pick(parts, bits):
    level = 0
    while len(parts) > 1:
        nxt = [
            jnp.where(bits[level], parts[i + 1], parts[i]) for i in range(0, len(parts) - 1, 2)
        ]
        if len(parts) % 2:
            nxt.append(parts[-1])
        parts = nxt
        level += 1
    return parts[0]


def split(v):
    top = v.astype(BF16).astype(F32)
    return jnp.concatenate([top, v - top], 0).astype(BF16)


def halves(v):
    top = v.astype(BF16)
    return top, (v - top.astype(F32)).astype(BF16)


def lanes_sum(v):
    return jnp.sum(v, axis=1, keepdims=True)


def fold(v, low):
    return jnp.where(low, v, pltpu.roll(v, PER, 0))


def brick_at(dx, dy):
    return {
        "gx": lax.rem(lax.axis_index("gx") + dx + SIDE, SIDE),
        "gy": lax.rem(lax.axis_index("gy") + dy + SIDE, SIDE),
    }


AROUND = [(a, c) for a in range(3) for c in range(3) if (a, c) != (1, 1)]


def load_weights(w1_ref, w2_ref, w3_ref, wide1, wide2, wide3):
    rows, cols = w1_ref.shape[0], w1_ref.shape[2]
    for ref in (wide1, wide2, wide3):
        ref[...] = jnp.zeros_like(ref)
    for e in range(2):
        at = e * PAD
        wide1[at : at + rows, 0:cols] = w1_ref[:, e, :]
        wide2[at : at + rows, at : at + rows] = w2_ref[:, e, :]
        wide3[e : e + 1, at : at + rows] = w3_ref[e : e + 1, :]


def product(w, f):
    w_top, w_rest = halves(w)
    f_top, f_rest = halves(f)
    rows = w.shape[0]
    both = jnp.dot(jnp.concatenate([w_top, w_rest], 0), f_top, preferred_element_type=F32)
    return both[0:rows] + both[rows:] + jnp.dot(w_top, f_rest, preferred_element_type=F32)


def features_of(feat_ref):
    return jnp.concatenate(
        [feat_ref[d, pl.ds(b, PAD, stride=PER), :] for b in range(PER) for d in range(CHUNKS)], 1
    )


def network(hidden, wide2, wide3, heavy):
    out = product(wide3[...], jnp.tanh(product(wide2[...], jnp.tanh(hidden))))
    return [
        jnp.where(
            heavy, out[0:1, b * ATOMS : (b + 1) * ATOMS], out[1:2, b * ATOMS : (b + 1) * ATOMS]
        )
        for b in range(PER)
    ]


def main_kernel(
    hardness_hbm,
    matrix_hbm,
    pos_hbm,
    mom_hbm,
    types_hbm,
    ghost_hbm,
    idx_hbm,
    counts_hbm,
    w1_hbm,
    w2_hbm,
    w3_hbm,
    v1_hbm,
    v2_hbm,
    v3_hbm,
    newpos_hbm,
    newmom_hbm,
    charge_hbm,
    energy_hbm,
    hardness_ref,
    matrix_ref,
    pos_ref,
    mom_ref,
    types_ref,
    ghost_ref,
    idx_ref,
    counts_ref,
    w1_ref,
    w2_ref,
    w3_ref,
    v1_ref,
    v2_ref,
    v3_ref,
    newpos_ref,
    newmom_ref,
    charge_ref,
    energy_ref,
    feat_ref,
    stage,
    modes,
    moved,
    back,
    lent_pos,
    lent_heavy,
    tab,
    idx16,
    heavy16,
    rows_all,
    pairs,
    heavy_pairs,
    block_ids,
    onehot,
    onehot_t,
    ghost_onehot,
    coup,
    dist,
    weight_h,
    weight_l,
    wide1,
    wide2,
    wide3,
    last1,
    last2,
    last3,
    first_layer,
    residual,
    image,
    image2,
    direction,
    steps,
    total,
    degree,
    spread,
    lent,
    ghost_in,
    backin,
    parts,
    send1,
    recv1,
    send2,
    recv2,
    send3,
    recv3,
    send4,
    recv4,
    send_a,
    recv_a,
    send_b,
    recv_b,
    send_d,
    recv_d,
    loads,
    stores,
):
    group = lax.axis_index("bead")
    me = lax.axis_index("gx") * SIDE + lax.axis_index("gy")
    others = [(o // SIDE, o % SIDE) for o in range(1, BRICKS)]
    parts[...] = jnp.zeros_like(parts)
    barrier = pltpu.get_barrier_semaphore()
    for o in range(1, GROUPS):
        pl.semaphore_signal(
            barrier, inc=1, device_id={"bead": lax.rem(group + o, GROUPS)}, device_id_type=MESH
        )
    for a, c in AROUND:
        pl.semaphore_signal(barrier, inc=1, device_id=brick_at(a - 1, c - 1), device_id_type=MESH)
    loading = [
        pltpu.make_async_copy(src, dst, loads.at[n])
        for n, (src, dst) in enumerate(
            (
                (pos_hbm, pos_ref),
                (mom_hbm, mom_ref),
                (ghost_hbm, ghost_ref),
                (types_hbm, types_ref),
                (idx_hbm, idx_ref),
                (matrix_hbm, matrix_ref),
                (counts_hbm, counts_ref),
                (hardness_hbm, hardness_ref),
                (w1_hbm, w1_ref),
                (w2_hbm, w2_ref),
                (w3_hbm, w3_ref),
                (v1_hbm, v1_ref),
                (v2_hbm, v2_ref),
                (v3_hbm, v3_ref),
            )
        )
    ]
    for cp in loading:
        cp.start()
    for cp in loading[0:4]:
        cp.wait()

    low = sublanes((8, LANES)) < PER
    low_all = sublanes((8, ATOMS)) < PER
    own_width = 3 * LANES
    width = 2 * own_width
    ghost_rows = jnp.broadcast_to(ghost_ref[...], (8, LANES))
    ghost_lane = ghost_rows & (LANES - 1)
    ghost_bits = row_bits(ghost_rows, 3)

    def at_ghosts(v):
        return pick(
            [lane_take(v[:, d * LANES : (d + 1) * LANES], ghost_lane) for d in range(CHUNKS)],
            ghost_bits,
        )

    heavy_row = types_ref[...] == 0
    heavy = jnp.where(heavy_row, 1.0, 0.0)
    tab[3, :, 0:ATOMS] = jnp.broadcast_to(heavy, (8, ATOMS))
    ghost_heavy = at_ghosts(jnp.broadcast_to(heavy, (8, ATOMS)))
    lent_heavy[...] = ghost_heavy
    for c in range(3):
        v = jnp.concatenate([pos_ref[c], mom_ref[c]], 0)
        g = at_ghosts(v)
        for d in range(CHUNKS):
            at = d * width + c * LANES
            stage[:, at : at + LANES] = v[:, d * LANES : (d + 1) * LANES]
            stage[:, at + own_width : at + own_width + LANES] = g
    pl.semaphore_wait(barrier, GROUPS - 1 + len(AROUND))

    mine = pl.ds(pl.multiple_of(group * 8, 8), 8)
    mine_too = pl.ds(pl.multiple_of(64 + group * 8, 8), 8)
    copies = []
    for o in range(1, GROUPS):
        to = lax.rem(group + o, GROUPS)
        cp = pltpu.make_async_remote_copy(
            src_ref=stage.at[:, pl.ds(pl.multiple_of(to * width, LANES), width)],
            dst_ref=modes.at[mine, :],
            send_sem=send1.at[o],
            recv_sem=recv1.at[o],
            device_id={"bead": to},
            device_id_type=MESH,
        )
        cp.start()
        copies.append(cp)
    heavy_copies = []
    for g, (a, c) in enumerate(AROUND):
        at = ATOMS + g * LANES
        cp = pltpu.make_async_remote_copy(
            src_ref=lent_heavy,
            dst_ref=tab.at[3, :, at : at + LANES],
            send_sem=send4.at[g],
            recv_sem=recv4.at[g],
            device_id=brick_at(1 - a, 1 - c),
            device_id_type=MESH,
        )
        cp.start()
        heavy_copies.append(cp)
    modes[mine, :] = stage[:, pl.ds(pl.multiple_of(group * width, LANES), width)]

    for cp in loading[4:]:
        cp.wait()
    def renumber(d, carry):
        lanes = pl.ds(pl.multiple_of(d * LANES, LANES), LANES)
        for half in range(2):
            rows = idx_ref[half * 8 : half * 8 + 8, lanes]
            local = lane_take(ghost_rows, rows & (LANES - 1))
            rows = jnp.where(
                rows < SELF, rows, jnp.where(rows < SELF + LANES, local, rows - LANES)
            )
            idx16[half * 8 : half * 8 + 8, lanes] = rows
        return carry

    lax.fori_loop(0, CHUNKS, renumber, 0)
    for k in range(SLOTS):
        rows_all[k] = jnp.broadcast_to(idx16[k : k + 1, :], (8, ATOMS))
    within = sublanes((WIDE, ATOMS)).astype(F32).astype(BF16)

    def build(k, carry):
        rows = rows_all[k]
        ids = (rows >> 8).astype(F32)
        block_ids[k] = jnp.concatenate([ids, ids], 0).astype(BF16)
        wide = (rows & (WIDE - 1)).astype(F32)
        wide = jnp.concatenate([wide, wide], 0).astype(BF16)
        wide = jnp.concatenate([wide] * (WIDE // BAND), 0)
        edges = pl.ds(pl.multiple_of(k * ATOMS, ATOMS), ATOMS)
        hits = jnp.where(within == wide, 1.0, 0.0).astype(BF16)
        onehot[:, edges] = hits
        onehot_t[edges, :] = jnp.transpose(hits)
        return carry

    lax.fori_loop(0, SLOTS, build, 0)
    for ref in (coup, dist, weight_h, weight_l, feat_ref):
        ref[...] = jnp.zeros_like(ref)

    def pair_up(kp, carry):
        pairs[kp] = jnp.where(low_all, rows_all[2 * kp], rows_all[2 * kp + 1])
        return carry

    lax.fori_loop(0, SLOTS // 2, pair_up, 0)
    load_weights(w1_ref, w2_ref, w3_ref, wide1, wide2, wide3)
    load_weights(v1_ref, v2_ref, v3_ref, last1, last2, last3)
    my_types = types_ref[:, pl.ds(pl.multiple_of(group * LANES, LANES), LANES)]
    mass = jnp.broadcast_to(jnp.where(my_types == 0, HEAVY_MASS, 1.0), (8, LANES))
    factor = jnp.concatenate([jnp.where(low, 1.0 / mass, mass)] * 3, 1)
    ghost_mass = jnp.where(ghost_heavy > 0.0, HEAVY_MASS, 1.0)
    ghost_factor = jnp.concatenate([1.0 / ghost_mass] * 3, 1)

    for cp in copies:
        cp.wait()
    ghost_matrix = jnp.concatenate([matrix_ref[mine, :], matrix_ref[mine_too, :]], 0)
    both = jnp.dot(
        ghost_matrix, modes[:, own_width:width], precision=HIGHEST, preferred_element_type=F32
    )
    ghost_pos = both[0:8] + both[8:16] * ghost_factor
    for c in range(3):
        lent_pos[c] = fold(ghost_pos[:, c * LANES : (c + 1) * LANES], low)
    pos_copies = []
    for g, (a, c) in enumerate(AROUND):
        at = ATOMS + g * LANES
        cp = pltpu.make_async_remote_copy(
            src_ref=lent_pos,
            dst_ref=tab.at[0:3, :, at : at + LANES],
            send_sem=send3.at[g],
            recv_sem=recv3.at[g],
            device_id=brick_at(1 - a, 1 - c),
            device_id_type=MESH,
        )
        cp.start()
        pos_copies.append(cp)
    both = jnp.dot(
        matrix_ref[...], modes[:, 0:own_width], precision=HIGHEST, preferred_element_type=F32
    )
    for g in range(GROUPS):
        rows = slice(g * 8, g * 8 + 8)
        moved[rows, :] = both[rows] + both[64 + g * 8 : 72 + g * 8] * factor
    my_lanes = pl.ds(pl.multiple_of(group * own_width, LANES), own_width)
    copies = []
    for o in range(1, GROUPS):
        to = lax.rem(group + o, GROUPS)
        cp = pltpu.make_async_remote_copy(
            src_ref=moved.at[pl.ds(pl.multiple_of(to * 8, 8), 8), :],
            dst_ref=back.at[:, my_lanes],
            send_sem=send2.at[o],
            recv_sem=recv2.at[o],
            device_id={"bead": to},
            device_id_type=MESH,
        )
        cp.start()
        copies.append(cp)
    back[:, my_lanes] = moved[mine, :]

    def ghost_hits(d, carry):
        rows = sublanes((LANES, LANES)) + d * LANES
        hit = rows == jnp.broadcast_to(ghost_ref[...], (LANES, LANES))
        hit = jnp.where(hit, 1.0, 0.0).astype(BF16)
        ghost_onehot[:, pl.ds(pl.multiple_of(d * LANES, LANES), LANES)] = jnp.transpose(hit)
        return carry

    lax.fori_loop(0, CHUNKS, ghost_hits, 0)
    for cp in heavy_copies:
        cp.wait()

    def near_heavy(d, carry):
        lanes = pl.ds(pl.multiple_of(d * LANES, LANES), LANES)
        for half in range(2):
            rows = idx16[half * 8 : half * 8 + 8, lanes]
            lane = rows & (LANES - 1)
            heavy16[half * 8 : half * 8 + 8, lanes] = pick(
                [
                    lane_take(tab[3, :, t * LANES : (t + 1) * LANES], lane)
                    for t in range(TABLE // LANES)
                ],
                row_bits(rows, 4),
            )
        return carry

    lax.fori_loop(0, CHUNKS, near_heavy, 0)
    for kp in range(SLOTS // 2):
        heavy_pairs[kp] = jnp.where(
            low_all,
            jnp.broadcast_to(heavy16[2 * kp : 2 * kp + 1, :], (8, ATOMS)),
            jnp.broadcast_to(heavy16[2 * kp + 1 : 2 * kp + 2, :], (8, ATOMS)),
        )


    for cp in copies:
        cp.wait()
    for c in range(3):
        for d in range(CHUNKS):
            at = d * own_width + c * LANES
            v = back[:, at : at + LANES]
            newpos_ref[c, :, d * LANES : (d + 1) * LANES] = v[0:PER]
            newmom_ref[c, :, d * LANES : (d + 1) * LANES] = v[PER:8]
            tab[c, :, d * LANES : (d + 1) * LANES] = fold(v, low)
    storing = [
        pltpu.make_async_copy(newpos_ref, newpos_hbm, stores.at[0]),
        pltpu.make_async_copy(newmom_ref, newmom_hbm, stores.at[1]),
    ]
    for cp in storing:
        cp.start()
    for cp in pos_copies:
        cp.wait()

    slot_off = jnp.where(low, 0, 1)
    cos_scale = (math.pi / (2.0 * CUTOFF)) ** 2
    cos_terms = [(-1.0) ** n * cos_scale**n / math.factorial(2 * n) for n in range(8)]

    def by_block(terms, ids):
        terms = split(terms)
        zero = jnp.zeros_like(terms)
        return jnp.concatenate([jnp.where(ids == b, terms, zero) for b in range(BLOCKS)], 0)

    def radial(ci):
        lanes = pl.ds(pl.multiple_of(ci * LANES, LANES), LANES)
        sums = [jnp.zeros((8, LANES), F32) for _ in range(FEATS)]
        for kp in range(SLOTS // 2):
            d = dist[kp, :, lanes]
            wh = weight_h[kp, :, lanes]
            wl = weight_l[kp, :, lanes]
            for s in range(HALF):
                rate = -0.2 * 20.0 ** (s / (HALF - 1)) * math.log2(math.e)
                falloff = jnp.exp2(d * rate)
                sums[s] = sums[s] + wh * falloff
                sums[HALF + s] = sums[HALF + s] + wl * falloff
        for s in range(FEATS):
            v = jnp.log(1.0 + (sums[s] + pltpu.roll(sums[s], PER, 0)))
            feat_ref[ci, s * PER : (s + 1) * PER, :] = v[0:PER]

    def degree_part(ci, acc):
        lanes = pl.ds(pl.multiple_of(ci * LANES, LANES), LANES)
        tall = jnp.concatenate(
            [by_block(coup[k, :, lanes], block_ids[k, :, lanes]) for k in range(SLOTS)], 1
        )
        hits = jnp.concatenate(
            [
                onehot_t[pl.ds(pl.multiple_of(k * ATOMS + ci * LANES, LANES), LANES), :]
                for k in range(SLOTS)
            ],
            0,
        )
        return acc + jnp.dot(tall, hits, preferred_element_type=F32)

    def geometry(ci, acc):
        before = lax.rem(ci + CHUNKS - 1, CHUNKS)
        acc = degree_part(before, acc)
        radial(before)
        lanes = pl.ds(pl.multiple_of(ci * LANES, LANES), LANES)
        own = [tab[c, :, lanes] for c in range(3)]
        count = jnp.broadcast_to(counts_ref[:, lanes], (8, LANES))
        for kp in range(SLOTS // 2):
            rows = pairs[kp, :, lanes]
            lane = rows & (LANES - 1)
            bits = row_bits(rows, 4)
            dist_sq = jnp.zeros((8, LANES), F32)
            for c in range(3):
                near = pick(
                    [
                        lane_take(tab[c, :, t * LANES : (t + 1) * LANES], lane)
                        for t in range(TABLE // LANES)
                    ],
                    bits,
                )
                dist_sq = dist_sq + (near - own[c]) ** 2
            close = jnp.minimum(dist_sq, CUTOFF * CUTOFF)
            wave = jnp.full_like(close, cos_terms[-1])
            for term in cos_terms[-2::-1]:
                wave = wave * close + term
            used = ((2 * kp + slot_off) < count) & (dist_sq < CUTOFF * CUTOFF)
            smooth = jnp.where(used, wave * wave, 0.0)
            heavy_w = smooth * heavy_pairs[kp, :, lanes]
            dist[kp, :, lanes] = dist_sq
            weight_h[kp, :, lanes] = heavy_w
            weight_l[kp, :, lanes] = smooth - heavy_w
            coupling = smooth * lax.rsqrt(1.0 + dist_sq)
            turned = pltpu.roll(coupling, PER, 0)
            for k, v in ((2 * kp, jnp.where(low, coupling, turned)), (2 * kp + 1, jnp.where(low, turned, coupling))):
                coup[k, :, lanes] = v
        return acc

    acc = lax.fori_loop(0, CHUNKS, geometry, jnp.zeros((BLOCKS * BAND, WIDE), F32))
    acc = degree_part(CHUNKS - 1, acc)

    def scatter(terms_of):
        acc = jnp.zeros((BLOCKS * BAND, WIDE), F32)
        for g in range(SLOTS // GROUP):
            group_slots = range(g * GROUP, (g + 1) * GROUP)
            tall = jnp.concatenate([by_block(terms_of(k), block_ids[k]) for k in group_slots], 1)
            rows = slice(g * GROUP * ATOMS, (g + 1) * GROUP * ATOMS)
            acc = acc + jnp.dot(tall, onehot_t[rows, :], preferred_element_type=F32)
        return acc

    def chunk_of(acc, n):
        row, col = (n // 2) * BAND, (n % 2) * LANES
        return acc[row : row + 8, col : col + LANES] + acc[row + 8 : row + 16, col : col + LANES]

    def send_back(acc, par):
        out = []
        for g, (a, c) in enumerate(AROUND):
            spread[par, g] = chunk_of(acc, CHUNKS + g)
        for g, (a, c) in enumerate(AROUND):
            cp = pltpu.make_async_remote_copy(
                src_ref=spread.at[par, g],
                dst_ref=backin.at[par, g],
                send_sem=send_b.at[par, g],
                recv_sem=recv_b.at[par, g],
                device_id=brick_at(a - 1, c - 1),
                device_id_type=MESH,
            )
            cp.start()
            out.append(cp)
        return out

    def own_part(acc):
        return jnp.concatenate([chunk_of(acc, d) for d in range(CHUNKS)], 1)

    def take_back(copies, par):
        for cp in copies:
            cp.wait()
        received = backin[par, 0]
        for g in range(1, len(AROUND)):
            received = received + backin[par, g]
        returned = lax.dot_general(
            split(received), ghost_onehot[...], (((1,), (0,)), ((), ())), preferred_element_type=F32
        )
        return returned[0:8] + returned[8:16]

    def blocks_of(pieces):
        return jnp.concatenate([split(v) for v in pieces], 0)

    def by_product(tall, g, inside, acc):
        cols = slice(g * GROUP * ATOMS, (g + 1) * GROUP * ATOMS)
        found = jnp.dot(tall, onehot[:, cols], preferred_element_type=F32)
        for kk in range(GROUP):
            k = g * GROUP + kk
            f = found[:, kk * ATOMS : (kk + 1) * ATOMS]
            near = [
                f[q * BAND : q * BAND + 8] + f[q * BAND + 8 : q * BAND + 16]
                for q in range(OWN_BLOCKS)
            ]
            rows = rows_all[k]
            near = pick(near, [(rows & WIDE) != 0, (rows & (2 * WIDE)) != 0])
            hit = (rows < ATOMS) if inside else (rows >= ATOMS)
            acc = acc + jnp.where(hit, coup[k], 0.0) * near
        return acc

    def by_lookup(chunks, g, acc):
        out = []
        for d in range(CHUNKS):
            lanes = slice(d * LANES, (d + 1) * LANES)
            v = acc[:, lanes]
            for k in range(g * GROUP, (g + 1) * GROUP):
                rows = rows_all[k, :, lanes]
                lane = rows & (LANES - 1)
                near = pick([lane_take(t, lane) for t in chunks], row_bits(rows, 3))
                v = v + jnp.where(rows >= ATOMS, coup[k, :, lanes], 0.0) * near
            out.append(v)
        return jnp.concatenate(out, 1)

    def forward_own(v, acc):
        tall = blocks_of([v[:, q * WIDE : (q + 1) * WIDE] for q in range(OWN_BLOCKS)])
        for g in range(SLOTS // GROUP):
            acc = by_product(tall, g, True, acc)
        return acc

    def forward_ghosts(par, acc):
        chunks = [ghost_in[par, t] for t in range(len(AROUND))]
        tall = blocks_of(
            [jnp.concatenate(chunks[2 * q : 2 * q + 2], 1) for q in range(OWN_BLOCKS)]
        )
        half = SLOTS // GROUP // 2
        for g in range(half):
            acc = by_product(tall, g, False, acc)
            acc = by_lookup(chunks, half + g, acc)
        return acc

    first_back = send_back(acc, 2)
    radial(CHUNKS - 1)
    around = own_part(acc)
    for k in range(SLOTS):
        around = around + coup[k]
    degree[...] = around

    hidden = product(wide1[...], features_of(feat_ref))
    for b, chi in enumerate(network(hidden, wide2, wide3, heavy_row)):
        residual[b : b + 1, :] = -CHI_SCALE * chi
    residual[PER:8, :] = jnp.broadcast_to(1.0 - heavy, (PER, ATOMS))
    h0, h1 = hardness_ref[0], hardness_ref[1]
    hard = jnp.where(heavy_row, h0, h1)

    lane_id = lax.broadcasted_iota(jnp.int32, (8, LANES), 1)

    def dots_of(r):
        dots = [lanes_sum(r * r), lanes_sum(r * image[...]), lanes_sum(r * steps[...]), lanes_sum(r)]
        v = dots[3]
        for n in (2, 1, 0):
            v = jnp.where(lane_id == n, dots[n], v)
        return v

    def send_lent(ref, par):
        lent[par] = at_ghosts(ref[...])
        out = []
        for g, (a, c) in enumerate(AROUND):
            cp = pltpu.make_async_remote_copy(
                src_ref=lent.at[par],
                dst_ref=ghost_in.at[par, g],
                send_sem=send_a.at[par, g],
                recv_sem=recv_a.at[par, g],
                device_id=brick_at(1 - a, 1 - c),
                device_id_type=MESH,
            )
            cp.start()
            out.append(cp)
        return out

    def dot_copies(par, targets):
        out = []
        for dx, dy in targets:
            n = dx * SIDE + dy
            out.append(
                pltpu.make_async_remote_copy(
                    src_ref=parts.at[par, me],
                    dst_ref=parts.at[par, me],
                    send_sem=send_d.at[par, n],
                    recv_sem=recv_d.at[par, n],
                    device_id=brick_at(dx, dy),
                    device_id_type=MESH,
                )
            )
        return out

    def send_dots(par, targets):
        out = dot_copies(par, targets)
        for cp in out:
            cp.start()
        return out

    def take_dots(copies, par):
        for cp in copies:
            cp.wait()
        whole = parts[par, 0]
        for n in range(1, BRICKS):
            whole = whole + parts[par, n]
        return [whole[:, n : n + 1] for n in range(4)]

    alpha_max = 2.0 / jnp.minimum(h0, h1)

    def step_sizes(dots, state, start):
        norm, rw, rs, r_sum = dots
        norm_prev, curve_prev, sum_prev, sum_total = state
        beta = jnp.where(start, 0.0, norm / jnp.maximum(norm_prev, TINY))
        curve = rw + 2.0 * beta * rs + beta * beta * curve_prev
        alpha = jnp.minimum(norm / jnp.maximum(curve, TINY), alpha_max)
        p_sum = r_sum + beta * sum_prev
        return alpha, beta, (norm, curve, p_sum, sum_total + alpha * p_sum)

    image[...] = residual[...]
    for ref in (direction, steps, image2, total):
        ref[...] = jnp.zeros_like(ref)
    high = jnp.logical_not(low_all)
    high_col = sublanes((8, 1)) >= PER

    def sweep(it, state):
        par = lax.rem(it, 2)
        start = it == 1
        r, w = residual[...], image[...]
        first = send_lent(image, par)

        @pl.when(it > 0)
        def _():
            parts[par, me] = dots_of(r)
            send_dots(par, others)

        acc = scatter(lambda k: coup[k] * image[...])
        second = send_back(acc, par)
        around = forward_own(w, own_part(acc))
        for cp in first:
            cp.wait()
        around = forward_ghosts(par, around)

        @pl.when(it == 0)
        def _():
            degree[...] = hard + 0.5 * (degree[...] + take_back(first_back, 2))

        @pl.when(it > 0)
        def _():
            for cp in dot_copies(par, others):
                cp.wait()

        dots = take_dots([], par)
        light = dots[3]
        alpha, beta, state = step_sizes(dots, state, start)
        q = degree[...] * w - 0.5 * (around + take_back(second, par))
        z = q + beta * image2[...]
        s = w + beta * steps[...]
        p = r + beta * direction[...]
        x = total[...] + alpha * p
        r_new = r - alpha * s
        w_new = w - alpha * z
        known = jnp.logical_and(start, high)
        gap = h1 - h0
        hard_sum = (TOTAL_ATOMS - light) * h0 + light * h1
        c0 = light / hard_sum
        c1 = -TOTAL_ATOMS / hard_sum
        direction[...] = jnp.where(known, 1.0, p)
        steps[...] = jnp.where(known, hard, s)
        image2[...] = jnp.where(known, h0 * hard + gap * w, z)
        total[...] = jnp.where(known, TOTAL_ATOMS / hard_sum, x)
        residual[...] = jnp.where(known, gap * (c0 + c1 * r), r_new)
        image[...] = jnp.where(it == 0, q, jnp.where(known, gap * (c0 * hard + c1 * w), w_new))
        exact = (
            jnp.full((8, 1), TOTAL_ATOMS, F32),
            hard_sum,
            jnp.full((8, 1), TOTAL_ATOMS, F32),
            TOTAL_ATOMS / hard_sum * TOTAL_ATOMS,
        )
        known_col = jnp.logical_and(start, high_col)
        return tuple(jnp.where(known_col, e, v) for e, v in zip(exact, state))

    zero = jnp.zeros((8, 1), F32)
    state = lax.fori_loop(0, ITERS, sweep, (zero, zero, zero, zero))
    par = ITERS % 2
    parts[par, me] = dots_of(residual[...])
    third = send_dots(par, others)

    first_layer[...] = product(last1[...], features_of(feat_ref))
    dots = take_dots(third, par)
    alpha, beta, state = step_sizes(dots, state, False)
    x = total[...] + alpha * (residual[...] + beta * direction[...])
    sums = state[3]
    charges = x[0:PER] - (sums[0:PER] / sums[PER:8]) * x[PER:8]
    charge_ref[...] = charges
    storing.append(pltpu.make_async_copy(charge_ref, charge_hbm, stores.at[2]))
    storing[2].start()
    column = last1[:, FEATS : FEATS + 1]

    hidden = jnp.concatenate(
        [
            first_layer[:, b * ATOMS : (b + 1) * ATOMS] + column * charges[b : b + 1]
            for b in range(PER)
        ],
        1,
    )
    for b, e in enumerate(network(hidden, last2, last3, heavy_row)):
        energy_ref[b : b + 1, :] = e
    storing.append(pltpu.make_async_copy(energy_ref, energy_hbm, stores.at[3]))
    storing[3].start()
    for cp in storing:
        cp.wait()


def outputs_kernel(a_ref, b_ref, c_ref, d_ref, a_out, b_out, c_out, d_out):
    for src, dst in ((a_ref, a_out), (b_ref, b_out), (c_ref, c_out), (d_ref, d_out)):
        dst[...] = src[...]


def vmem(count):
    return [pl.BlockSpec(memory_space=pltpu.VMEM)] * count


def anywhere(count):
    return [pl.BlockSpec(memory_space=pl.ANY)] * count


def sds(*shape, dtype=F32):
    return jax.ShapeDtypeStruct(shape, dtype)


def f32(*shape):
    return pltpu.VMEM(shape, F32)


def on_device(
    positions,
    momenta,
    types,
    ghost_rows,
    neighbours,
    counts,
    hardness,
    chi_w1,
    chi_w2,
    chi_w3,
    en_w1,
    en_w2,
    en_w3,
):
    turn = lambda v: jnp.transpose(v, (1, 0, 2))
    dma = pltpu.SemaphoreType.DMA
    networks = [f32(2 * PAD, PAD), f32(2 * PAD, 2 * PAD), f32(8, 2 * PAD)]
    operands = (
        hardness,
        jnp.asarray(propagator()),
        turn(positions),
        turn(momenta),
        types.reshape(1, ATOMS),
        ghost_rows.reshape(1, LANES),
        neighbours,
        counts.reshape(1, ATOMS),
        turn(chi_w1),
        turn(chi_w2),
        chi_w3,
        turn(en_w1),
        turn(en_w2),
        en_w3,
    )
    outputs = (sds(3, PER, ATOMS), sds(3, PER, ATOMS), sds(PER, ATOMS), sds(PER, ATOMS))
    results = pl.pallas_call(
        main_kernel,
        name="main",
        out_shape=outputs,
        in_specs=anywhere(len(operands)),
        out_specs=tuple(anywhere(len(outputs))),
        scratch_shapes=[
            pltpu.SMEM(hardness.shape, F32),
            *[pltpu.VMEM(v.shape, v.dtype) for v in operands[1:]],
            *[f32(*v.shape) for v in outputs],
            f32(CHUNKS, LANES, LANES),
            f32(8, 6 * ATOMS),
            f32(64, 6 * LANES),
            f32(64, 3 * LANES),
            f32(8, 3 * ATOMS),
            f32(3, 8, LANES),
            f32(8, LANES),
            f32(4, 8, TABLE),
            pltpu.VMEM((SLOTS, ATOMS), jnp.int32),
            f32(SLOTS, ATOMS),
            pltpu.VMEM((SLOTS, 8, ATOMS), jnp.int32),
            pltpu.VMEM((SLOTS // 2, 8, ATOMS), jnp.int32),
            f32(SLOTS // 2, 8, ATOMS),
            pltpu.VMEM((SLOTS, BAND, ATOMS), BF16),
            pltpu.VMEM((WIDE, EDGES), BF16),
            pltpu.VMEM((EDGES, WIDE), BF16),
            pltpu.VMEM((LANES, ATOMS), BF16),
            f32(SLOTS, 8, ATOMS),
            f32(SLOTS // 2, 8, ATOMS),
            f32(SLOTS // 2, 8, ATOMS),
            f32(SLOTS // 2, 8, ATOMS),
            *networks,
            *networks,
            f32(2 * PAD, PER * ATOMS),
            *[f32(8, ATOMS) for _ in range(7)],
            f32(3, 8, 8, LANES),
            f32(2, 8, LANES),
            f32(2, 8, 8, LANES),
            f32(3, 8, 8, LANES),
            f32(2, BRICKS, 8, LANES),
            *[dma((GROUPS,)) for _ in range(4)],
            *[dma((8,)) for _ in range(4)],
            *[dma((2, 8)) for _ in range(2)],
            *[dma((3, 8)) for _ in range(2)],
            *[dma((2, BRICKS)) for _ in range(2)],
            dma((len(operands),)),
            dma((len(outputs),)),
        ],
        compiler_params=pltpu.CompilerParams(
            vmem_limit_bytes=VMEM_LIMIT, collective_id=0, has_side_effects=True
        ),
    )(*operands)
    new_pos, new_mom, charges, energies = pl.pallas_call(
        outputs_kernel,
        name="outputs",
        out_shape=outputs,
        in_specs=vmem(len(outputs)),
        out_specs=tuple(vmem(len(outputs))),
    )(*results)
    return (turn(new_pos), turn(new_mom), charges, energies)


def solution(mesh):
    placed = (
        P("bead", None, ("gx", "gy")),
        P("bead", None, ("gx", "gy")),
        P(("gx", "gy")),
        P(("gx", "gy")),
        P(None, ("gx", "gy")),
        P(("gx", "gy")),
        P(),
        P(),
        P(),
        P(),
        P(),
        P(),
        P(),
    )
    return jax.shard_map(
        on_device,
        mesh=mesh,
        in_specs=placed,
        out_specs=(
            P("bead", None, ("gx", "gy")),
            P("bead", None, ("gx", "gy")),
            P("bead", ("gx", "gy")),
            P("bead", ("gx", "gy")),
        ),
        check_vma=False,
    )
```

```python
import functools
import math

import jax
import jax.numpy as jnp
import numpy as np
from jax import lax
from jax.experimental import pallas as pl
from jax.experimental.pallas import tpu as pltpu
from jax.sharding import PartitionSpec as P

MESH = pl.DeviceIdType.MESH
F32 = jnp.float32
BF16 = jnp.bfloat16
HIGHEST = lax.Precision.HIGHEST
ITERS = 5
STEP = 0.5
TOP_FREQ = 80.0
CUTOFF = 4.0
HEAVY_MASS = 16.0
CHI_SCALE = 4.0
LANES = 128
BEADS = 32
GROUPS = 8
PER = 4
ATOMS = 1024
CHUNKS = ATOMS // LANES
SLOTS = 16
TABLE = ATOMS + 8 * LANES
HALF = 15
FEATS = 2 * HALF
SIDE = 4
PAD = 32
BRICKS = SIDE * SIDE
BAND = 16
WIDE = 256
BLOCKS = TABLE // WIDE
OWN_BLOCKS = ATOMS // WIDE
EDGES = SLOTS * ATOMS
GROUP = 4
EARLY = 10
TOTAL_ATOMS = ATOMS * BRICKS
TINY = 1e-30
SELF = ATOMS + 4 * LANES
VMEM_LIMIT = 60 * 1024 * 1024


def propagator():
    k = np.arange(BEADS)
    omega = TOP_FREQ * np.sin(math.pi * k / BEADS)
    cosine = np.cos(omega * STEP)
    sine = np.sin(omega * STEP)
    drift = np.where(k > 0, TOP_FREQ * sine / np.where(k > 0, omega, 1.0), TOP_FREQ * STEP)
    restoring = -(omega / TOP_FREQ) * sine
    gap = (k[:, None] - k[None, :]) % BEADS

    def spread(weights):
        line = (weights[None, :] * np.cos(2 * math.pi * k[:, None] * k[None, :] / BEADS)).sum(1) / BEADS
        return line[gap]

    keep, push, pull = spread(cosine), spread(drift), spread(restoring)
    zero = np.zeros_like(keep)
    plain = np.block([[keep, zero], [zero, keep]])
    massive = np.block([[zero, push], [pull, zero]])
    order = np.array([half * BEADS + g * PER + b for g in range(GROUPS) for half in range(2) for b in range(PER)])
    both = np.concatenate([plain[order][:, order], massive[order][:, order]], 0)
    return both.astype(np.float32)


def sublanes(shape):
    return lax.broadcasted_iota(jnp.int32, shape, 0)


def lane_take(table, lane):
    return jnp.take_along_axis(table, lane, axis=1, mode="promise_in_bounds")


def row_bits(rows, count):
    return [(rows & (LANES << bit)) != 0 for bit in range(count)]


def pick(parts, bits):
    level = 0
    while len(parts) > 1:
        nxt = [
            jnp.where(bits[level], parts[i + 1], parts[i]) for i in range(0, len(parts) - 1, 2)
        ]
        if len(parts) % 2:
            nxt.append(parts[-1])
        parts = nxt
        level += 1
    return parts[0]


def split(v):
    top = v.astype(BF16).astype(F32)
    return jnp.concatenate([top, v - top], 0).astype(BF16)


def halves(v):
    top = v.astype(BF16)
    return top, (v - top.astype(F32)).astype(BF16)


def lanes_sum(v):
    return jnp.sum(v, axis=1, keepdims=True)


def fold(v, low):
    return jnp.where(low, v, pltpu.roll(v, PER, 0))


def brick_at(dx, dy):
    return {
        "gx": lax.rem(lax.axis_index("gx") + dx + SIDE, SIDE),
        "gy": lax.rem(lax.axis_index("gy") + dy + SIDE, SIDE),
    }


AROUND = [(a, c) for a in range(3) for c in range(3) if (a, c) != (1, 1)]


def load_weights(w1_ref, w2_ref, w3_ref, wide1, wide2, wide3):
    rows, cols = w1_ref.shape[0], w1_ref.shape[2]
    for ref in (wide1, wide2, wide3):
        ref[...] = jnp.zeros_like(ref)
    for e in range(2):
        at = e * PAD
        wide1[at : at + rows, 0:cols] = w1_ref[:, e, :]
        wide2[at : at + rows, at : at + rows] = w2_ref[:, e, :]
        wide3[e : e + 1, at : at + rows] = w3_ref[e : e + 1, :]


def product(w, f):
    w_top, w_rest = halves(w)
    f_top, f_rest = halves(f)
    rows = w.shape[0]
    both = jnp.dot(jnp.concatenate([w_top, w_rest], 0), f_top, preferred_element_type=F32)
    return both[0:rows] + both[rows:] + jnp.dot(w_top, f_rest, preferred_element_type=F32)


def features_of(feat_ref):
    return jnp.concatenate(
        [feat_ref[d, pl.ds(b, PAD, stride=PER), :] for b in range(PER) for d in range(CHUNKS)], 1
    )


def network(hidden, wide2, wide3, heavy):
    out = product(wide3[...], jnp.tanh(product(wide2[...], jnp.tanh(hidden))))
    return [
        jnp.where(
            heavy, out[0:1, b * ATOMS : (b + 1) * ATOMS], out[1:2, b * ATOMS : (b + 1) * ATOMS]
        )
        for b in range(PER)
    ]


def main_kernel(
    hardness_hbm,
    matrix_hbm,
    pos_hbm,
    mom_hbm,
    types_hbm,
    ghost_hbm,
    idx_hbm,
    counts_hbm,
    w1_hbm,
    w2_hbm,
    w3_hbm,
    v1_hbm,
    v2_hbm,
    v3_hbm,
    newpos_hbm,
    newmom_hbm,
    charge_hbm,
    energy_hbm,
    hardness_ref,
    matrix_ref,
    pos_ref,
    mom_ref,
    types_ref,
    ghost_ref,
    idx_ref,
    counts_ref,
    w1_ref,
    w2_ref,
    w3_ref,
    v1_ref,
    v2_ref,
    v3_ref,
    newpos_ref,
    newmom_ref,
    charge_ref,
    energy_ref,
    feat_ref,
    stage,
    modes,
    moved,
    back,
    lent_pos,
    lent_heavy,
    tab,
    idx16,
    heavy16,
    rows_all,
    pairs,
    heavy_pairs,
    block_ids,
    onehot,
    onehot_t,
    ghost_onehot,
    coup,
    dist,
    weight_h,
    weight_l,
    wide1,
    wide2,
    wide3,
    last1,
    last2,
    last3,
    first_layer,
    residual,
    image,
    image2,
    direction,
    steps,
    total,
    degree,
    spread,
    lent,
    ghost_in,
    backin,
    parts,
    send1,
    recv1,
    send2,
    recv2,
    send3,
    recv3,
    send4,
    recv4,
    send_a,
    recv_a,
    send_b,
    recv_b,
    send_d,
    recv_d,
    loads,
    stores,
):
    group = lax.axis_index("bead")
    me = lax.axis_index("gx") * SIDE + lax.axis_index("gy")
    others = [(o // SIDE, o % SIDE) for o in range(1, BRICKS)]
    parts[...] = jnp.zeros_like(parts)
    barrier = pltpu.get_barrier_semaphore()
    for o in range(1, GROUPS):
        pl.semaphore_signal(
            barrier, inc=1, device_id={"bead": lax.rem(group + o, GROUPS)}, device_id_type=MESH
        )
    for a, c in AROUND:
        pl.semaphore_signal(barrier, inc=1, device_id=brick_at(a - 1, c - 1), device_id_type=MESH)
    loading = [
        pltpu.make_async_copy(src, dst, loads.at[n])
        for n, (src, dst) in enumerate(
            (
                (pos_hbm, pos_ref),
                (mom_hbm, mom_ref),
                (ghost_hbm, ghost_ref),
                (types_hbm, types_ref),
                (idx_hbm, idx_ref),
                (matrix_hbm, matrix_ref),
                (counts_hbm, counts_ref),
                (hardness_hbm, hardness_ref),
                (w1_hbm, w1_ref),
                (w2_hbm, w2_ref),
                (w3_hbm, w3_ref),
                (v1_hbm, v1_ref),
                (v2_hbm, v2_ref),
                (v3_hbm, v3_ref),
            )
        )
    ]
    for cp in loading:
        cp.start()
    for cp in loading[0:4]:
        cp.wait()

    low = sublanes((8, LANES)) < PER
    low_all = sublanes((8, ATOMS)) < PER
    own_width = 3 * LANES
    width = 2 * own_width
    ghost_rows = jnp.broadcast_to(ghost_ref[...], (8, LANES))
    ghost_lane = ghost_rows & (LANES - 1)
    ghost_bits = row_bits(ghost_rows, 3)

    def at_ghosts(v):
        return pick(
            [lane_take(v[:, d * LANES : (d + 1) * LANES], ghost_lane) for d in range(CHUNKS)],
            ghost_bits,
        )

    heavy_row = types_ref[...] == 0
    heavy = jnp.where(heavy_row, 1.0, 0.0)
    tab[3, :, 0:ATOMS] = jnp.broadcast_to(heavy, (8, ATOMS))
    ghost_heavy = at_ghosts(jnp.broadcast_to(heavy, (8, ATOMS)))
    lent_heavy[...] = ghost_heavy
    for c in range(3):
        v = jnp.concatenate([pos_ref[c], mom_ref[c]], 0)
        g = at_ghosts(v)
        for d in range(CHUNKS):
            at = d * width + c * LANES
            stage[:, at : at + LANES] = v[:, d * LANES : (d + 1) * LANES]
            stage[:, at + own_width : at + own_width + LANES] = g
    pl.semaphore_wait(barrier, GROUPS - 1 + len(AROUND))

    mine = pl.ds(pl.multiple_of(group * 8, 8), 8)
    mine_too = pl.ds(pl.multiple_of(64 + group * 8, 8), 8)
    copies = []
    for o in range(1, GROUPS):
        to = lax.rem(group + o, GROUPS)
        cp = pltpu.make_async_remote_copy(
            src_ref=stage.at[:, pl.ds(pl.multiple_of(to * width, LANES), width)],
            dst_ref=modes.at[mine, :],
            send_sem=send1.at[o],
            recv_sem=recv1.at[o],
            device_id={"bead": to},
            device_id_type=MESH,
        )
        cp.start()
        copies.append(cp)
    heavy_copies = []
    for g, (a, c) in enumerate(AROUND):
        at = ATOMS + g * LANES
        cp = pltpu.make_async_remote_copy(
            src_ref=lent_heavy,
            dst_ref=tab.at[3, :, at : at + LANES],
            send_sem=send4.at[g],
            recv_sem=recv4.at[g],
            device_id=brick_at(1 - a, 1 - c),
            device_id_type=MESH,
        )
        cp.start()
        heavy_copies.append(cp)
    modes[mine, :] = stage[:, pl.ds(pl.multiple_of(group * width, LANES), width)]

    for cp in loading[4:]:
        cp.wait()
    def renumber(d, carry):
        lanes = pl.ds(pl.multiple_of(d * LANES, LANES), LANES)
        for half in range(2):
            rows = idx_ref[half * 8 : half * 8 + 8, lanes]
            local = lane_take(ghost_rows, rows & (LANES - 1))
            rows = jnp.where(
                rows < SELF, rows, jnp.where(rows < SELF + LANES, local, rows - LANES)
            )
            idx16[half * 8 : half * 8 + 8, lanes] = rows
        return carry

    lax.fori_loop(0, CHUNKS, renumber, 0)
    for k in range(SLOTS):
        rows_all[k] = jnp.broadcast_to(idx16[k : k + 1, :], (8, ATOMS))
    within = sublanes((WIDE, ATOMS)).astype(F32).astype(BF16)

    def build(k, carry):
        rows = rows_all[k]
        ids = (rows >> 8).astype(F32)
        block_ids[k] = jnp.concatenate([ids, ids], 0).astype(BF16)
        wide = (rows & (WIDE - 1)).astype(F32)
        wide = jnp.concatenate([wide, wide], 0).astype(BF16)
        wide = jnp.concatenate([wide] * (WIDE // BAND), 0)
        edges = pl.ds(pl.multiple_of(k * ATOMS, ATOMS), ATOMS)
        hits = jnp.where(within == wide, 1.0, 0.0).astype(BF16)
        onehot[:, edges] = hits
        onehot_t[edges, :] = jnp.transpose(hits)
        return carry

    lax.fori_loop(0, EARLY, build, 0)
    for ref in (coup, dist, weight_h, weight_l, feat_ref):
        ref[...] = jnp.zeros_like(ref)

    def pair_up(kp, carry):
        pairs[kp] = jnp.where(low_all, rows_all[2 * kp], rows_all[2 * kp + 1])
        return carry

    lax.fori_loop(0, SLOTS // 2, pair_up, 0)
    load_weights(w1_ref, w2_ref, w3_ref, wide1, wide2, wide3)
    load_weights(v1_ref, v2_ref, v3_ref, last1, last2, last3)
    my_types = types_ref[:, pl.ds(pl.multiple_of(group * LANES, LANES), LANES)]
    mass = jnp.broadcast_to(jnp.where(my_types == 0, HEAVY_MASS, 1.0), (8, LANES))
    factor = jnp.concatenate([jnp.where(low, 1.0 / mass, mass)] * 3, 1)
    ghost_mass = jnp.where(ghost_heavy > 0.0, HEAVY_MASS, 1.0)
    ghost_factor = jnp.concatenate([1.0 / ghost_mass] * 3, 1)

    for cp in copies:
        cp.wait()
    ghost_matrix = jnp.concatenate([matrix_ref[mine, :], matrix_ref[mine_too, :]], 0)
    both = jnp.dot(
        ghost_matrix, modes[:, own_width:width], precision=HIGHEST, preferred_element_type=F32
    )
    ghost_pos = both[0:8] + both[8:16] * ghost_factor
    for c in range(3):
        lent_pos[c] = fold(ghost_pos[:, c * LANES : (c + 1) * LANES], low)
    pos_copies = []
    for g, (a, c) in enumerate(AROUND):
        at = ATOMS + g * LANES
        cp = pltpu.make_async_remote_copy(
            src_ref=lent_pos,
            dst_ref=tab.at[0:3, :, at : at + LANES],
            send_sem=send3.at[g],
            recv_sem=recv3.at[g],
            device_id=brick_at(1 - a, 1 - c),
            device_id_type=MESH,
        )
        cp.start()
        pos_copies.append(cp)
    both = jnp.dot(
        matrix_ref[...], modes[:, 0:own_width], precision=HIGHEST, preferred_element_type=F32
    )
    for g in range(GROUPS):
        rows = slice(g * 8, g * 8 + 8)
        moved[rows, :] = both[rows] + both[64 + g * 8 : 72 + g * 8] * factor
    my_lanes = pl.ds(pl.multiple_of(group * own_width, LANES), own_width)
    copies = []
    for o in range(1, GROUPS):
        to = lax.rem(group + o, GROUPS)
        cp = pltpu.make_async_remote_copy(
            src_ref=moved.at[pl.ds(pl.multiple_of(to * 8, 8), 8), :],
            dst_ref=back.at[:, my_lanes],
            send_sem=send2.at[o],
            recv_sem=recv2.at[o],
            device_id={"bead": to},
            device_id_type=MESH,
        )
        cp.start()
        copies.append(cp)
    back[:, my_lanes] = moved[mine, :]

    def ghost_hits(d, carry):
        rows = sublanes((LANES, LANES)) + d * LANES
        hit = rows == jnp.broadcast_to(ghost_ref[...], (LANES, LANES))
        hit = jnp.where(hit, 1.0, 0.0).astype(BF16)
        ghost_onehot[:, pl.ds(pl.multiple_of(d * LANES, LANES), LANES)] = jnp.transpose(hit)
        return carry

    lax.fori_loop(0, CHUNKS, ghost_hits, 0)
    for cp in heavy_copies:
        cp.wait()

    def near_heavy(d, carry):
        lanes = pl.ds(pl.multiple_of(d * LANES, LANES), LANES)
        for half in range(2):
            rows = idx16[half * 8 : half * 8 + 8, lanes]
            lane = rows & (LANES - 1)
            heavy16[half * 8 : half * 8 + 8, lanes] = pick(
                [
                    lane_take(tab[3, :, t * LANES : (t + 1) * LANES], lane)
                    for t in range(TABLE // LANES)
                ],
                row_bits(rows, 4),
            )
        return carry

    lax.fori_loop(0, CHUNKS, near_heavy, 0)
    lax.fori_loop(EARLY, SLOTS, build, 0)
    for kp in range(SLOTS // 2):
        heavy_pairs[kp] = jnp.where(
            low_all,
            jnp.broadcast_to(heavy16[2 * kp : 2 * kp + 1, :], (8, ATOMS)),
            jnp.broadcast_to(heavy16[2 * kp + 1 : 2 * kp + 2, :], (8, ATOMS)),
        )


    for cp in copies:
        cp.wait()
    for c in range(3):
        for d in range(CHUNKS):
            at = d * own_width + c * LANES
            v = back[:, at : at + LANES]
            newpos_ref[c, :, d * LANES : (d + 1) * LANES] = v[0:PER]
            newmom_ref[c, :, d * LANES : (d + 1) * LANES] = v[PER:8]
            tab[c, :, d * LANES : (d + 1) * LANES] = fold(v, low)
    storing = [
        pltpu.make_async_copy(newpos_ref, newpos_hbm, stores.at[0]),
        pltpu.make_async_copy(newmom_ref, newmom_hbm, stores.at[1]),
    ]
    for cp in storing:
        cp.start()
    for cp in pos_copies:
        cp.wait()

    slot_off = jnp.where(low, 0, 1)
    cos_scale = (math.pi / (2.0 * CUTOFF)) ** 2
    cos_terms = [(-1.0) ** n * cos_scale**n / math.factorial(2 * n) for n in range(8)]

    def by_block(terms, ids):
        terms = split(terms)
        zero = jnp.zeros_like(terms)
        return jnp.concatenate([jnp.where(ids == b, terms, zero) for b in range(BLOCKS)], 0)

    def radial(ci):
        lanes = pl.ds(pl.multiple_of(ci * LANES, LANES), LANES)
        sums = [jnp.zeros((8, LANES), F32) for _ in range(FEATS)]
        for kp in range(SLOTS // 2):
            d = dist[kp, :, lanes]
            wh = weight_h[kp, :, lanes]
            wl = weight_l[kp, :, lanes]
            for s in range(HALF):
                rate = -0.2 * 20.0 ** (s / (HALF - 1)) * math.log2(math.e)
                falloff = jnp.exp2(d * rate)
                sums[s] = sums[s] + wh * falloff
                sums[HALF + s] = sums[HALF + s] + wl * falloff
        for s in range(FEATS):
            v = jnp.log(1.0 + (sums[s] + pltpu.roll(sums[s], PER, 0)))
            feat_ref[ci, s * PER : (s + 1) * PER, :] = v[0:PER]

    def degree_part(ci, acc):
        lanes = pl.ds(pl.multiple_of(ci * LANES, LANES), LANES)
        tall = jnp.concatenate(
            [by_block(coup[k, :, lanes], block_ids[k, :, lanes]) for k in range(SLOTS)], 1
        )
        hits = jnp.concatenate(
            [
                onehot_t[pl.ds(pl.multiple_of(k * ATOMS + ci * LANES, LANES), LANES), :]
                for k in range(SLOTS)
            ],
            0,
        )
        return acc + jnp.dot(tall, hits, preferred_element_type=F32)

    def geometry(ci, acc):
        before = lax.rem(ci + CHUNKS - 1, CHUNKS)
        acc = degree_part(before, acc)
        radial(before)
        lanes = pl.ds(pl.multiple_of(ci * LANES, LANES), LANES)
        own = [tab[c, :, lanes] for c in range(3)]
        count = jnp.broadcast_to(counts_ref[:, lanes], (8, LANES))
        for kp in range(SLOTS // 2):
            rows = pairs[kp, :, lanes]
            lane = rows & (LANES - 1)
            bits = row_bits(rows, 4)
            dist_sq = jnp.zeros((8, LANES), F32)
            for c in range(3):
                near = pick(
                    [
                        lane_take(tab[c, :, t * LANES : (t + 1) * LANES], lane)
                        for t in range(TABLE // LANES)
                    ],
                    bits,
                )
                dist_sq = dist_sq + (near - own[c]) ** 2
            close = jnp.minimum(dist_sq, CUTOFF * CUTOFF)
            wave = jnp.full_like(close, cos_terms[-1])
            for term in cos_terms[-2::-1]:
                wave = wave * close + term
            used = ((2 * kp + slot_off) < count) & (dist_sq < CUTOFF * CUTOFF)
            smooth = jnp.where(used, wave * wave, 0.0)
            heavy_w = smooth * heavy_pairs[kp, :, lanes]
            dist[kp, :, lanes] = dist_sq
            weight_h[kp, :, lanes] = heavy_w
            weight_l[kp, :, lanes] = smooth - heavy_w
            coupling = smooth * lax.rsqrt(1.0 + dist_sq)
            turned = pltpu.roll(coupling, PER, 0)
            for k, v in ((2 * kp, jnp.where(low, coupling, turned)), (2 * kp + 1, jnp.where(low, turned, coupling))):
                coup[k, :, lanes] = v
        return acc

    acc = lax.fori_loop(0, CHUNKS, geometry, jnp.zeros((BLOCKS * BAND, WIDE), F32))
    acc = degree_part(CHUNKS - 1, acc)

    def scatter(terms_of, beside):
        acc = jnp.zeros((BLOCKS * BAND, WIDE), F32)
        for g in range(SLOTS // GROUP):
            beside(g)
            group_slots = range(g * GROUP, (g + 1) * GROUP)
            tall = jnp.concatenate([by_block(terms_of(k), block_ids[k]) for k in group_slots], 1)
            rows = slice(g * GROUP * ATOMS, (g + 1) * GROUP * ATOMS)
            acc = acc + jnp.dot(tall, onehot_t[rows, :], preferred_element_type=F32)
        return acc

    def chunk_of(acc, n):
        row, col = (n // 2) * BAND, (n % 2) * LANES
        return acc[row : row + 8, col : col + LANES] + acc[row + 8 : row + 16, col : col + LANES]

    def send_back(acc, par):
        out = []
        for g, (a, c) in enumerate(AROUND):
            spread[par, g] = chunk_of(acc, CHUNKS + g)
        for g, (a, c) in enumerate(AROUND):
            cp = pltpu.make_async_remote_copy(
                src_ref=spread.at[par, g],
                dst_ref=backin.at[par, g],
                send_sem=send_b.at[par, g],
                recv_sem=recv_b.at[par, g],
                device_id=brick_at(a - 1, c - 1),
                device_id_type=MESH,
            )
            cp.start()
            out.append(cp)
        return out

    def own_part(acc):
        return jnp.concatenate([chunk_of(acc, d) for d in range(CHUNKS)], 1)

    def take_back(copies, par):
        for cp in copies:
            cp.wait()
        received = backin[par, 0]
        for g in range(1, len(AROUND)):
            received = received + backin[par, g]
        returned = lax.dot_general(
            split(received), ghost_onehot[...], (((1,), (0,)), ((), ())), preferred_element_type=F32
        )
        return returned[0:8] + returned[8:16]

    def blocks_of(pieces):
        return jnp.concatenate([split(v) for v in pieces], 0)

    def by_product(tall, g, inside, acc):
        cols = slice(g * GROUP * ATOMS, (g + 1) * GROUP * ATOMS)
        found = jnp.dot(tall, onehot[:, cols], preferred_element_type=F32)
        for kk in range(GROUP):
            k = g * GROUP + kk
            f = found[:, kk * ATOMS : (kk + 1) * ATOMS]
            near = [
                f[q * BAND : q * BAND + 8] + f[q * BAND + 8 : q * BAND + 16]
                for q in range(OWN_BLOCKS)
            ]
            rows = rows_all[k]
            near = pick(near, [(rows & WIDE) != 0, (rows & (2 * WIDE)) != 0])
            hit = (rows < ATOMS) if inside else (rows >= ATOMS)
            acc = acc + jnp.where(hit, coup[k], 0.0) * near
        return acc

    def by_lookup(chunks, g, acc):
        out = []
        for d in range(CHUNKS):
            lanes = slice(d * LANES, (d + 1) * LANES)
            v = acc[:, lanes]
            for k in range(g * GROUP, (g + 1) * GROUP):
                rows = rows_all[k, :, lanes]
                lane = rows & (LANES - 1)
                near = pick([lane_take(t, lane) for t in chunks], row_bits(rows, 3))
                v = v + jnp.where(rows >= ATOMS, coup[k, :, lanes], 0.0) * near
            out.append(v)
        return jnp.concatenate(out, 1)

    def forward_own(v, acc):
        tall = blocks_of([v[:, q * WIDE : (q + 1) * WIDE] for q in range(OWN_BLOCKS)])
        for g in range(SLOTS // GROUP):
            acc = by_product(tall, g, True, acc)
        return acc

    def forward_ghosts(par, acc):
        chunks = [ghost_in[par, t] for t in range(len(AROUND))]
        tall = blocks_of(
            [jnp.concatenate(chunks[2 * q : 2 * q + 2], 1) for q in range(OWN_BLOCKS)]
        )
        half = SLOTS // GROUP // 2
        for g in range(half):
            acc = by_product(tall, g, False, acc)
            acc = by_lookup(chunks, half + g, acc)
        return acc

    first_back = send_back(acc, 2)
    radial(CHUNKS - 1)
    around = own_part(acc)
    for k in range(SLOTS):
        around = around + coup[k]
    degree[...] = around

    hidden = product(wide1[...], features_of(feat_ref))
    for b, chi in enumerate(network(hidden, wide2, wide3, heavy_row)):
        residual[b : b + 1, :] = -CHI_SCALE * chi
    residual[PER:8, :] = jnp.broadcast_to(1.0 - heavy, (PER, ATOMS))
    h0, h1 = hardness_ref[0], hardness_ref[1]
    hard = jnp.where(heavy_row, h0, h1)

    lane_id = lax.broadcasted_iota(jnp.int32, (8, LANES), 1)

    def dots_of(r):
        dots = [lanes_sum(r * r), lanes_sum(r * image[...]), lanes_sum(r * steps[...]), lanes_sum(r)]
        v = dots[3]
        for n in (2, 1, 0):
            v = jnp.where(lane_id == n, dots[n], v)
        return v

    def send_lent(ref, par):
        lent[par] = at_ghosts(ref[...])
        out = []
        for g, (a, c) in enumerate(AROUND):
            cp = pltpu.make_async_remote_copy(
                src_ref=lent.at[par],
                dst_ref=ghost_in.at[par, g],
                send_sem=send_a.at[par, g],
                recv_sem=recv_a.at[par, g],
                device_id=brick_at(1 - a, 1 - c),
                device_id_type=MESH,
            )
            cp.start()
            out.append(cp)
        return out

    def dot_copies(par, targets):
        out = []
        for dx, dy in targets:
            n = dx * SIDE + dy
            out.append(
                pltpu.make_async_remote_copy(
                    src_ref=parts.at[par, me],
                    dst_ref=parts.at[par, me],
                    send_sem=send_d.at[par, n],
                    recv_sem=recv_d.at[par, n],
                    device_id=brick_at(dx, dy),
                    device_id_type=MESH,
                )
            )
        return out

    def send_dots(par, targets):
        out = dot_copies(par, targets)
        for cp in out:
            cp.start()
        return out

    def take_dots(copies, par):
        for cp in copies:
            cp.wait()
        whole = parts[par, 0]
        for n in range(1, BRICKS):
            whole = whole + parts[par, n]
        return [whole[:, n : n + 1] for n in range(4)]

    alpha_max = 2.0 / jnp.minimum(h0, h1)

    def step_sizes(dots, state, start):
        norm, rw, rs, r_sum = dots
        norm_prev, curve_prev, sum_prev, sum_total = state
        beta = jnp.where(start, 0.0, norm / jnp.maximum(norm_prev, TINY))
        curve = rw + 2.0 * beta * rs + beta * beta * curve_prev
        alpha = jnp.minimum(norm / jnp.maximum(curve, TINY), alpha_max)
        p_sum = r_sum + beta * sum_prev
        return alpha, beta, (norm, curve, p_sum, sum_total + alpha * p_sum)

    image[...] = residual[...]
    for ref in (direction, steps, image2, total):
        ref[...] = jnp.zeros_like(ref)
    high = jnp.logical_not(low_all)
    high_col = sublanes((8, 1)) >= PER

    def sweep(it, state):
        par = lax.rem(it, 2)
        start = it == 1
        r, w = residual[...], image[...]
        first = send_lent(image, par)
        third = []

        def dots_beside(g):
            if g == 2:
                parts[par, me] = dots_of(r)
                third.extend(send_dots(par, others))

        acc = scatter(lambda k: coup[k] * image[...], dots_beside)
        second = send_back(acc, par)
        around = forward_own(w, own_part(acc))
        for cp in first:
            cp.wait()
        around = forward_ghosts(par, around)

        @pl.when(it == 0)
        def _():
            degree[...] = hard + 0.5 * (degree[...] + take_back(first_back, 2))
        dots = take_dots(third, par)
        light = dots[3]
        alpha, beta, state = step_sizes(dots, state, it <= 1)
        alpha = jnp.where(it == 0, 0.0, alpha)
        state = tuple(jnp.where(it == 0, 0.0, v) for v in state)
        q = degree[...] * w - 0.5 * (around + take_back(second, par))
        z = q + beta * image2[...]
        s = w + beta * steps[...]
        p = r + beta * direction[...]
        x = total[...] + alpha * p
        r_new = r - alpha * s
        w_new = w - alpha * z
        known = jnp.logical_and(start, high)
        gap = h1 - h0
        hard_sum = (TOTAL_ATOMS - light) * h0 + light * h1
        c0 = light / hard_sum
        c1 = -TOTAL_ATOMS / hard_sum
        direction[...] = jnp.where(known, 1.0, p)
        steps[...] = jnp.where(known, hard, s)
        image2[...] = jnp.where(known, h0 * hard + gap * w, z)
        total[...] = jnp.where(known, TOTAL_ATOMS / hard_sum, x)
        residual[...] = jnp.where(known, gap * (c0 + c1 * r), r_new)
        image[...] = jnp.where(it == 0, q, jnp.where(known, gap * (c0 * hard + c1 * w), w_new))
        exact = (
            jnp.full((8, 1), TOTAL_ATOMS, F32),
            hard_sum,
            jnp.full((8, 1), TOTAL_ATOMS, F32),
            TOTAL_ATOMS / hard_sum * TOTAL_ATOMS,
        )
        known_col = jnp.logical_and(start, high_col)
        return tuple(jnp.where(known_col, e, v) for e, v in zip(exact, state))

    zero = jnp.zeros((8, 1), F32)
    state = lax.fori_loop(0, ITERS, sweep, (zero, zero, zero, zero))
    par = ITERS % 2
    parts[par, me] = dots_of(residual[...])
    third = send_dots(par, others)

    first_layer[...] = product(last1[...], features_of(feat_ref))
    dots = take_dots(third, par)
    alpha, beta, state = step_sizes(dots, state, False)
    x = total[...] + alpha * (residual[...] + beta * direction[...])
    sums = state[3]
    charges = x[0:PER] - (sums[0:PER] / sums[PER:8]) * x[PER:8]
    charge_ref[...] = charges
    storing.append(pltpu.make_async_copy(charge_ref, charge_hbm, stores.at[2]))
    storing[2].start()
    column = last1[:, FEATS : FEATS + 1]

    hidden = jnp.concatenate(
        [
            first_layer[:, b * ATOMS : (b + 1) * ATOMS] + column * charges[b : b + 1]
            for b in range(PER)
        ],
        1,
    )
    for b, e in enumerate(network(hidden, last2, last3, heavy_row)):
        energy_ref[b : b + 1, :] = e
    storing.append(pltpu.make_async_copy(energy_ref, energy_hbm, stores.at[3]))
    storing[3].start()
    for cp in storing:
        cp.wait()


def outputs_kernel(a_ref, b_ref, c_ref, d_ref, a_out, b_out, c_out, d_out):
    for src, dst in ((a_ref, a_out), (b_ref, b_out), (c_ref, c_out), (d_ref, d_out)):
        dst[...] = src[...]


def vmem(count):
    return [pl.BlockSpec(memory_space=pltpu.VMEM)] * count


def anywhere(count):
    return [pl.BlockSpec(memory_space=pl.ANY)] * count


def sds(*shape, dtype=F32):
    return jax.ShapeDtypeStruct(shape, dtype)


def f32(*shape):
    return pltpu.VMEM(shape, F32)


def on_device(
    positions,
    momenta,
    types,
    ghost_rows,
    neighbours,
    counts,
    hardness,
    chi_w1,
    chi_w2,
    chi_w3,
    en_w1,
    en_w2,
    en_w3,
):
    turn = lambda v: jnp.transpose(v, (1, 0, 2))
    dma = pltpu.SemaphoreType.DMA
    networks = [f32(2 * PAD, PAD), f32(2 * PAD, 2 * PAD), f32(8, 2 * PAD)]
    operands = (
        hardness,
        jnp.asarray(propagator()),
        turn(positions),
        turn(momenta),
        types.reshape(1, ATOMS),
        ghost_rows.reshape(1, LANES),
        neighbours,
        counts.reshape(1, ATOMS),
        turn(chi_w1),
        turn(chi_w2),
        chi_w3,
        turn(en_w1),
        turn(en_w2),
        en_w3,
    )
    outputs = (sds(3, PER, ATOMS), sds(3, PER, ATOMS), sds(PER, ATOMS), sds(PER, ATOMS))
    results = pl.pallas_call(
        main_kernel,
        name="main",
        out_shape=outputs,
        in_specs=anywhere(len(operands)),
        out_specs=tuple(anywhere(len(outputs))),
        scratch_shapes=[
            pltpu.SMEM(hardness.shape, F32),
            *[pltpu.VMEM(v.shape, v.dtype) for v in operands[1:]],
            *[f32(*v.shape) for v in outputs],
            f32(CHUNKS, LANES, LANES),
            f32(8, 6 * ATOMS),
            f32(64, 6 * LANES),
            f32(64, 3 * LANES),
            f32(8, 3 * ATOMS),
            f32(3, 8, LANES),
            f32(8, LANES),
            f32(4, 8, TABLE),
            pltpu.VMEM((SLOTS, ATOMS), jnp.int32),
            f32(SLOTS, ATOMS),
            pltpu.VMEM((SLOTS, 8, ATOMS), jnp.int32),
            pltpu.VMEM((SLOTS // 2, 8, ATOMS), jnp.int32),
            f32(SLOTS // 2, 8, ATOMS),
            pltpu.VMEM((SLOTS, BAND, ATOMS), BF16),
            pltpu.VMEM((WIDE, EDGES), BF16),
            pltpu.VMEM((EDGES, WIDE), BF16),
            pltpu.VMEM((LANES, ATOMS), BF16),
            f32(SLOTS, 8, ATOMS),
            f32(SLOTS // 2, 8, ATOMS),
            f32(SLOTS // 2, 8, ATOMS),
            f32(SLOTS // 2, 8, ATOMS),
            *networks,
            *networks,
            f32(2 * PAD, PER * ATOMS),
            *[f32(8, ATOMS) for _ in range(7)],
            f32(3, 8, 8, LANES),
            f32(2, 8, LANES),
            f32(2, 8, 8, LANES),
            f32(3, 8, 8, LANES),
            f32(2, BRICKS, 8, LANES),
            *[dma((GROUPS,)) for _ in range(4)],
            *[dma((8,)) for _ in range(4)],
            *[dma((2, 8)) for _ in range(2)],
            *[dma((3, 8)) for _ in range(2)],
            *[dma((2, BRICKS)) for _ in range(2)],
            dma((len(operands),)),
            dma((len(outputs),)),
        ],
        compiler_params=pltpu.CompilerParams(
            vmem_limit_bytes=VMEM_LIMIT, collective_id=0, has_side_effects=True
        ),
    )(*operands)
    new_pos, new_mom, charges, energies = pl.pallas_call(
        outputs_kernel,
        name="outputs",
        out_shape=outputs,
        in_specs=vmem(len(outputs)),
        out_specs=tuple(vmem(len(outputs))),
    )(*results)
    return (turn(new_pos), turn(new_mom), charges, energies)


def solution(mesh):
    placed = (
        P("bead", None, ("gx", "gy")),
        P("bead", None, ("gx", "gy")),
        P(("gx", "gy")),
        P(("gx", "gy")),
        P(None, ("gx", "gy")),
        P(("gx", "gy")),
        P(),
        P(),
        P(),
        P(),
        P(),
        P(),
        P(),
    )
    return jax.shard_map(
        on_device,
        mesh=mesh,
        in_specs=placed,
        out_specs=(
            P("bead", None, ("gx", "gy")),
            P("bead", None, ("gx", "gy")),
            P("bead", ("gx", "gy")),
            P("bead", ("gx", "gy")),
        ),
        check_vma=False,
    )
```

```python
import functools
import math

import jax
import jax.numpy as jnp
import numpy as np
from jax import lax
from jax.experimental import pallas as pl
from jax.experimental.pallas import tpu as pltpu
from jax.sharding import PartitionSpec as P

MESH = pl.DeviceIdType.MESH
F32 = jnp.float32
BF16 = jnp.bfloat16
HIGHEST = lax.Precision.HIGHEST
ITERS = 5
STEP = 0.5
TOP_FREQ = 80.0
CUTOFF = 4.0
HEAVY_MASS = 16.0
CHI_SCALE = 4.0
LANES = 128
BEADS = 32
GROUPS = 8
PER = 4
ATOMS = 1024
CHUNKS = ATOMS // LANES
SLOTS = 16
TABLE = ATOMS + 8 * LANES
HALF = 15
FEATS = 2 * HALF
SIDE = 4
PAD = 32
BRICKS = SIDE * SIDE
BAND = 16
WIDE = 256
BLOCKS = TABLE // WIDE
OWN_BLOCKS = ATOMS // WIDE
EDGES = SLOTS * ATOMS
GROUP = 4
EARLY = 10
TOTAL_ATOMS = ATOMS * BRICKS
TINY = 1e-30
SELF = ATOMS + 4 * LANES
VMEM_LIMIT = 60 * 1024 * 1024


def propagator():
    k = np.arange(BEADS)
    omega = TOP_FREQ * np.sin(math.pi * k / BEADS)
    cosine = np.cos(omega * STEP)
    sine = np.sin(omega * STEP)
    drift = np.where(k > 0, TOP_FREQ * sine / np.where(k > 0, omega, 1.0), TOP_FREQ * STEP)
    restoring = -(omega / TOP_FREQ) * sine
    gap = (k[:, None] - k[None, :]) % BEADS

    def spread(weights):
        line = (weights[None, :] * np.cos(2 * math.pi * k[:, None] * k[None, :] / BEADS)).sum(1) / BEADS
        return line[gap]

    keep, push, pull = spread(cosine), spread(drift), spread(restoring)
    zero = np.zeros_like(keep)
    plain = np.block([[keep, zero], [zero, keep]])
    massive = np.block([[zero, push], [pull, zero]])
    order = np.array([half * BEADS + g * PER + b for g in range(GROUPS) for half in range(2) for b in range(PER)])
    both = np.concatenate([plain[order][:, order], massive[order][:, order]], 0)
    return both.astype(np.float32)


def sublanes(shape):
    return lax.broadcasted_iota(jnp.int32, shape, 0)


def lane_take(table, lane):
    return jnp.take_along_axis(table, lane, axis=1, mode="promise_in_bounds")


def row_bits(rows, count):
    return [(rows & (LANES << bit)) != 0 for bit in range(count)]


def pick(parts, bits):
    level = 0
    while len(parts) > 1:
        nxt = [
            jnp.where(bits[level], parts[i + 1], parts[i]) for i in range(0, len(parts) - 1, 2)
        ]
        if len(parts) % 2:
            nxt.append(parts[-1])
        parts = nxt
        level += 1
    return parts[0]


def split(v):
    top = v.astype(BF16).astype(F32)
    return jnp.concatenate([top, v - top], 0).astype(BF16)


def halves(v):
    top = v.astype(BF16)
    return top, (v - top.astype(F32)).astype(BF16)


def lanes_sum(v):
    return jnp.sum(v, axis=1, keepdims=True)


def fold(v, low):
    return jnp.where(low, v, pltpu.roll(v, PER, 0))


def brick_at(dx, dy):
    return {
        "gx": lax.rem(lax.axis_index("gx") + dx + SIDE, SIDE),
        "gy": lax.rem(lax.axis_index("gy") + dy + SIDE, SIDE),
    }


AROUND = [(a, c) for a in range(3) for c in range(3) if (a, c) != (1, 1)]


def load_weights(w1_ref, w2_ref, w3_ref, wide1, wide2, wide3):
    rows, cols = w1_ref.shape[0], w1_ref.shape[2]
    for ref in (wide1, wide2, wide3):
        ref[...] = jnp.zeros_like(ref)
    for e in range(2):
        at = e * PAD
        wide1[at : at + rows, 0:cols] = w1_ref[:, e, :]
        wide2[at : at + rows, at : at + rows] = w2_ref[:, e, :]
        wide3[e : e + 1, at : at + rows] = w3_ref[e : e + 1, :]


def product(w, f):
    w_top, w_rest = halves(w)
    f_top, f_rest = halves(f)
    rows = w.shape[0]
    both = jnp.dot(jnp.concatenate([w_top, w_rest], 0), f_top, preferred_element_type=F32)
    return both[0:rows] + both[rows:] + jnp.dot(w_top, f_rest, preferred_element_type=F32)


def features_of(feat_ref):
    return jnp.concatenate(
        [feat_ref[d, pl.ds(b, PAD, stride=PER), :] for b in range(PER) for d in range(CHUNKS)], 1
    )


def network(hidden, wide2, wide3, heavy):
    out = product(wide3[...], jnp.tanh(product(wide2[...], jnp.tanh(hidden))))
    return [
        jnp.where(
            heavy, out[0:1, b * ATOMS : (b + 1) * ATOMS], out[1:2, b * ATOMS : (b + 1) * ATOMS]
        )
        for b in range(PER)
    ]


def main_kernel(
    hardness_hbm,
    matrix_hbm,
    pos_hbm,
    mom_hbm,
    types_hbm,
    ghost_hbm,
    idx_hbm,
    counts_hbm,
    w1_hbm,
    w2_hbm,
    w3_hbm,
    v1_hbm,
    v2_hbm,
    v3_hbm,
    newpos_hbm,
    newmom_hbm,
    charge_hbm,
    energy_hbm,
    hardness_ref,
    matrix_ref,
    pos_ref,
    mom_ref,
    types_ref,
    ghost_ref,
    idx_ref,
    counts_ref,
    w1_ref,
    w2_ref,
    w3_ref,
    v1_ref,
    v2_ref,
    v3_ref,
    newpos_ref,
    newmom_ref,
    charge_ref,
    energy_ref,
    feat_ref,
    stage,
    modes,
    moved,
    back,
    lent_pos,
    lent_heavy,
    tab,
    idx16,
    heavy16,
    rows_all,
    pairs,
    heavy_pairs,
    block_ids,
    onehot,
    onehot_t,
    ghost_onehot,
    coup,
    dist,
    weight_h,
    weight_l,
    wide1,
    wide2,
    wide3,
    last1,
    last2,
    last3,
    first_layer,
    residual,
    image,
    image2,
    direction,
    steps,
    total,
    degree,
    spread,
    lent,
    ghost_in,
    backin,
    parts,
    send1,
    recv1,
    send2,
    recv2,
    send3,
    recv3,
    send4,
    recv4,
    send_a,
    recv_a,
    send_b,
    recv_b,
    send_d,
    recv_d,
    loads,
    stores,
):
    group = lax.axis_index("bead")
    me = lax.axis_index("gx") * SIDE + lax.axis_index("gy")
    others = [(o // SIDE, o % SIDE) for o in range(1, BRICKS)]
    parts[...] = jnp.zeros_like(parts)
    barrier = pltpu.get_barrier_semaphore()
    for o in range(1, GROUPS):
        pl.semaphore_signal(
            barrier, inc=1, device_id={"bead": lax.rem(group + o, GROUPS)}, device_id_type=MESH
        )
    for a, c in AROUND:
        pl.semaphore_signal(barrier, inc=1, device_id=brick_at(a - 1, c - 1), device_id_type=MESH)
    loading = [
        pltpu.make_async_copy(src, dst, loads.at[n])
        for n, (src, dst) in enumerate(
            (
                (pos_hbm, pos_ref),
                (mom_hbm, mom_ref),
                (ghost_hbm, ghost_ref),
                (types_hbm, types_ref),
                (idx_hbm, idx_ref),
                (matrix_hbm, matrix_ref),
                (counts_hbm, counts_ref),
                (hardness_hbm, hardness_ref),
                (w1_hbm, w1_ref),
                (w2_hbm, w2_ref),
                (w3_hbm, w3_ref),
                (v1_hbm, v1_ref),
                (v2_hbm, v2_ref),
                (v3_hbm, v3_ref),
            )
        )
    ]
    for cp in loading:
        cp.start()
    for cp in loading[0:4]:
        cp.wait()

    low = sublanes((8, LANES)) < PER
    low_all = sublanes((8, ATOMS)) < PER
    own_width = 3 * LANES
    width = 2 * own_width
    ghost_rows = jnp.broadcast_to(ghost_ref[...], (8, LANES))
    ghost_lane = ghost_rows & (LANES - 1)
    ghost_bits = row_bits(ghost_rows, 3)

    def at_ghosts(v):
        return pick(
            [lane_take(v[:, d * LANES : (d + 1) * LANES], ghost_lane) for d in range(CHUNKS)],
            ghost_bits,
        )

    heavy_row = types_ref[...] == 0
    heavy = jnp.where(heavy_row, 1.0, 0.0)
    tab[3, :, 0:ATOMS] = jnp.broadcast_to(heavy, (8, ATOMS))
    ghost_heavy = at_ghosts(jnp.broadcast_to(heavy, (8, ATOMS)))
    lent_heavy[...] = ghost_heavy
    for c in range(3):
        v = jnp.concatenate([pos_ref[c], mom_ref[c]], 0)
        g = at_ghosts(v)
        for d in range(CHUNKS):
            at = d * width + c * LANES
            stage[:, at : at + LANES] = v[:, d * LANES : (d + 1) * LANES]
            stage[:, at + own_width : at + own_width + LANES] = g
    pl.semaphore_wait(barrier, GROUPS - 1 + len(AROUND))

    mine = pl.ds(pl.multiple_of(group * 8, 8), 8)
    mine_too = pl.ds(pl.multiple_of(64 + group * 8, 8), 8)
    copies = []
    for o in range(1, GROUPS):
        to = lax.rem(group + o, GROUPS)
        cp = pltpu.make_async_remote_copy(
            src_ref=stage.at[:, pl.ds(pl.multiple_of(to * width, LANES), width)],
            dst_ref=modes.at[mine, :],
            send_sem=send1.at[o],
            recv_sem=recv1.at[o],
            device_id={"bead": to},
            device_id_type=MESH,
        )
        cp.start()
        copies.append(cp)
    heavy_copies = []
    for g, (a, c) in enumerate(AROUND):
        at = ATOMS + g * LANES
        cp = pltpu.make_async_remote_copy(
            src_ref=lent_heavy,
            dst_ref=tab.at[3, :, at : at + LANES],
            send_sem=send4.at[g],
            recv_sem=recv4.at[g],
            device_id=brick_at(1 - a, 1 - c),
            device_id_type=MESH,
        )
        cp.start()
        heavy_copies.append(cp)
    modes[mine, :] = stage[:, pl.ds(pl.multiple_of(group * width, LANES), width)]

    for cp in loading[4:]:
        cp.wait()
    def renumber(d, carry):
        lanes = pl.ds(pl.multiple_of(d * LANES, LANES), LANES)
        for half in range(2):
            rows = idx_ref[half * 8 : half * 8 + 8, lanes]
            local = lane_take(ghost_rows, rows & (LANES - 1))
            rows = jnp.where(
                rows < SELF, rows, jnp.where(rows < SELF + LANES, local, rows - LANES)
            )
            idx16[half * 8 : half * 8 + 8, lanes] = rows
        return carry

    lax.fori_loop(0, CHUNKS, renumber, 0)
    for k in range(SLOTS):
        rows_all[k] = jnp.broadcast_to(idx16[k : k + 1, :], (8, ATOMS))
    within = sublanes((WIDE, ATOMS)).astype(F32).astype(BF16)

    def build(k, carry):
        rows = rows_all[k]
        ids = (rows >> 8).astype(F32)
        block_ids[k] = jnp.concatenate([ids, ids], 0).astype(BF16)
        wide = (rows & (WIDE - 1)).astype(F32)
        wide = jnp.concatenate([wide, wide], 0).astype(BF16)
        wide = jnp.concatenate([wide] * (WIDE // BAND), 0)
        edges = pl.ds(pl.multiple_of(k * ATOMS, ATOMS), ATOMS)
        hits = jnp.where(within == wide, 1.0, 0.0).astype(BF16)
        onehot[:, edges] = hits
        onehot_t[edges, :] = jnp.transpose(hits)
        return carry

    lax.fori_loop(0, EARLY, build, 0)
    for ref in (coup, dist, weight_h, weight_l, feat_ref):
        ref[...] = jnp.zeros_like(ref)

    def pair_up(kp, carry):
        pairs[kp] = jnp.where(low_all, rows_all[2 * kp], rows_all[2 * kp + 1])
        return carry

    lax.fori_loop(0, SLOTS // 2, pair_up, 0)
    load_weights(w1_ref, w2_ref, w3_ref, wide1, wide2, wide3)
    load_weights(v1_ref, v2_ref, v3_ref, last1, last2, last3)
    my_types = types_ref[:, pl.ds(pl.multiple_of(group * LANES, LANES), LANES)]
    mass = jnp.broadcast_to(jnp.where(my_types == 0, HEAVY_MASS, 1.0), (8, LANES))
    factor = jnp.concatenate([jnp.where(low, 1.0 / mass, mass)] * 3, 1)
    ghost_mass = jnp.where(ghost_heavy > 0.0, HEAVY_MASS, 1.0)
    ghost_factor = jnp.concatenate([1.0 / ghost_mass] * 3, 1)

    for cp in copies:
        cp.wait()
    ghost_matrix = jnp.concatenate([matrix_ref[mine, :], matrix_ref[mine_too, :]], 0)
    both = jnp.dot(
        ghost_matrix, modes[:, own_width:width], precision=HIGHEST, preferred_element_type=F32
    )
    ghost_pos = both[0:8] + both[8:16] * ghost_factor
    for c in range(3):
        lent_pos[c] = fold(ghost_pos[:, c * LANES : (c + 1) * LANES], low)
    pos_copies = []
    for g, (a, c) in enumerate(AROUND):
        at = ATOMS + g * LANES
        cp = pltpu.make_async_remote_copy(
            src_ref=lent_pos,
            dst_ref=tab.at[0:3, :, at : at + LANES],
            send_sem=send3.at[g],
            recv_sem=recv3.at[g],
            device_id=brick_at(1 - a, 1 - c),
            device_id_type=MESH,
        )
        cp.start()
        pos_copies.append(cp)
    both = jnp.dot(
        matrix_ref[...], modes[:, 0:own_width], precision=HIGHEST, preferred_element_type=F32
    )
    for g in range(GROUPS):
        rows = slice(g * 8, g * 8 + 8)
        moved[rows, :] = both[rows] + both[64 + g * 8 : 72 + g * 8] * factor
    my_lanes = pl.ds(pl.multiple_of(group * own_width, LANES), own_width)
    copies = []
    for o in range(1, GROUPS):
        to = lax.rem(group + o, GROUPS)
        cp = pltpu.make_async_remote_copy(
            src_ref=moved.at[pl.ds(pl.multiple_of(to * 8, 8), 8), :],
            dst_ref=back.at[:, my_lanes],
            send_sem=send2.at[o],
            recv_sem=recv2.at[o],
            device_id={"bead": to},
            device_id_type=MESH,
        )
        cp.start()
        copies.append(cp)
    back[:, my_lanes] = moved[mine, :]

    def ghost_hits(d, carry):
        rows = sublanes((LANES, LANES)) + d * LANES
        hit = rows == jnp.broadcast_to(ghost_ref[...], (LANES, LANES))
        hit = jnp.where(hit, 1.0, 0.0).astype(BF16)
        ghost_onehot[:, pl.ds(pl.multiple_of(d * LANES, LANES), LANES)] = jnp.transpose(hit)
        return carry

    lax.fori_loop(0, CHUNKS, ghost_hits, 0)
    for cp in heavy_copies:
        cp.wait()

    def near_heavy(d, carry):
        lanes = pl.ds(pl.multiple_of(d * LANES, LANES), LANES)
        for half in range(2):
            rows = idx16[half * 8 : half * 8 + 8, lanes]
            lane = rows & (LANES - 1)
            heavy16[half * 8 : half * 8 + 8, lanes] = pick(
                [
                    lane_take(tab[3, :, t * LANES : (t + 1) * LANES], lane)
                    for t in range(TABLE // LANES)
                ],
                row_bits(rows, 4),
            )
        return carry

    lax.fori_loop(0, CHUNKS, near_heavy, 0)
    lax.fori_loop(EARLY, SLOTS, build, 0)
    for kp in range(SLOTS // 2):
        heavy_pairs[kp] = jnp.where(
            low_all,
            jnp.broadcast_to(heavy16[2 * kp : 2 * kp + 1, :], (8, ATOMS)),
            jnp.broadcast_to(heavy16[2 * kp + 1 : 2 * kp + 2, :], (8, ATOMS)),
        )


    for cp in copies:
        cp.wait()
    for c in range(3):
        for d in range(CHUNKS):
            at = d * own_width + c * LANES
            v = back[:, at : at + LANES]
            newpos_ref[c, :, d * LANES : (d + 1) * LANES] = v[0:PER]
            newmom_ref[c, :, d * LANES : (d + 1) * LANES] = v[PER:8]
            tab[c, :, d * LANES : (d + 1) * LANES] = fold(v, low)
    storing = [
        pltpu.make_async_copy(newpos_ref, newpos_hbm, stores.at[0]),
        pltpu.make_async_copy(newmom_ref, newmom_hbm, stores.at[1]),
    ]
    for cp in storing:
        cp.start()
    for cp in pos_copies:
        cp.wait()

    slot_off = jnp.where(low, 0, 1)
    cos_scale = (math.pi / (2.0 * CUTOFF)) ** 2
    cos_terms = [(-1.0) ** n * cos_scale**n / math.factorial(2 * n) for n in range(8)]

    def by_block(terms, ids):
        terms = split(terms)
        zero = jnp.zeros_like(terms)
        return jnp.concatenate([jnp.where(ids == b, terms, zero) for b in range(BLOCKS)], 0)

    def radial(ci):
        lanes = pl.ds(pl.multiple_of(ci * LANES, LANES), LANES)
        sums = [jnp.zeros((8, LANES), F32) for _ in range(FEATS)]
        for kp in range(SLOTS // 2):
            d = dist[kp, :, lanes]
            wh = weight_h[kp, :, lanes]
            wl = weight_l[kp, :, lanes]
            for s in range(HALF):
                rate = -0.2 * 20.0 ** (s / (HALF - 1)) * math.log2(math.e)
                falloff = jnp.exp2(d * rate)
                sums[s] = sums[s] + wh * falloff
                sums[HALF + s] = sums[HALF + s] + wl * falloff
        for s in range(FEATS):
            v = jnp.log(1.0 + (sums[s] + pltpu.roll(sums[s], PER, 0)))
            feat_ref[ci, s * PER : (s + 1) * PER, :] = v[0:PER]

    def degree_part(ci, acc):
        lanes = pl.ds(pl.multiple_of(ci * LANES, LANES), LANES)
        tall = jnp.concatenate(
            [by_block(coup[k, :, lanes], block_ids[k, :, lanes]) for k in range(SLOTS)], 1
        )
        hits = jnp.concatenate(
            [
                onehot_t[pl.ds(pl.multiple_of(k * ATOMS + ci * LANES, LANES), LANES), :]
                for k in range(SLOTS)
            ],
            0,
        )
        return acc + jnp.dot(tall, hits, preferred_element_type=F32)

    def geometry(ci, acc):
        before = lax.rem(ci + CHUNKS - 1, CHUNKS)
        acc = degree_part(before, acc)
        radial(before)
        lanes = pl.ds(pl.multiple_of(ci * LANES, LANES), LANES)
        own = [tab[c, :, lanes] for c in range(3)]
        count = jnp.broadcast_to(counts_ref[:, lanes], (8, LANES))
        for kp in range(SLOTS // 2):
            rows = pairs[kp, :, lanes]
            lane = rows & (LANES - 1)
            bits = row_bits(rows, 4)
            dist_sq = jnp.zeros((8, LANES), F32)
            for c in range(3):
                near = pick(
                    [
                        lane_take(tab[c, :, t * LANES : (t + 1) * LANES], lane)
                        for t in range(TABLE // LANES)
                    ],
                    bits,
                )
                dist_sq = dist_sq + (near - own[c]) ** 2
            close = jnp.minimum(dist_sq, CUTOFF * CUTOFF)
            wave = jnp.full_like(close, cos_terms[-1])
            for term in cos_terms[-2::-1]:
                wave = wave * close + term
            used = ((2 * kp + slot_off) < count) & (dist_sq < CUTOFF * CUTOFF)
            smooth = jnp.where(used, wave * wave, 0.0)
            heavy_w = smooth * heavy_pairs[kp, :, lanes]
            dist[kp, :, lanes] = dist_sq
            weight_h[kp, :, lanes] = heavy_w
            weight_l[kp, :, lanes] = smooth - heavy_w
            coupling = smooth * lax.rsqrt(1.0 + dist_sq)
            turned = pltpu.roll(coupling, PER, 0)
            for k, v in ((2 * kp, jnp.where(low, coupling, turned)), (2 * kp + 1, jnp.where(low, turned, coupling))):
                coup[k, :, lanes] = v
        return acc

    acc = lax.fori_loop(0, CHUNKS, geometry, jnp.zeros((BLOCKS * BAND, WIDE), F32))
    acc = degree_part(CHUNKS - 1, acc)

    def scatter(terms_of, beside):
        acc = jnp.zeros((BLOCKS * BAND, WIDE), F32)
        for g in range(SLOTS // GROUP):
            beside(g)
            group_slots = range(g * GROUP, (g + 1) * GROUP)
            tall = jnp.concatenate([by_block(terms_of(k), block_ids[k]) for k in group_slots], 1)
            rows = slice(g * GROUP * ATOMS, (g + 1) * GROUP * ATOMS)
            acc = acc + jnp.dot(tall, onehot_t[rows, :], preferred_element_type=F32)
        return acc

    def chunk_of(acc, n):
        row, col = (n // 2) * BAND, (n % 2) * LANES
        return acc[row : row + 8, col : col + LANES] + acc[row + 8 : row + 16, col : col + LANES]

    def send_back(acc, par):
        out = []
        for g, (a, c) in enumerate(AROUND):
            spread[par, g] = chunk_of(acc, CHUNKS + g)
        for g, (a, c) in enumerate(AROUND):
            cp = pltpu.make_async_remote_copy(
                src_ref=spread.at[par, g],
                dst_ref=backin.at[par, g],
                send_sem=send_b.at[par, g],
                recv_sem=recv_b.at[par, g],
                device_id=brick_at(a - 1, c - 1),
                device_id_type=MESH,
            )
            cp.start()
            out.append(cp)
        return out

    def own_part(acc):
        return jnp.concatenate([chunk_of(acc, d) for d in range(CHUNKS)], 1)

    def take_back(copies, par):
        for cp in copies:
            cp.wait()
        received = backin[par, 0]
        for g in range(1, len(AROUND)):
            received = received + backin[par, g]
        returned = lax.dot_general(
            split(received), ghost_onehot[...], (((1,), (0,)), ((), ())), preferred_element_type=F32
        )
        return returned[0:8] + returned[8:16]

    def blocks_of(pieces):
        return jnp.concatenate([split(v) for v in pieces], 0)

    def by_product(tall, g, inside, acc):
        cols = slice(g * GROUP * ATOMS, (g + 1) * GROUP * ATOMS)
        found = jnp.dot(tall, onehot[:, cols], preferred_element_type=F32)
        for kk in range(GROUP):
            k = g * GROUP + kk
            f = found[:, kk * ATOMS : (kk + 1) * ATOMS]
            near = [
                f[q * BAND : q * BAND + 8] + f[q * BAND + 8 : q * BAND + 16]
                for q in range(OWN_BLOCKS)
            ]
            rows = rows_all[k]
            near = pick(near, [(rows & WIDE) != 0, (rows & (2 * WIDE)) != 0])
            hit = (rows < ATOMS) if inside else (rows >= ATOMS)
            acc = acc + jnp.where(hit, coup[k], 0.0) * near
        return acc

    def by_lookup(chunks, g, acc):
        out = []
        for d in range(CHUNKS):
            lanes = slice(d * LANES, (d + 1) * LANES)
            v = acc[:, lanes]
            for k in range(g * GROUP, (g + 1) * GROUP):
                rows = rows_all[k, :, lanes]
                lane = rows & (LANES - 1)
                near = pick([lane_take(t, lane) for t in chunks], row_bits(rows, 3))
                v = v + jnp.where(rows >= ATOMS, coup[k, :, lanes], 0.0) * near
            out.append(v)
        return jnp.concatenate(out, 1)

    def forward_own(v, acc):
        tall = blocks_of([v[:, q * WIDE : (q + 1) * WIDE] for q in range(OWN_BLOCKS)])
        for g in range(SLOTS // GROUP):
            acc = by_product(tall, g, True, acc)
        return acc

    def forward_ghosts(par, acc):
        chunks = [ghost_in[par, t] for t in range(len(AROUND))]
        tall = blocks_of(
            [jnp.concatenate(chunks[2 * q : 2 * q + 2], 1) for q in range(OWN_BLOCKS)]
        )
        half = SLOTS // GROUP // 2
        for g in range(half):
            acc = by_product(tall, g, False, acc)
            acc = by_lookup(chunks, half + g, acc)
        return acc

    first_back = send_back(acc, 2)
    radial(CHUNKS - 1)
    around = own_part(acc)
    for k in range(SLOTS):
        around = around + coup[k]
    degree[...] = around

    hidden = product(wide1[...], features_of(feat_ref))
    for b, chi in enumerate(network(hidden, wide2, wide3, heavy_row)):
        residual[b : b + 1, :] = -CHI_SCALE * chi
    residual[PER:8, :] = jnp.broadcast_to(1.0 - heavy, (PER, ATOMS))
    h0, h1 = hardness_ref[0], hardness_ref[1]
    hard = jnp.where(heavy_row, h0, h1)

    lane_id = lax.broadcasted_iota(jnp.int32, (8, LANES), 1)

    def dots_of(r):
        dots = [lanes_sum(r * r), lanes_sum(r * image[...]), lanes_sum(r * steps[...]), lanes_sum(r)]
        v = dots[3]
        for n in (2, 1, 0):
            v = jnp.where(lane_id == n, dots[n], v)
        return v

    def send_lent(ref, par):
        lent[par] = at_ghosts(ref[...])
        out = []
        for g, (a, c) in enumerate(AROUND):
            cp = pltpu.make_async_remote_copy(
                src_ref=lent.at[par],
                dst_ref=ghost_in.at[par, g],
                send_sem=send_a.at[par, g],
                recv_sem=recv_a.at[par, g],
                device_id=brick_at(1 - a, 1 - c),
                device_id_type=MESH,
            )
            cp.start()
            out.append(cp)
        return out

    def dot_copies(par, targets):
        out = []
        for dx, dy in targets:
            n = dx * SIDE + dy
            out.append(
                pltpu.make_async_remote_copy(
                    src_ref=parts.at[par, me],
                    dst_ref=parts.at[par, me],
                    send_sem=send_d.at[par, n],
                    recv_sem=recv_d.at[par, n],
                    device_id=brick_at(dx, dy),
                    device_id_type=MESH,
                )
            )
        return out

    def send_dots(par, targets):
        out = dot_copies(par, targets)
        for cp in out:
            cp.start()
        return out

    def take_dots(copies, par):
        for cp in copies:
            cp.wait()
        whole = parts[par, 0]
        for n in range(1, BRICKS):
            whole = whole + parts[par, n]
        return [whole[:, n : n + 1] for n in range(4)]

    alpha_max = 2.0 / jnp.minimum(h0, h1)

    def step_sizes(dots, state, start):
        norm, rw, rs, r_sum = dots
        norm_prev, curve_prev, sum_prev, sum_total = state
        beta = jnp.where(start, 0.0, norm / jnp.maximum(norm_prev, TINY))
        curve = rw + 2.0 * beta * rs + beta * beta * curve_prev
        alpha = jnp.minimum(norm / jnp.maximum(curve, TINY), alpha_max)
        p_sum = r_sum + beta * sum_prev
        return alpha, beta, (norm, curve, p_sum, sum_total + alpha * p_sum)

    image[...] = residual[...]
    for ref in (direction, steps, image2, total):
        ref[...] = jnp.zeros_like(ref)
    high = jnp.logical_not(low_all)
    high_col = sublanes((8, 1)) >= PER

    def sweep(it, state):
        par = lax.rem(it, 2)
        start = it == 1
        r, w = residual[...], image[...]
        first = send_lent(image, par)
        third = []

        def dots_beside(g):
            if g == 2:
                parts[par, me] = dots_of(r)
                third.extend(send_dots(par, others))

        acc = scatter(lambda k: coup[k] * image[...], dots_beside)
        second = send_back(acc, par)
        around = forward_own(w, own_part(acc))

        @pl.when(it == 0)
        def _():
            degree[...] = hard + 0.5 * (degree[...] + take_back(first_back, 2))

        for cp in first:
            cp.wait()
        around = forward_ghosts(par, around)

        dots = take_dots(third, par)
        light = dots[3]
        alpha, beta, state = step_sizes(dots, state, it <= 1)
        alpha = jnp.where(it == 0, 0.0, alpha)
        state = tuple(jnp.where(it == 0, 0.0, v) for v in state)
        q = degree[...] * w - 0.5 * (around + take_back(second, par))
        z = q + beta * image2[...]
        s = w + beta * steps[...]
        p = r + beta * direction[...]
        x = total[...] + alpha * p
        r_new = r - alpha * s
        w_new = w - alpha * z
        known = jnp.logical_and(start, high)
        gap = h1 - h0
        hard_sum = (TOTAL_ATOMS - light) * h0 + light * h1
        c0 = light / hard_sum
        c1 = -TOTAL_ATOMS / hard_sum
        direction[...] = jnp.where(known, 1.0, p)
        steps[...] = jnp.where(known, hard, s)
        image2[...] = jnp.where(known, h0 * hard + gap * w, z)
        total[...] = jnp.where(known, TOTAL_ATOMS / hard_sum, x)
        residual[...] = jnp.where(known, gap * (c0 + c1 * r), r_new)
        image[...] = jnp.where(it == 0, q, jnp.where(known, gap * (c0 * hard + c1 * w), w_new))
        exact = (
            jnp.full((8, 1), TOTAL_ATOMS, F32),
            hard_sum,
            jnp.full((8, 1), TOTAL_ATOMS, F32),
            TOTAL_ATOMS / hard_sum * TOTAL_ATOMS,
        )
        known_col = jnp.logical_and(start, high_col)
        return tuple(jnp.where(known_col, e, v) for e, v in zip(exact, state))

    zero = jnp.zeros((8, 1), F32)
    state = lax.fori_loop(0, ITERS, sweep, (zero, zero, zero, zero))
    par = ITERS % 2
    parts[par, me] = dots_of(residual[...])
    third = send_dots(par, others)

    first_layer[...] = product(last1[...], features_of(feat_ref))
    dots = take_dots(third, par)
    alpha, beta, state = step_sizes(dots, state, False)
    x = total[...] + alpha * (residual[...] + beta * direction[...])
    sums = state[3]
    charges = x[0:PER] - (sums[0:PER] / sums[PER:8]) * x[PER:8]
    charge_ref[...] = charges
    storing.append(pltpu.make_async_copy(charge_ref, charge_hbm, stores.at[2]))
    storing[2].start()
    column = last1[:, FEATS : FEATS + 1]

    hidden = jnp.concatenate(
        [
            first_layer[:, b * ATOMS : (b + 1) * ATOMS] + column * charges[b : b + 1]
            for b in range(PER)
        ],
        1,
    )
    for b, e in enumerate(network(hidden, last2, last3, heavy_row)):
        energy_ref[b : b + 1, :] = e
    storing.append(pltpu.make_async_copy(energy_ref, energy_hbm, stores.at[3]))
    storing[3].start()
    for cp in storing:
        cp.wait()


def outputs_kernel(a_ref, b_ref, c_ref, d_ref, a_out, b_out, c_out, d_out):
    for src, dst in ((a_ref, a_out), (b_ref, b_out), (c_ref, c_out), (d_ref, d_out)):
        dst[...] = src[...]


def vmem(count):
    return [pl.BlockSpec(memory_space=pltpu.VMEM)] * count


def anywhere(count):
    return [pl.BlockSpec(memory_space=pl.ANY)] * count


def sds(*shape, dtype=F32):
    return jax.ShapeDtypeStruct(shape, dtype)


def f32(*shape):
    return pltpu.VMEM(shape, F32)


def on_device(
    positions,
    momenta,
    types,
    ghost_rows,
    neighbours,
    counts,
    hardness,
    chi_w1,
    chi_w2,
    chi_w3,
    en_w1,
    en_w2,
    en_w3,
):
    turn = lambda v: jnp.transpose(v, (1, 0, 2))
    dma = pltpu.SemaphoreType.DMA
    networks = [f32(2 * PAD, PAD), f32(2 * PAD, 2 * PAD), f32(8, 2 * PAD)]
    operands = (
        hardness,
        jnp.asarray(propagator()),
        turn(positions),
        turn(momenta),
        types.reshape(1, ATOMS),
        ghost_rows.reshape(1, LANES),
        neighbours,
        counts.reshape(1, ATOMS),
        turn(chi_w1),
        turn(chi_w2),
        chi_w3,
        turn(en_w1),
        turn(en_w2),
        en_w3,
    )
    outputs = (sds(3, PER, ATOMS), sds(3, PER, ATOMS), sds(PER, ATOMS), sds(PER, ATOMS))
    results = pl.pallas_call(
        main_kernel,
        name="main",
        out_shape=outputs,
        in_specs=anywhere(len(operands)),
        out_specs=tuple(anywhere(len(outputs))),
        scratch_shapes=[
            pltpu.SMEM(hardness.shape, F32),
            *[pltpu.VMEM(v.shape, v.dtype) for v in operands[1:]],
            *[f32(*v.shape) for v in outputs],
            f32(CHUNKS, LANES, LANES),
            f32(8, 6 * ATOMS),
            f32(64, 6 * LANES),
            f32(64, 3 * LANES),
            f32(8, 3 * ATOMS),
            f32(3, 8, LANES),
            f32(8, LANES),
            f32(4, 8, TABLE),
            pltpu.VMEM((SLOTS, ATOMS), jnp.int32),
            f32(SLOTS, ATOMS),
            pltpu.VMEM((SLOTS, 8, ATOMS), jnp.int32),
            pltpu.VMEM((SLOTS // 2, 8, ATOMS), jnp.int32),
            f32(SLOTS // 2, 8, ATOMS),
            pltpu.VMEM((SLOTS, BAND, ATOMS), BF16),
            pltpu.VMEM((WIDE, EDGES), BF16),
            pltpu.VMEM((EDGES, WIDE), BF16),
            pltpu.VMEM((LANES, ATOMS), BF16),
            f32(SLOTS, 8, ATOMS),
            f32(SLOTS // 2, 8, ATOMS),
            f32(SLOTS // 2, 8, ATOMS),
            f32(SLOTS // 2, 8, ATOMS),
            *networks,
            *networks,
            f32(2 * PAD, PER * ATOMS),
            *[f32(8, ATOMS) for _ in range(7)],
            f32(3, 8, 8, LANES),
            f32(2, 8, LANES),
            f32(2, 8, 8, LANES),
            f32(3, 8, 8, LANES),
            f32(2, BRICKS, 8, LANES),
            *[dma((GROUPS,)) for _ in range(4)],
            *[dma((8,)) for _ in range(4)],
            *[dma((2, 8)) for _ in range(2)],
            *[dma((3, 8)) for _ in range(2)],
            *[dma((2, BRICKS)) for _ in range(2)],
            dma((len(operands),)),
            dma((len(outputs),)),
        ],
        compiler_params=pltpu.CompilerParams(
            vmem_limit_bytes=VMEM_LIMIT, collective_id=0, has_side_effects=True
        ),
    )(*operands)
    new_pos, new_mom, charges, energies = pl.pallas_call(
        outputs_kernel,
        name="outputs",
        out_shape=outputs,
        in_specs=vmem(len(outputs)),
        out_specs=tuple(vmem(len(outputs))),
    )(*results)
    return (turn(new_pos), turn(new_mom), charges, energies)


def solution(mesh):
    placed = (
        P("bead", None, ("gx", "gy")),
        P("bead", None, ("gx", "gy")),
        P(("gx", "gy")),
        P(("gx", "gy")),
        P(None, ("gx", "gy")),
        P(("gx", "gy")),
        P(),
        P(),
        P(),
        P(),
        P(),
        P(),
        P(),
    )
    return jax.shard_map(
        on_device,
        mesh=mesh,
        in_specs=placed,
        out_specs=(
            P("bead", None, ("gx", "gy")),
            P("bead", None, ("gx", "gy")),
            P("bead", ("gx", "gy")),
            P("bead", ("gx", "gy")),
        ),
        check_vma=False,
    )
```
